32 devices in a mesh: seq: 8 (over y, x, core), head: 4 (over z).
Axes of the slice: x: 2, y: 2, z: 4, core: 2. Of those that a mesh axis runs over, the one named last changes fastest.
Arguments:
- tokens: bfloat16 [2, 8192, 1024], P(None, 'seq', 'head'), may hold values from -6 to 6
- decay_codes: int32 [2, 8192, 512], P(None, 'seq', 'head'), may hold values from 1 to 32704
- cotangent: bfloat16 [2, 8192, 1024], P(None, 'seq', 'head'), may hold values from -6 to 6
- attn_gain: float32 [1024], replicated, may hold values from 0.5 to 1.5
- w_query: bfloat16 [1024, 512], P(None, 'head'), may hold values from -0.1875 to 0.1875
- w_key: bfloat16 [1024, 512], P(None, 'head'), may hold values from -0.1875 to 0.1875
- w_value: bfloat16 [1024, 1024], P(None, 'head'), may hold values from -0.1875 to 0.1875
- w_out_gate: bfloat16 [1024, 1024], P(None, 'head'), may hold values from -0.1875 to 0.1875
- conv_query: float32 [4, 512], P(None, 'head'), may hold values from -3 to 3
- conv_key: float32 [4, 512], P(None, 'head'), may hold values from -3 to 3
- conv_value: float32 [4, 1024], P(None, 'head'), may hold values from -3 to 3
- out_gain: float32 [256], replicated, may hold values from 0.5 to 1.5
- w_out: bfloat16 [1024, 1024], P('head'), may hold values from -0.375 to 0.375
- mlp_gain: float32 [1024], replicated, may hold values from 0.5 to 1.5
- w_gate: bfloat16 [1024, 2816], P(None, 'head'), may hold values from -0.1875 to 0.1875
- w_up: bfloat16 [1024, 2816], P(None, 'head'), may hold values from -0.1875 to 0.1875
- w_down: bfloat16 [2816, 1024], P('head'), may hold values from -0.21875 to 0.21875
Outputs:
- layer_out: float32 [2, 8192, 1024], P(None, 'seq', 'head')
- tokens_grad: float32 [2, 8192, 1024], P(None, 'seq', 'head')
- attn_gain_grad: float32 [1024], P('head')
- w_query_grad: float32 [1024, 512], P(None, 'head')
- w_key_grad: float32 [1024, 512], P(None, 'head')
- w_value_grad: float32 [1024, 1024], P(None, 'head')
- w_out_gate_grad: float32 [1024, 1024], P(None, 'head')
- conv_query_grad: float32 [4, 512], P(None, 'head')
- conv_key_grad: float32 [4, 512], P(None, 'head')
- conv_value_grad: float32 [4, 1024], P(None, 'head')
- out_gain_grad: float32 [256], replicated
- w_out_grad: float32 [1024, 1024], P('head')
- mlp_gain_grad: float32 [1024], P('head')
- w_gate_grad: float32 [1024, 2816], P(None, 'head')
- w_up_grad: float32 [1024, 2816], P(None, 'head')
- w_down_grad: float32 [2816, 1024], P('head')
The draws below stay inside these ranges and needn't reach their ends.
All inputs are finite; a program needn't handle non-finite values.
Results may differ from the reference program's by a relative error of at most 0.035.
The reference program's roundings to bfloat16 on the way count: a program that leaves them out, or rounds other values in their place, can miss the bound.
Values may be sent and summed in bfloat16 or wider, within the bound.
A program may use at most 192 MiB of HBM per device.

```python
from functools import partial
import jax
import jax.numpy as jnp
from jax import lax

D = 1024
HEADS = 4
FF = 2816
SEQS = 2
LEN_DEV = 1024
SPAN = 64
CONV = 4
KEY_HEAD = 128
VALUE_HEAD = 256
KEY_DIM = 512
LENGTH = 8192
N_HEAD = 4


def draw_decay_codes(key, part):
    key = jax.random.fold_in(key, 11)
    subkeys = jax.random.split(key, 6)
    complete_shape = (SEQS, LENGTH, KEY_DIM)
    slow_low = max(1, 13107 // LENGTH)
    slow_high = max(slow_low + 1, 65536 // LENGTH)
    slow_codes = jax.random.randint(subkeys[0], complete_shape, slow_low, slow_high + 1)
    fast_codes = jax.random.randint(subkeys[1], complete_shape, 2621, 4370)
    chosen = jax.random.randint(subkeys[2], (SEQS, 1, KEY_DIM), 0, 2)
    baseline_codes = chosen * fast_codes + (1 - chosen) * slow_codes
    factor = jax.random.randint(subkeys[3], (SEQS, LENGTH // LEN_DEV, 1, 1), 1, 3)
    baseline_codes = (baseline_codes.reshape(SEQS, LENGTH // LEN_DEV, LEN_DEV, KEY_DIM) * factor).reshape(complete_shape)
    target_positions = jax.random.randint(subkeys[4], (SEQS, 2), 0, LENGTH - 3)
    spike_magnitude = jax.random.randint(subkeys[5], (SEQS, 2, KEY_DIM), 7300, 22701)
    spike_magnitude = spike_magnitude.at[:, 0, 0].set(32704)
    places = jnp.arange(LENGTH, dtype=jnp.int32)
    spike_events = jnp.zeros(complete_shape, jnp.int32)
    for spike_index in range(2):
        begin_offset = target_positions[:, spike_index:spike_index + 1]
        struck_mask = ((places[None, :] >= begin_offset) & (places[None, :] < begin_offset + 4)).astype(jnp.int32)
        spike_events = spike_events + struck_mask[:, :, None] * spike_magnitude[:, spike_index][:, None, :]
    return jnp.minimum(baseline_codes + spike_events, 32704).astype(jnp.int32)


def level_of(stream_key, shape, cuts, least, high):
    def one(dim, blocks):
        draws = jax.random.uniform(jax.random.fold_in(jax.random.fold_in(stream_key, 6), dim), (blocks,), jnp.float32, least / len(cuts), high / len(cuts))
        return jnp.repeat(jnp.exp(draws), shape[dim] // blocks).reshape((-1,) + (1,) * (len(shape) - dim - 1))

    gain = one(*cuts[0])
    for cut in cuts[1:]:
        gain = gain * one(*cut)
    return gain


def noise(stream_key, dims, spread, reach, cuts=(), kind=jnp.bfloat16):
    entries = spread * jax.random.normal(stream_key, dims, jnp.float32)
    if cuts:
        entries = entries * level_of(stream_key, dims, cuts, -0.22, 0.18)
    return jnp.clip(entries, -reach, reach).astype(kind)


def setup_inputs(seed: int = 0) -> dict:
    keys = jax.random.split(jax.random.key(seed), 18)
    return {
        "tokens": noise(keys[0], (SEQS, LENGTH, D), 1.0, 6.0, ((1, 8), (2, 4))),
        "decay_codes": draw_decay_codes(jax.random.fold_in(keys[17], 71), 0),
        "cotangent": noise(keys[2], (SEQS, LENGTH, D), 1.0, 6.0, ((1, 8), (2, 4))),
        "attn_gain": jnp.clip(1.0 + 0.1 * jax.random.normal(keys[3], (D,), jnp.float32), 0.5, 1.5),
        "w_query": noise(keys[4], (D, KEY_DIM), D ** -0.5, 0.1875, ((1, 4),)),
        "w_key": noise(keys[5], (D, KEY_DIM), D ** -0.5, 0.1875, ((1, 4),)),
        "w_value": noise(keys[6], (D, D), D ** -0.5, 0.1875, ((1, 4),)),
        "w_out_gate": noise(keys[7], (D, D), D ** -0.5, 0.1875, ((1, 4),)),
        "conv_query": noise(keys[8], (CONV, KEY_DIM), CONV ** -0.5, 3.0, ((1, 4),), jnp.float32),
        "conv_key": noise(keys[9], (CONV, KEY_DIM), CONV ** -0.5, 3.0, ((1, 4),), jnp.float32),
        "conv_value": noise(keys[10], (CONV, D), CONV ** -0.5, 3.0, ((1, 4),), jnp.float32),
        "out_gain": jnp.clip(1.0 + 0.1 * jax.random.normal(keys[11], (VALUE_HEAD,), jnp.float32), 0.5, 1.5),
        "w_out": noise(keys[12], (D, D), (D // 4) ** -0.5, 0.375, ((0, 4),)),
        "mlp_gain": jnp.clip(1.0 + 0.1 * jax.random.normal(keys[13], (D,), jnp.float32), 0.5, 1.5),
        "w_gate": noise(keys[14], (D, FF), D ** -0.5, 0.1875, ((1, 4),)),
        "w_up": noise(keys[15], (D, FF), D ** -0.5, 0.1875, ((1, 4),)),
        "w_down": noise(keys[16], (FF, D), (FF // 4) ** -0.5, 0.21875, ((0, 4),)),
    }


epsilon = 1e-06
decay_unit = 2.0 ** (-17)
highest = lax.Precision.HIGHEST

@jax.custom_vjp
def low(v):
    return lax.optimization_barrier(v.astype(jnp.bfloat16)).astype(jnp.float32)

@jax.custom_vjp
def low_back(v):
    return v

def low_keep(v):
    return (low(v), None)

def low_pass(kept, grad):
    return (grad,)

def back_keep(v):
    return (v, None)

def back_low(kept, grad):
    return (low(grad),)
low.defvjp(low_keep, low_pass)
low_back.defvjp(back_keep, back_low)

def rounded_both(values):
    return low(low_back(values))

def row_scale(values):
    return lax.rsqrt(lax.optimization_barrier(jnp.mean(values * values, axis=-1, keepdims=True)) + epsilon)

def matmul_high(left, right):
    return jnp.matmul(left, right, precision=highest)

def short_conv(pre_values, taps):
    width = taps.shape[0]
    length = pre_values.shape[1]
    padded = jnp.pad(pre_values, ((0, 0), (width - 1, 0), (0, 0)))
    total = jnp.zeros_like(pre_values)
    for offset in range(width):
        total = total + taps[offset] * padded[:, offset:offset + length]
    return total

def gated_linear(query, keyed, valued, log_decay):
    seqs, length, heads, key_head = query.shape
    value_head = valued.shape[-1]
    count = length // SPAN

    def blocks(values):
        return jnp.moveaxis(values.reshape(seqs, count, SPAN, heads, values.shape[-1]), 1, 0)
    positions = jnp.arange(SPAN)
    causal = positions[:, None] >= positions[None, :]

    def span_step(state, pieces):
        query_c, keyed_c, valued_c, decay_c = pieces
        cumul = jnp.cumsum(decay_c, axis=1)
        query_exp = query_c * key_head ** (-0.5) * jnp.exp(cumul)
        keyed_exp = keyed_c * jnp.exp(-cumul)
        span_log = cumul[:, -1]
        keyed_end = keyed_c * jnp.exp(span_log[:, None] - cumul)
        scores = jnp.einsum('sthk,suhk->shtu', query_exp, keyed_exp, precision=highest)
        scores = jnp.where(causal, scores, 0.0)
        output = jnp.einsum('shtu,suhv->sthv', scores, valued_c, precision=highest)
        output = output + jnp.einsum('sthk,shkv->sthv', query_exp, state, precision=highest)
        update = jnp.einsum('sthk,sthv->shkv', keyed_end, valued_c, precision=highest)
        state = jnp.exp(span_log)[..., None] * state + update
        return (state, output)
    start = jnp.zeros((seqs, heads, key_head, value_head), jnp.float32)
    final_state, outputs = lax.scan(jax.checkpoint(span_step), start, (blocks(query), blocks(keyed), blocks(valued), blocks(log_decay)))
    return jnp.moveaxis(outputs, 0, 1).reshape(seqs, length, heads, value_head)

def layer(log_decay, tokens, attn_gain, w_query, w_key, w_value, w_out_gate, conv_query, conv_key, conv_value, out_gain, w_out, mlp_gain, w_gate, w_up, w_down):
    seqs, length, width = tokens.shape
    normed = low(tokens * row_scale(tokens) * attn_gain)
    query_pre = rounded_both(matmul_high(normed, w_query))
    key_pre = rounded_both(matmul_high(normed, w_key))
    value_pre = rounded_both(matmul_high(normed, w_value))
    gate_pre = rounded_both(matmul_high(normed, w_out_gate)).reshape(seqs, length, HEADS, VALUE_HEAD)
    query = jax.nn.silu(short_conv(query_pre, conv_query)).reshape(seqs, length, HEADS, KEY_HEAD)
    keyed = jax.nn.silu(short_conv(key_pre, conv_key)).reshape(seqs, length, HEADS, KEY_HEAD)
    valued = jax.nn.silu(short_conv(value_pre, conv_value)).reshape(seqs, length, HEADS, VALUE_HEAD)
    core = gated_linear(query, keyed, valued, log_decay.reshape(seqs, length, HEADS, KEY_HEAD))
    normed_out = core * row_scale(core) * out_gain
    gated = rounded_both(normed_out * jax.nn.silu(gate_pre)).reshape(seqs, length, N_HEAD, D // N_HEAD)
    mixer_parts = low(jnp.einsum('slgc,gcd->slgd', gated, w_out.reshape(N_HEAD, D // N_HEAD, D), precision=highest))
    mixer = low_back(lax.optimization_barrier(jnp.sum(mixer_parts, axis=2)))
    hidden_in = tokens + mixer
    normed_two = low(hidden_in * row_scale(hidden_in) * mlp_gain)
    gate_val = low_back(matmul_high(normed_two, w_gate))
    up_val = low_back(matmul_high(normed_two, w_up))
    hidden = rounded_both(jax.nn.silu(gate_val) * up_val).reshape(seqs, length, N_HEAD, FF // N_HEAD)
    mlp_parts = low(jnp.einsum('slgf,gfd->slgd', hidden, w_down.reshape(N_HEAD, FF // N_HEAD, D), precision=highest))
    return hidden_in + low_back(lax.optimization_barrier(jnp.sum(mlp_parts, axis=2)))

def reference(tokens, decay_codes, cotangent, attn_gain, w_query, w_key, w_value, w_out_gate, conv_query, conv_key, conv_value, out_gain, w_out, mlp_gain, w_gate, w_up, w_down):
    log_decay = -decay_codes.astype(jnp.float32) * decay_unit
    params = (tokens.astype(jnp.float32), attn_gain, w_query.astype(jnp.float32), w_key.astype(jnp.float32), w_value.astype(jnp.float32), w_out_gate.astype(jnp.float32), conv_query, conv_key, conv_value, out_gain, w_out.astype(jnp.float32), mlp_gain, w_gate.astype(jnp.float32), w_up.astype(jnp.float32), w_down.astype(jnp.float32))
    output, pullback = jax.vjp(partial(layer, log_decay), *params)
    grads = pullback(cotangent.astype(jnp.float32))
    return (output, grads[0], grads[1], grads[2], grads[3], grads[4], grads[5], grads[6], grads[7], grads[8], grads[9], grads[10], grads[11], grads[12], grads[13], grads[14])
```

```python
from functools import partial

import jax
import jax.numpy as jnp
from jax import lax
from jax.sharding import PartitionSpec as P

SPAN = 64
KEY_HEAD = 128

epsilon = 1e-06
decay_unit = 2.0 ** (-17)
BOTH = ("seq", "head")
f32 = jnp.float32
bf16 = jnp.bfloat16


def shifted(block, distance):
    count = lax.axis_size("seq") * lax.axis_size("head")
    route = [(i - distance, i) for i in range(count) if 0 <= i - distance < count]
    return lax.ppermute(block, BOTH, route)


def row_scale(values):
    return lax.rsqrt(jnp.mean(values * values, axis=-1, keepdims=True) + epsilon)


def silu_slope(values):
    logistic = jax.nn.sigmoid(values)
    return logistic * (1.0 + values * (1.0 - logistic))


def norm_back(values, inverse, weights, upstream):
    weighted = weights * upstream
    return inverse * weighted - values * inverse**3 * jnp.mean(
        weighted * values, axis=-1, keepdims=True
    )


def rounded(values):
    return values.astype(bf16).astype(f32)


def dot(spec, left, right):
    return jnp.einsum(spec, left.astype(bf16), right.astype(bf16), preferred_element_type=f32)


def cumulated(spec, values, count):
    at = jnp.arange(count)
    lower = (at[:, None] >= at[None, :]).astype(f32)
    return jnp.einsum(spec, lower, values, precision=lax.Precision.HIGHEST, preferred_element_type=f32)


def whole(weight):
    seq = lax.axis_size("seq")
    part = weight.shape[0] // seq
    mine = lax.dynamic_slice_in_dim(weight, lax.axis_index("seq") * part, part, 0)
    every = lax.all_gather(mine, ("head", "seq"), axis=0, tiled=True)
    return every.reshape(lax.axis_size("head"), *weight.shape)


def reduced(grad):
    flat = grad.astype(bf16).reshape(-1, grad.shape[-1])
    mine = lax.psum_scatter(flat, ("head", "seq"), scatter_dimension=0, tiled=True)
    return lax.all_gather(mine, "seq", axis=0, tiled=True).astype(f32)


def exchange(log_total, value, back):
    count = lax.axis_size("seq") * lax.axis_size("head")
    rows, width = value.shape
    part = rows // count
    pieces = lax.all_to_all(value.astype(bf16).reshape(count, part, width), BOTH, 0, 0, tiled=True)
    logs = lax.all_to_all(log_total.reshape(count, part), BOTH, 0, 0, tiled=True)
    upto = cumulated("pq,qr->pr", logs, count)
    before = upto - logs
    at = jnp.arange(count)
    if back:
        mask = at[:, None] < at[None, :]
        gap = before[None, :] - upto[:, None]
    else:
        mask = at[:, None] > at[None, :]
        gap = before[:, None] - upto[None, :]
    weight = jnp.where(mask[:, :, None], jnp.exp(jnp.minimum(gap, 0.0)), 0.0)
    total = jnp.einsum(
        "pqr,qrv->prv", weight, pieces.astype(f32), preferred_element_type=f32, precision=lax.Precision.HIGHEST
    )
    ours = lax.all_to_all(total.astype(bf16), BOTH, 0, 0, tiled=True)
    return ours.reshape(rows, width).astype(f32)


def local(
    tokens,
    decay_codes,
    cotangent,
    attn_gain,
    w_query,
    w_key,
    w_value,
    w_out_gate,
    conv_query,
    conv_key,
    conv_value,
    out_gain,
    w_out,
    mlp_gain,
    w_gate,
    w_up,
    w_down,
):
    seqs, rows, own_width = tokens.shape
    heads = lax.axis_size("head")
    own_head = lax.axis_index("head")
    mine = rows // heads

    def to_tokens(array):
        return lax.all_to_all(array, "head", 1, 2, tiled=True)

    def to_features(array):
        return lax.all_to_all(array, "head", 2, 1, tiled=True)

    resid = to_tokens(tokens).astype(f32)
    codes = to_tokens(decay_codes.astype(jnp.int16))
    upstream = to_tokens(cotangent)
    key_width = w_query.shape[1]
    value_width = w_value.shape[1]
    conv_width = 2 * key_width + value_width
    w_mixer = whole(jnp.concatenate([w_query, w_key, w_value, w_out_gate], axis=1))
    w_proj = whole(w_out)
    w_pair = whole(jnp.concatenate([w_gate, w_up], axis=1))
    w_low = whole(w_down)
    taps = lax.all_gather(jnp.concatenate([conv_query, conv_key, conv_value], axis=1), "head")

    first_scale = row_scale(resid)
    normed = (resid * first_scale * attn_gain).astype(bf16)
    projected = dot("std,hde->hste", normed, w_mixer).astype(bf16)
    mixed_in = projected[..., :conv_width]
    gate_rows = projected[..., conv_width:].astype(f32)
    tap_count = taps.shape[1]
    edge_rows = shifted(mixed_in[:, :, mine - tap_count + 1 :], 1)
    extended = jnp.concatenate([edge_rows, mixed_in], axis=2).astype(f32)
    conv_sum = sum(
        taps[:, j, None, None, :] * extended[:, :, j : j + mine] for j in range(tap_count)
    )
    activated = jax.nn.silu(conv_sum)
    blocks = mine // SPAN

    def spanned(values):
        return values.reshape(heads, seqs, blocks, SPAN, values.shape[-1])

    query = spanned(activated[..., :key_width])
    keyed = spanned(activated[..., key_width : 2 * key_width])
    valued = spanned(activated[..., 2 * key_width :])
    log_decay = -codes.astype(f32) * decay_unit
    log_decay = jnp.moveaxis(log_decay.reshape(seqs, blocks, SPAN, heads, key_width), 3, 0)
    cumul = cumulated("tu,hanuk->hantk", log_decay, SPAN)
    span_log = cumul[:, :, :, -1]
    running = cumulated("mn,hank->hamk", span_log, blocks)
    carry_decay = jnp.exp(running - span_log)
    log_total = running[:, :, -1]
    positions = jnp.arange(SPAN)
    causal = positions[:, None] >= positions[None, :]
    grow = jnp.exp(cumul)
    shrink = jnp.exp(-cumul)
    to_end = jnp.exp(span_log[:, :, :, None] - cumul)
    scale = key_width ** (-0.5)
    query_exp = query * scale * grow
    keyed_exp = keyed * shrink
    keyed_end = keyed * to_end
    scores = jnp.where(causal, dot("hantk,hanuk->hantu", query_exp, keyed_exp), 0.0)
    inner = dot("hantu,hanuv->hantv", scores, valued)
    update = dot("hantk,hantv->hankv", keyed_end, valued)
    span_decay = jnp.exp(span_log)
    starts = [jnp.zeros_like(update[:, :, 0])]
    for n in range(blocks):
        starts.append(span_decay[:, :, n, :, None] * starts[n] + update[:, :, n])
    local_end = starts.pop()
    flat = (-1, value_width)
    incoming = exchange(log_total.reshape(-1), local_end.reshape(flat), False).reshape(local_end.shape)
    states = jnp.stack(starts, 2) + carry_decay[..., None] * incoming[:, :, None]
    core_rows = (inner + dot("hantk,hankv->hantv", query_exp, states)).reshape(heads, seqs, mine, value_width)
    out_scale = row_scale(core_rows)
    normed_out = core_rows * out_scale * out_gain
    gate_silu = jax.nn.silu(gate_rows)
    gated = (normed_out * gate_silu).astype(bf16)
    mixer = jnp.sum(rounded(dot("hste,hed->hstd", gated, w_proj)), axis=0)
    hidden_in = resid + mixer
    second_scale = row_scale(hidden_in)
    normed_two = (hidden_in * second_scale * mlp_gain).astype(bf16)
    gate_up = dot("std,hdf->hstf", normed_two, w_pair)
    ff_here = w_gate.shape[1]
    gate_val = gate_up[..., :ff_here]
    up_val = gate_up[..., ff_here:]
    gate_act = jax.nn.silu(gate_val)
    hidden = (gate_act * up_val).astype(bf16)
    layer_out = hidden_in + jnp.sum(rounded(dot("hstf,hfd->hstd", hidden, w_low)), axis=0)
    layer_out = to_features(layer_out.astype(bf16)).astype(f32)

    d_hidden = rounded(dot("std,hfd->hstf", upstream, w_low))
    grad_down = reduced(dot("hstf,std->hfd", hidden, upstream))
    d_gate_up = jnp.concatenate(
        [d_hidden * up_val * silu_slope(gate_val), d_hidden * gate_act], axis=-1
    ).astype(bf16)
    grad_pair = reduced(dot("std,hstf->hdf", normed_two, d_gate_up))
    d_normed_two = dot("hstf,hdf->std", d_gate_up, w_pair)
    d_hidden_in = upstream.astype(f32) + norm_back(hidden_in, second_scale, mlp_gain, d_normed_two)
    grad_mlp_gain = jnp.sum(d_normed_two * hidden_in * second_scale, axis=(0, 1))
    d_mixer = d_hidden_in.astype(bf16)
    grad_out = reduced(dot("hste,std->hed", gated, d_mixer))
    d_gated = rounded(dot("std,hed->hste", d_mixer, w_proj))
    d_normed_out = d_gated * gate_silu
    d_gate_rows = d_gated * normed_out * silu_slope(gate_rows)
    grad_out_gain = jnp.sum(d_normed_out * core_rows * out_scale, axis=(0, 1, 2))
    d_core = norm_back(core_rows, out_scale, out_gain, d_normed_out)
    d_core = spanned(d_core)

    d_states = dot("hantk,hantv->hankv", query_exp, d_core)
    own_grad = jnp.sum(carry_decay[..., None] * d_states, axis=2)
    leaving = exchange(log_total.reshape(-1), own_grad.reshape(flat), True).reshape(own_grad.shape)
    d_ends = [leaving]
    for n in range(blocks - 1, 0, -1):
        d_ends.append(span_decay[:, :, n, :, None] * d_ends[-1] + d_states[:, :, n])
    d_ends = jnp.stack(d_ends[::-1], 2)
    d_scores = jnp.where(causal, dot("hantv,hanuv->hantu", d_core, valued), 0.0)
    d_query = dot("hantu,hanuk->hantk", d_scores, keyed_exp) + dot("hantv,hankv->hantk", d_core, states)
    d_query = d_query * scale * grow
    d_keyed = dot("hantu,hantk->hanuk", d_scores, query_exp) * shrink + dot("hanuv,hankv->hanuk", valued, d_ends) * to_end
    d_valued = dot("hantu,hantv->hanuv", scores, d_core) + dot("hanuk,hankv->hanuv", keyed_end, d_ends)
    d_activated = jnp.concatenate(
        [a.reshape(heads, seqs, mine, -1) for a in (d_query, d_keyed, d_valued)], axis=-1
    )
    d_conv = d_activated * silu_slope(conv_sum)
    tap_grads = []
    d_extended = jnp.zeros(extended.shape, f32)
    for j in range(tap_count):
        tap_grads.append(jnp.sum(d_conv * extended[:, :, j : j + mine], axis=(1, 2)))
        d_extended = d_extended + jnp.pad(
            taps[:, j, None, None, :] * d_conv, ((0, 0), (0, 0), (j, tap_count - 1 - j), (0, 0))
        )
    grad_taps = jnp.stack(tap_grads)
    edge_back = shifted(d_extended[:, :, : tap_count - 1], -1)
    d_mixed = d_extended[:, :, tap_count - 1 :] + jnp.pad(
        edge_back, ((0, 0), (0, 0), (mine - tap_count + 1, 0), (0, 0))
    )
    d_projected = jnp.concatenate([d_mixed, d_gate_rows], axis=-1).astype(bf16)
    grad_mixer = reduced(dot("std,hste->hde", normed, d_projected))
    d_normed = dot("hste,hde->std", d_projected, w_mixer)
    tokens_grad = d_hidden_in + norm_back(resid, first_scale, attn_gain, d_normed)
    tokens_grad = to_features(tokens_grad.astype(bf16)).astype(f32)
    grad_attn_gain = jnp.sum(d_normed * resid * first_scale, axis=(0, 1))

    small = jnp.concatenate([grad_attn_gain, grad_mlp_gain, grad_out_gain, grad_taps.reshape(-1)])
    small = lax.psum(small.astype(bf16), BOTH).astype(f32)
    width = grad_attn_gain.shape[0]
    own = own_head * own_width
    grad_attn_gain = lax.dynamic_slice_in_dim(small[:width], own, own_width, 0)
    grad_mlp_gain = lax.dynamic_slice_in_dim(small[width : 2 * width], own, own_width, 0)
    grad_out_gain = small[2 * width : 2 * width + value_width]
    grad_taps = small[2 * width + value_width :].reshape(grad_taps.shape)
    grad_taps = lax.dynamic_index_in_dim(grad_taps, own_head, 1, False)
    return (
        layer_out,
        tokens_grad,
        grad_attn_gain,
        grad_mixer[:, :key_width],
        grad_mixer[:, key_width : 2 * key_width],
        grad_mixer[:, 2 * key_width : conv_width],
        grad_mixer[:, conv_width:],
        grad_taps[:, :key_width],
        grad_taps[:, key_width : 2 * key_width],
        grad_taps[:, 2 * key_width :],
        grad_out_gain,
        grad_out,
        grad_mlp_gain,
        grad_pair[:, :ff_here],
        grad_pair[:, ff_here:],
        grad_down,
    )

def solution(mesh):
    in_specs = (
        P(None, "seq", "head"),
        P(None, "seq", "head"),
        P(None, "seq", "head"),
        P(),
        P(None, "head"),
        P(None, "head"),
        P(None, "head"),
        P(None, "head"),
        P(None, "head"),
        P(None, "head"),
        P(None, "head"),
        P(),
        P("head", None),
        P(),
        P(None, "head"),
        P(None, "head"),
        P("head", None),
    )
    out_specs = (
        P(None, "seq", "head"),
        P(None, "seq", "head"),
        P("head"),
        P(None, "head"),
        P(None, "head"),
        P(None, "head"),
        P(None, "head"),
        P(None, "head"),
        P(None, "head"),
        P(None, "head"),
        P(),
        P("head", None),
        P("head"),
        P(None, "head"),
        P(None, "head"),
        P("head", None),
    )
    return jax.shard_map(local, mesh=mesh, in_specs=in_specs, out_specs=out_specs, check_vma=False)
```

```python
from functools import partial

import jax
import jax.numpy as jnp
from jax import lax
from jax.experimental import pallas as pl
from jax.experimental.pallas import tpu as pltpu
from jax.sharding import PartitionSpec as P

SPAN = 64
KEY_HEAD = 128

epsilon = 1e-06
decay_unit = 2.0 ** (-17)
BOTH = ("seq", "head")
f32 = jnp.float32
bf16 = jnp.bfloat16


MESH = pl.DeviceIdType.MESH


def bits_of(count):
    return [1 << k for k in range(count.bit_length() - 1)]

def reduce_body(seq, head, plan, n_arrays, *refs):
    grads, outs, scratch = refs[:n_arrays], refs[n_arrays : 2 * n_arrays], refs[2 * n_arrays :]
    s, z = lax.axis_index("seq"), lax.axis_index("head")
    seq_bits, head_bits = bits_of(seq), bits_of(head)
    ns, nz = len(seq_bits), len(head_bits)
    per = 1 + ns + nz
    owns = scratch[: len(plan)]
    recvs = [scratch[len(plan) + i * (ns + nz) : len(plan) + (i + 1) * (ns + nz)] for i in range(len(plan))]
    load_sem, send_sem, recv_sem, zsend, zrecv, gsend, grecv, keep_sem = scratch[len(plan) * per :]

    def flip(place, mask):
        return place + mask - 2 * mask * (place // mask % 2)

    def seq_peer(mask):
        return {"seq": flip(s, mask), "head": z}

    def head_peer(mask):
        return {"seq": s, "head": flip(z, mask)}

    barrier = pltpu.get_barrier_semaphore()
    for mask in seq_bits:
        pl.semaphore_signal(barrier, 1, device_id=seq_peer(mask), device_id_type=MESH)
    for mask in head_bits:
        pl.semaphore_signal(barrier, 1, device_id=head_peer(mask), device_id_type=MESH)
    pl.semaphore_wait(barrier, ns + nz)

    def masks(c):
        rest = seq_bits[1:]
        return seq_bits[:1] + (rest if c % 2 == 0 else rest[::-1])

    def rows_of(c):
        return plan[c][2]

    def bit(c, k):
        return s // masks(c)[k] % 2

    def kept(c, k):
        size = rows_of(c)
        return sum((bit(c, j) * (size >> (j + 1)) for j in range(1, k + 1)), 0)

    def aligned(x, size):
        return pl.multiple_of(x, size) if not isinstance(x, int) else x

    def seq_copy(c, k):
        array, first, size = plan[c]
        half = size >> (k + 1)
        other = (1 - bit(c, k)) * half
        if k == 0:
            source = grads[array].at[:, pl.ds(aligned(first + other, half), half)]
        else:
            source = owns[c].at[:, pl.ds(aligned(kept(c, k - 1) + other, half), half)]
        return pltpu.make_async_remote_copy(
            source, recvs[c][k], send_sem.at[c, k], recv_sem.at[c, k],
            device_id=seq_peer(masks(c)[k]), device_id_type=MESH)

    def load(c):
        array, first, size = plan[c]
        half = size // 2
        return pltpu.make_async_copy(
            grads[array].at[:, pl.ds(aligned(first + bit(c, 0) * half, half), half)], owns[c], load_sem.at[c])

    def quarters(k):
        low = z % (1 << k)
        return [low + (i << k) for i in range(head >> k)]

    def head_copies(c, k):
        size = rows_of(c) // seq
        at = pl.ds(aligned(kept(c, ns - 1), size), size)
        low = z % (1 << k)
        b = z // (1 << k) % 2
        copies = []
        for i in range(head >> (k + 1)):
            q = low + (1 - b) * (1 << k) + (i << (k + 1))
            copies.append(pltpu.make_async_remote_copy(
                owns[c].at[q, at], recvs[c][ns + k].at[i], zsend.at[c, k, i], zrecv.at[c, k, i],
                device_id=head_peer(1 << k), device_id_type=MESH))
        return copies

    def add(c, k):
        size = rows_of(c)
        if k < ns:
            many, rows, first = head, size >> (k + 1), kept(c, k)
            place = lambda i: i
        else:
            j = k - ns
            many, rows, first = head >> (j + 1), size // seq, kept(c, ns - 1)
            place = lambda i: z % (1 << j) + (z // (1 << j) % 2) * (1 << j) + i * (1 << (j + 1))
        tile = min(16, rows)
        tiles = rows // tile
        received = recvs[c][k]

        def one(t, carry):
            i, r = t // tiles, t % tiles * tile
            here = pl.ds(pl.multiple_of(first + r, tile), tile)
            q = place(i)
            owns[c][q, here] = (
                owns[c][q, here].astype(f32) + received[i, pl.ds(pl.multiple_of(r, tile), tile)].astype(f32)
            ).astype(bf16)
            return carry

        lax.fori_loop(0, many * tiles, one, 0)

    def result_row(c, upto):
        array, first, size = plan[c]
        return first + sum(bit(c, j) * (size >> (j + 1)) for j in range(upto))

    def keep(c):
        array, first, size = plan[c]
        rows = size // seq
        return pltpu.make_async_copy(
            owns[c].at[z, pl.ds(aligned(kept(c, ns - 1), rows), rows)],
            outs[array].at[pl.ds(aligned(result_row(c, ns), rows), rows)], keep_sem.at[c])

    def gather_copy(c, j):
        array, first, size = plan[c]
        level = ns - j
        rows = size >> level
        at = pl.ds(aligned(result_row(c, level), rows), rows)
        return pltpu.make_async_remote_copy(
            outs[array].at[at], outs[array].at[at], gsend.at[c, j], grecv.at[c, j],
            device_id=seq_peer(masks(c)[level - 1]), device_id_type=MESH)

    count = len(plan)
    for c in range(count):
        seq_copy(c, 0).start()
        load(c).start()

    def advance(c, k):
        if k == 0:
            load(c).wait()
        if k < ns:
            seq_copy(c, k).wait_recv()
            add(c, k)
        elif k < ns + nz:
            for copy in head_copies(c, k - ns):
                copy.wait_recv()
            add(c, k)
        elif k == ns + nz:
            keep(c).wait()
        else:
            gather_copy(c, k - ns - nz - 1).wait_recv()
        n = k + 1
        if n < ns:
            seq_copy(c, n).start()
        elif n < ns + nz:
            for copy in head_copies(c, n - ns):
                copy.start()
        elif n == ns + nz:
            keep(c).start()
        elif n - ns - nz - 1 < ns:
            gather_copy(c, n - ns - nz - 1).start()

    stages = ns + nz + 1 + ns
    pairs = count // 2
    for t in range(pairs + stages - 1):
        for k in reversed(range(stages)):
            p = t - k
            if 0 <= p < pairs:
                advance(2 * p, k)
                advance(2 * p + 1, k)
    for c in range(count):
        for k in range(ns):
            seq_copy(c, k).wait_send()
        for k in range(nz):
            for copy in head_copies(c, k):
                copy.wait_send()
        for j in range(ns):
            gather_copy(c, j).wait_send()

def reduce_all(arrays, cuts, collective_id):
    seq, head = lax.axis_size("seq"), lax.axis_size("head")
    ns, nz = len(bits_of(seq)), len(bits_of(head))
    plan = []
    for a, (array, cut) in enumerate(zip(arrays, cuts)):
        rows = array.shape[1] // cut
        plan += [(a, i * rows, rows) for i in range(cut)]
    scratch = []
    for a, first, size in plan:
        scratch.append(pltpu.VMEM((head, size // 2, arrays[a].shape[2]), bf16))
    for a, first, size in plan:
        columns = arrays[a].shape[2]
        scratch += [pltpu.VMEM((head, size >> (k + 1), columns), bf16) for k in range(ns)]
        scratch += [pltpu.VMEM((head >> (k + 1), size // seq, columns), bf16) for k in range(nz)]
    count = len(plan)
    dma = pltpu.SemaphoreType.DMA
    scratch += [dma((count,)), dma((count, ns)), dma((count, ns)), dma((count, nz, head // 2)), dma((count, nz, head // 2)),
                dma((count, ns)), dma((count, ns)), dma((count,))]
    anywhere = pl.BlockSpec(memory_space=pl.ANY)
    return pl.pallas_call(
        partial(reduce_body, seq, head, plan, len(arrays)),
        out_shape=[jax.ShapeDtypeStruct(a.shape[1:], bf16) for a in arrays],
        in_specs=[anywhere] * len(arrays),
        out_specs=[anywhere] * len(arrays),
        scratch_shapes=scratch,
        compiler_params=pltpu.CompilerParams(
            collective_id=collective_id, has_side_effects=True, vmem_limit_bytes=60 * 2**20),
        name="reduce_gradients",
    )(*arrays)


def shifted(block, distance):
    count = lax.axis_size("seq") * lax.axis_size("head")
    route = [(i - distance, i) for i in range(count) if 0 <= i - distance < count]
    return lax.ppermute(block, BOTH, route)


def row_scale(values):
    return lax.rsqrt(jnp.mean(values * values, axis=-1, keepdims=True) + epsilon)


def silu_slope(values):
    logistic = jax.nn.sigmoid(values)
    return logistic * (1.0 + values * (1.0 - logistic))


def norm_back(values, inverse, weights, upstream):
    weighted = weights * upstream
    return inverse * weighted - values * inverse**3 * jnp.mean(
        weighted * values, axis=-1, keepdims=True
    )


def rounded(values):
    return values.astype(bf16).astype(f32)


def dot(spec, left, right):
    return jnp.einsum(spec, left.astype(bf16), right.astype(bf16), preferred_element_type=f32)


def cumulated(spec, values, count):
    at = jnp.arange(count)
    lower = (at[:, None] >= at[None, :]).astype(f32)
    return jnp.einsum(spec, lower, values, precision=lax.Precision.HIGHEST, preferred_element_type=f32)


def whole(weight):
    seq = lax.axis_size("seq")
    part = weight.shape[0] // seq
    mine = lax.dynamic_slice_in_dim(weight, lax.axis_index("seq") * part, part, 0)
    every = lax.all_gather(mine, ("head", "seq"), axis=0, tiled=True)
    return every.reshape(lax.axis_size("head"), *weight.shape)


def exchange(log_total, value, back):
    count = lax.axis_size("seq") * lax.axis_size("head")
    rows, width = value.shape
    part = rows // count
    pieces = lax.all_to_all(value.astype(bf16).reshape(count, part, width), BOTH, 0, 0, tiled=True)
    logs = lax.all_to_all(log_total.reshape(count, part), BOTH, 0, 0, tiled=True)
    upto = cumulated("pq,qr->pr", logs, count)
    before = upto - logs
    at = jnp.arange(count)
    if back:
        mask = at[:, None] < at[None, :]
        gap = before[None, :] - upto[:, None]
    else:
        mask = at[:, None] > at[None, :]
        gap = before[:, None] - upto[None, :]
    weight = jnp.where(mask[:, :, None], jnp.exp(jnp.minimum(gap, 0.0)), 0.0)
    total = jnp.einsum(
        "pqr,qrv->prv", weight, pieces.astype(f32), preferred_element_type=f32, precision=lax.Precision.HIGHEST
    )
    ours = lax.all_to_all(total.astype(bf16), BOTH, 0, 0, tiled=True)
    return ours.reshape(rows, width).astype(f32)


def local(
    tokens,
    decay_codes,
    cotangent,
    attn_gain,
    w_query,
    w_key,
    w_value,
    w_out_gate,
    conv_query,
    conv_key,
    conv_value,
    out_gain,
    w_out,
    mlp_gain,
    w_gate,
    w_up,
    w_down,
):
    seqs, rows, own_width = tokens.shape
    heads = lax.axis_size("head")
    own_head = lax.axis_index("head")
    mine = rows // heads

    def to_tokens(array):
        return lax.all_to_all(array, "head", 1, 2, tiled=True)

    def to_features(array):
        return lax.all_to_all(array, "head", 2, 1, tiled=True)

    resid = to_tokens(tokens).astype(f32)
    codes = to_tokens(decay_codes.astype(jnp.int16))
    upstream = to_tokens(cotangent)
    key_width = w_query.shape[1]
    value_width = w_value.shape[1]
    conv_width = 2 * key_width + value_width
    w_mixer = whole(jnp.concatenate([w_query, w_key, w_value, w_out_gate], axis=1))
    w_proj = whole(w_out)
    w_pair = whole(jnp.concatenate([w_gate, w_up], axis=1))
    w_low = whole(w_down)
    taps = lax.all_gather(jnp.concatenate([conv_query, conv_key, conv_value], axis=1), "head")

    first_scale = row_scale(resid)
    normed = (resid * first_scale * attn_gain).astype(bf16)
    projected = dot("std,hde->hste", normed, w_mixer).astype(bf16)
    mixed_in = projected[..., :conv_width]
    gate_rows = projected[..., conv_width:].astype(f32)
    tap_count = taps.shape[1]
    edge_rows = shifted(mixed_in[:, :, mine - tap_count + 1 :], 1)
    extended = jnp.concatenate([edge_rows, mixed_in], axis=2).astype(f32)
    conv_sum = sum(
        taps[:, j, None, None, :] * extended[:, :, j : j + mine] for j in range(tap_count)
    )
    activated = jax.nn.silu(conv_sum)
    blocks = mine // SPAN

    def spanned(values):
        return values.reshape(heads, seqs, blocks, SPAN, values.shape[-1])

    query = spanned(activated[..., :key_width])
    keyed = spanned(activated[..., key_width : 2 * key_width])
    valued = spanned(activated[..., 2 * key_width :])
    log_decay = -codes.astype(f32) * decay_unit
    log_decay = jnp.moveaxis(log_decay.reshape(seqs, blocks, SPAN, heads, key_width), 3, 0)
    cumul = cumulated("tu,hanuk->hantk", log_decay, SPAN)
    span_log = cumul[:, :, :, -1]
    running = cumulated("mn,hank->hamk", span_log, blocks)
    carry_decay = jnp.exp(running - span_log)
    log_total = running[:, :, -1]
    positions = jnp.arange(SPAN)
    causal = positions[:, None] >= positions[None, :]
    grow = jnp.exp(cumul)
    shrink = jnp.exp(-cumul)
    to_end = jnp.exp(span_log[:, :, :, None] - cumul)
    scale = key_width ** (-0.5)
    query_exp = query * scale * grow
    keyed_exp = keyed * shrink
    keyed_end = keyed * to_end
    scores = jnp.where(causal, dot("hantk,hanuk->hantu", query_exp, keyed_exp), 0.0)
    inner = dot("hantu,hanuv->hantv", scores, valued)
    update = dot("hantk,hantv->hankv", keyed_end, valued)
    span_decay = jnp.exp(span_log)
    starts = [jnp.zeros_like(update[:, :, 0])]
    for n in range(blocks):
        starts.append(span_decay[:, :, n, :, None] * starts[n] + update[:, :, n])
    local_end = starts.pop()
    flat = (-1, value_width)
    incoming = exchange(log_total.reshape(-1), local_end.reshape(flat), False).reshape(local_end.shape)
    states = jnp.stack(starts, 2) + carry_decay[..., None] * incoming[:, :, None]
    core_rows = (inner + dot("hantk,hankv->hantv", query_exp, states)).reshape(heads, seqs, mine, value_width)
    out_scale = row_scale(core_rows)
    normed_out = core_rows * out_scale * out_gain
    gate_silu = jax.nn.silu(gate_rows)
    gated = (normed_out * gate_silu).astype(bf16)
    mixer = jnp.sum(rounded(dot("hste,hed->hstd", gated, w_proj)), axis=0)
    hidden_in = resid + mixer
    second_scale = row_scale(hidden_in)
    normed_two = (hidden_in * second_scale * mlp_gain).astype(bf16)
    gate_up = dot("std,hdf->hstf", normed_two, w_pair)
    ff_here = w_gate.shape[1]
    gate_val = gate_up[..., :ff_here]
    up_val = gate_up[..., ff_here:]
    gate_act = jax.nn.silu(gate_val)
    hidden = (gate_act * up_val).astype(bf16)
    layer_out = hidden_in + jnp.sum(rounded(dot("hstf,hfd->hstd", hidden, w_low)), axis=0)
    layer_out = to_features(layer_out.astype(bf16)).astype(f32)

    d_hidden = rounded(dot("std,hfd->hstf", upstream, w_low))
    grad_down = dot("std,hstf->hdf", upstream, hidden).astype(bf16)
    d_gate_up = jnp.concatenate(
        [d_hidden * up_val * silu_slope(gate_val), d_hidden * gate_act], axis=-1
    ).astype(bf16)
    grad_pair = dot("std,hstf->hdf", normed_two, d_gate_up).astype(bf16)
    d_normed_two = dot("hstf,hdf->std", d_gate_up, w_pair)
    d_hidden_in = upstream.astype(f32) + norm_back(hidden_in, second_scale, mlp_gain, d_normed_two)
    grad_mlp_gain = jnp.sum(d_normed_two * hidden_in * second_scale, axis=(0, 1))
    d_mixer = d_hidden_in.astype(bf16)
    grad_out = dot("std,hste->hde", d_mixer, gated)
    d_gated = rounded(dot("std,hed->hste", d_mixer, w_proj))
    d_normed_out = d_gated * gate_silu
    d_gate_rows = d_gated * normed_out * silu_slope(gate_rows)
    grad_out_gain = jnp.sum(d_normed_out * core_rows * out_scale, axis=(0, 1, 2))
    d_core = norm_back(core_rows, out_scale, out_gain, d_normed_out)
    d_core = spanned(d_core)

    d_states = dot("hantk,hantv->hankv", query_exp, d_core)
    own_grad = jnp.sum(carry_decay[..., None] * d_states, axis=2)
    leaving = exchange(log_total.reshape(-1), own_grad.reshape(flat), True).reshape(own_grad.shape)
    d_ends = [leaving]
    for n in range(blocks - 1, 0, -1):
        d_ends.append(span_decay[:, :, n, :, None] * d_ends[-1] + d_states[:, :, n])
    d_ends = jnp.stack(d_ends[::-1], 2)
    d_scores = jnp.where(causal, dot("hantv,hanuv->hantu", d_core, valued), 0.0)
    d_query = dot("hantu,hanuk->hantk", d_scores, keyed_exp) + dot("hantv,hankv->hantk", d_core, states)
    d_query = d_query * scale * grow
    d_keyed = dot("hantu,hantk->hanuk", d_scores, query_exp) * shrink + dot("hanuv,hankv->hanuk", valued, d_ends) * to_end
    d_valued = dot("hantu,hantv->hanuv", scores, d_core) + dot("hanuk,hankv->hanuv", keyed_end, d_ends)
    d_activated = jnp.concatenate(
        [a.reshape(heads, seqs, mine, -1) for a in (d_query, d_keyed, d_valued)], axis=-1
    )
    d_conv = d_activated * silu_slope(conv_sum)
    tap_grads = []
    d_extended = jnp.zeros(extended.shape, f32)
    for j in range(tap_count):
        tap_grads.append(jnp.sum(d_conv * extended[:, :, j : j + mine], axis=(1, 2)))
        d_extended = d_extended + jnp.pad(
            taps[:, j, None, None, :] * d_conv, ((0, 0), (0, 0), (j, tap_count - 1 - j), (0, 0))
        )
    grad_taps = jnp.stack(tap_grads)
    edge_back = shifted(d_extended[:, :, : tap_count - 1], -1)
    d_mixed = d_extended[:, :, tap_count - 1 :] + jnp.pad(
        edge_back, ((0, 0), (0, 0), (mine - tap_count + 1, 0), (0, 0))
    )
    d_projected = jnp.concatenate([d_mixed, d_gate_rows], axis=-1).astype(bf16)
    grad_mixer = dot("std,hste->hde", normed, d_projected)
    grad_mixer = jnp.concatenate([grad_mixer, grad_out], axis=2).astype(bf16)
    grad_pair, grad_down, grad_mixer = (
        a.astype(f32) for a in reduce_all((grad_pair, grad_down, grad_mixer), (4, 4, 4), 1)
    )
    grad_down = grad_down.T
    mixer_width = conv_width + value_width
    grad_out = grad_mixer[:, mixer_width:].T
    d_normed = dot("hste,hde->std", d_projected, w_mixer)
    tokens_grad = d_hidden_in + norm_back(resid, first_scale, attn_gain, d_normed)
    tokens_grad = to_features(tokens_grad.astype(bf16)).astype(f32)
    grad_attn_gain = jnp.sum(d_normed * resid * first_scale, axis=(0, 1))

    small = jnp.concatenate([grad_attn_gain, grad_mlp_gain, grad_out_gain, grad_taps.reshape(-1)])
    small = lax.psum(small.astype(bf16), BOTH).astype(f32)
    width = grad_attn_gain.shape[0]
    own = own_head * own_width
    grad_attn_gain = lax.dynamic_slice_in_dim(small[:width], own, own_width, 0)
    grad_mlp_gain = lax.dynamic_slice_in_dim(small[width : 2 * width], own, own_width, 0)
    grad_out_gain = small[2 * width : 2 * width + value_width]
    grad_taps = small[2 * width + value_width :].reshape(grad_taps.shape)
    grad_taps = lax.dynamic_index_in_dim(grad_taps, own_head, 1, False)
    return (
        layer_out,
        tokens_grad,
        grad_attn_gain,
        grad_mixer[:, :key_width],
        grad_mixer[:, key_width : 2 * key_width],
        grad_mixer[:, 2 * key_width : conv_width],
        grad_mixer[:, conv_width:mixer_width],
        grad_taps[:, :key_width],
        grad_taps[:, key_width : 2 * key_width],
        grad_taps[:, 2 * key_width :],
        grad_out_gain,
        grad_out,
        grad_mlp_gain,
        grad_pair[:, :ff_here],
        grad_pair[:, ff_here:],
        grad_down,
    )

def solution(mesh):
    in_specs = (
        P(None, "seq", "head"),
        P(None, "seq", "head"),
        P(None, "seq", "head"),
        P(),
        P(None, "head"),
        P(None, "head"),
        P(None, "head"),
        P(None, "head"),
        P(None, "head"),
        P(None, "head"),
        P(None, "head"),
        P(),
        P("head", None),
        P(),
        P(None, "head"),
        P(None, "head"),
        P("head", None),
    )
    out_specs = (
        P(None, "seq", "head"),
        P(None, "seq", "head"),
        P("head"),
        P(None, "head"),
        P(None, "head"),
        P(None, "head"),
        P(None, "head"),
        P(None, "head"),
        P(None, "head"),
        P(None, "head"),
        P(),
        P("head", None),
        P("head"),
        P(None, "head"),
        P(None, "head"),
        P("head", None),
    )
    return jax.shard_map(local, mesh=mesh, in_specs=in_specs, out_specs=out_specs, check_vma=False)
```

```python
from functools import partial

import jax
import jax.numpy as jnp
from jax import lax
from jax.experimental import pallas as pl
from jax.experimental.pallas import tpu as pltpu
from jax.sharding import PartitionSpec as P

SPAN = 64
KEY_HEAD = 128
HALO = 16
MESH = pl.DeviceIdType.MESH

epsilon = 1e-06
decay_unit = 2.0 ** (-17)
f32 = jnp.float32
bf16 = jnp.bfloat16

def flipped(place, mask):
    return place + mask - 2 * mask * (place // mask % 2)


def start_body(seq, n_weights, items, *refs):
    tokens, codes, cotangent = refs[:3]
    weights = refs[3 : 3 + n_weights]
    out_tokens, out_codes, out_cotangent = refs[3 + n_weights : 6 + n_weights]
    n_sem = 13
    gathered = refs[6 + n_weights : -n_sem]
    (tsend, trecv, csend, crecv, hsend, hrecv, stay, zsend, zrecv, ysend, yrecv, gsend, grecv) = refs[-n_sem:]
    s, z = lax.axis_index("seq"), lax.axis_index("head")
    heads = 4
    masks = [1, 2, 4]

    def peer(to_s, to_z):
        return {"seq": to_s, "head": to_z}

    barrier = pltpu.get_barrier_semaphore()

    def greet(to_s, to_z):
        pl.semaphore_signal(barrier, 1, device_id=peer(to_s, to_z), device_id_type=MESH)

    for d in range(1, heads):
        greet(s, (z + d) % heads)
    for mask in masks:
        greet(flipped(s, mask), z)

    @pl.when((z == 0) & (s > 0))
    def _():
        for q in range(heads):
            greet(s - 1, q)

    greeted = heads - 1 + len(masks)

    @pl.when(s < seq - 1)
    def _():
        pl.semaphore_wait(barrier, greeted + 1)

    @pl.when(s == seq - 1)
    def _():
        pl.semaphore_wait(barrier, greeted)

    seqs, rows, width = tokens.shape
    mine = rows // heads

    def remote(src, dst, send, recv, to_s, to_z):
        return pltpu.make_async_remote_copy(src, dst, send, recv, device_id=peer(to_s, to_z), device_id_type=MESH)

    def columns(ref, q):
        n = ref.shape[2] // heads
        return pl.ds(pl.multiple_of(q * n, n), n)

    def sends(target, act):
        here = pl.ds(target * mine, mine)
        if target == 0:
            src, dst = tokens.at[:, pl.ds(0, mine)], out_tokens.at[:, pl.ds(HALO, mine), columns(out_tokens, z)]
        else:
            src = tokens.at[:, pl.ds(target * mine - HALO, mine + HALO)]
            dst = out_tokens.at[:, :, columns(out_tokens, z)]
        triples = [
            (src, dst),
            (codes.at[:, here], out_codes.at[:, :, columns(out_codes, z)]),
            (cotangent.at[:, here], out_cotangent.at[:, :, columns(out_cotangent, z)]),
        ]

        @pl.when(z == target)
        def _():
            for i, (a, b) in enumerate(triples):
                copy = pltpu.make_async_copy(a, b, stay.at[i])
                if act == "start":
                    copy.start()
                else:
                    copy.wait()

        @pl.when(z != target)
        def _():
            for i, (a, b) in enumerate(triples):
                copy = remote(a, b, tsend.at[i, target], trecv.at[i, z], s, target)
                if act == "start":
                    copy.start()
                else:
                    copy.wait_send()

    def arrive(source):
        @pl.when(z != source)
        def _():
            here = pl.ds(0, mine)

            @pl.when(z == 0)
            def _():
                dst = out_tokens.at[:, pl.ds(HALO, mine), columns(out_tokens, source)]
                remote(tokens.at[:, here], dst, tsend.at[0, source], trecv.at[0, source], s, source).wait_recv()

            @pl.when(z != 0)
            def _():
                dst = out_tokens.at[:, :, columns(out_tokens, source)]
                remote(
                    tokens.at[:, pl.ds(0, mine + HALO)], dst, tsend.at[0, source], trecv.at[0, source], s, source
                ).wait_recv()

            for i, (a, b) in enumerate(((codes, out_codes), (cotangent, out_cotangent))):
                remote(
                    a.at[:, here], b.at[:, :, columns(b, source)], tsend.at[i + 1, source], trecv.at[i + 1, source],
                    s, source,
                ).wait_recv()

    def halo_copy(source, to_s):
        return remote(
            tokens.at[:, pl.ds(rows - HALO, HALO)], out_tokens.at[:, pl.ds(0, HALO), columns(out_tokens, source)],
            hsend, hrecv.at[source], to_s, 0,
        )

    @pl.when(s < seq - 1)
    def _():
        halo_copy(z, s + 1).start()

    def order(i):
        return [4, 2, 1] if i % 2 == 0 else [2, 4, 1]

    def span(i, j):
        weight, _, axis, first, count, _ = items[i]
        size = count if axis == 0 else weights[weight].shape[1]
        begin = first if axis == 0 else 0
        for k, mask in enumerate(reversed(order(i))):
            if k < len(masks) - j:
                size = size // 2
                begin = begin + (s // mask % 2) * size
        return pl.multiple_of(begin, size), size

    def piece(i, j):
        weight, _, axis, first, count, column = items[i]
        begin, size = span(i, j)
        wide = weights[weight].shape[1]
        if axis == 0:
            own = weights[weight].at[pl.ds(begin, size)]
            place = lambda ref, q: ref.at[q, pl.ds(begin, size), pl.ds(column, wide)]
        else:
            own = weights[weight].at[pl.ds(first, count), pl.ds(begin, size)]
            place = lambda ref, q: ref.at[q, pl.ds(first, count), pl.ds(begin, size)]
        return own, place

    def own_copy(i):
        weight, to, axis, first, count, column = items[i]
        wide = weights[weight].shape[1]
        return pltpu.make_async_copy(
            weights[weight].at[pl.ds(first, count)],
            gathered[to].at[z, pl.ds(first, count), pl.ds(column, wide)], stay.at[3 + i])

    def far_copy(i):
        own, place = piece(i, 0)
        return remote(own, place(gathered[items[i][1]], z), zsend.at[i], zrecv.at[i], s, flipped(z, 2))

    def near_copies(i):
        own, place = piece(i, 0)
        to = gathered[items[i][1]]
        far = flipped(z, 2)
        near = flipped(z, 1)
        return [
            remote(own, place(to, z), ysend.at[i, 0], yrecv.at[i, 0], s, near),
            remote(place(to, far), place(to, far), ysend.at[i, 1], yrecv.at[i, 1], s, near),
        ]

    def seq_copies(i, j):
        _, place = piece(i, j)
        to = gathered[items[i][1]]
        other = flipped(s, order(i)[j])
        return [
            remote(place(to, (z + d) % heads), place(to, (z + d) % heads), gsend.at[i, j, d - 1], grecv.at[i, j, d - 1],
                   other, z)
            for d in range(1, heads)
        ]

    count = len(items)
    for i in range(count):
        far_copy(i).start()
    for target in range(heads):
        sends(target, "start")
    for i in range(count):
        own_copy(i).start()

    def advance(i, k):
        if k == 0:
            far_copy(i).wait_recv()
        elif k == 1:
            for copy in near_copies(i):
                copy.wait_recv()
        else:
            for copy in seq_copies(i, k - 2):
                copy.wait_recv()
        if k == 0:
            for copy in near_copies(i):
                copy.start()
        elif k - 1 < len(masks):
            for copy in seq_copies(i, k - 1):
                copy.start()

    stages = 2 + len(masks)
    pairs = count // 2
    for t in range(pairs + stages - 1):
        for k in reversed(range(stages)):
            p = t - k
            if 0 <= p < pairs:
                advance(2 * p, k)
                advance(2 * p + 1, k)
    for source in range(heads):
        arrive(source)
    for target in range(heads):
        sends(target, "wait")

    @pl.when((z == 0) & (s > 0))
    def _():
        for q in range(heads):
            halo_copy(q, s - 1).wait_recv()

    @pl.when(s < seq - 1)
    def _():
        halo_copy(z, s + 1).wait_send()

    for i in range(count):
        own_copy(i).wait()
        far_copy(i).wait_send()
        for copy in near_copies(i):
            copy.wait_send()
        for j in range(len(masks)):
            for copy in seq_copies(i, j):
                copy.wait_send()


def start_all(tokens, codes, cotangent, weights, items, shapes, collective_id):
    seq, heads = lax.axis_size("seq"), lax.axis_size("head")
    seqs, rows, width = tokens.shape
    mine = rows // heads
    count = len(items)
    dma = pltpu.SemaphoreType.DMA
    anywhere = pl.BlockSpec(memory_space=pl.ANY)
    out_shape = [
        jax.ShapeDtypeStruct((seqs, mine + HALO, heads * width), tokens.dtype),
        jax.ShapeDtypeStruct((seqs, mine, heads * codes.shape[2]), codes.dtype),
        jax.ShapeDtypeStruct((seqs, mine, heads * width), cotangent.dtype),
    ] + [jax.ShapeDtypeStruct((heads, *shape), bf16) for shape in shapes]
    return pl.pallas_call(
        partial(start_body, seq, len(weights), items),
        out_shape=out_shape,
        in_specs=[anywhere] * (3 + len(weights)),
        out_specs=[anywhere] * len(out_shape),
        scratch_shapes=[
            dma((3, heads)), dma((3, heads)), dma((1,)), dma((1,)), dma, dma((heads,)), dma((3 + count,)),
            dma((count,)), dma((count,)), dma((count, 2)), dma((count, 2)), dma((count, 3, 3)), dma((count, 3, 3)),
        ],
        compiler_params=pltpu.CompilerParams(collective_id=collective_id, has_side_effects=True),
        name="start_exchange",
    )(tokens, codes, cotangent, *weights)


def exchange_body(count, heads, per_block, backward, value, logs, out, packed, got, ready, send, recv, bsend, brecv):
    me = lax.axis_index("seq") * heads + lax.axis_index("head")
    part = value.shape[0] // count
    tail = packed.shape[1] - part
    others = count - 1

    def peer(p):
        return {"seq": p // heads, "head": p % heads}

    barrier = pltpu.get_barrier_semaphore()

    def greet(d, carry):
        pl.semaphore_signal(barrier, 1, device_id=peer((me + d) % count), device_id_type=MESH)
        return carry

    lax.fori_loop(1, count, greet, 0)
    high = logs[...].astype(bf16)
    low = (logs[...] - high.astype(f32)).astype(bf16)

    def pack(p, carry):
        packed[p, pl.ds(0, part)] = value[pl.ds(pl.multiple_of(p * part, part), part)]
        return carry

    lax.fori_loop(0, count, pack, 0)
    parts_each = count * per_block // value.shape[0]
    for b in range(logs.shape[0]):
        both = jnp.concatenate([high[b : b + 1], low[b : b + 1], jnp.zeros((tail - 2, high.shape[1]), bf16)], axis=0)
        for i in range(parts_each):
            packed[b * parts_each + i, pl.ds(part, tail)] = both
    got[me] = packed[me]
    pl.semaphore_wait(barrier, others)

    def there(p):
        return pltpu.make_async_remote_copy(
            packed.at[p], got.at[me], send.at[p], recv.at[me], device_id=peer(p), device_id_type=MESH)

    def here(p):
        return pltpu.make_async_remote_copy(
            packed.at[p], got.at[p], send.at[p], recv.at[p], device_id=peer(p), device_id_type=MESH)

    def back(p):
        return pltpu.make_async_remote_copy(
            ready.at[p], out.at[pl.ds(pl.multiple_of(me * part, part), part)], bsend.at[p], brecv.at[me],
            device_id=peer(p), device_id_type=MESH)

    def home(p):
        return pltpu.make_async_remote_copy(
            ready.at[p], out.at[pl.ds(pl.multiple_of(p * part, part), part)], bsend.at[p], brecv.at[p],
            device_id=peer(p), device_id_type=MESH)

    def each(act):
        def one(d, carry):
            act((me + d) % count)
            return carry

        lax.fori_loop(1, count, one, 0)

    each(lambda p: there(p).start())

    def step(i, state):
        p = count - 1 - i if backward else i

        @pl.when(p != me)
        def _():
            here(p).wait_recv()

        ready[p] = state.astype(bf16)

        @pl.when(p != me)
        def _():
            back(p).start()

        decay = jnp.exp(got[p, pl.ds(part, 1)].astype(f32) + got[p, pl.ds(part + 1, 1)].astype(f32))
        return decay * state + got[p, pl.ds(0, part)].astype(f32)

    lax.fori_loop(0, count, step, jnp.zeros((part, value.shape[1]), f32))
    out[pl.ds(pl.multiple_of(me * part, part), part)] = ready[me]
    each(lambda p: home(p).wait_recv())
    each(lambda p: there(p).wait_send())
    each(lambda p: back(p).wait_send())


def exchange(value, logs, backward, collective_id):
    heads = lax.axis_size("head")
    count = lax.axis_size("seq") * heads
    rows, width = value.shape
    part = rows // count
    tail = 16
    dma = pltpu.SemaphoreType.DMA
    return pl.pallas_call(
        partial(exchange_body, count, heads, rows // logs.shape[0], backward),
        out_shape=jax.ShapeDtypeStruct((rows, width), bf16),
        in_specs=[pl.BlockSpec(memory_space=pltpu.VMEM)] * 2,
        out_specs=pl.BlockSpec(memory_space=pltpu.VMEM),
        scratch_shapes=[
            pltpu.VMEM((count, part + tail, width), bf16),
            pltpu.VMEM((count, part + tail, width), bf16),
            pltpu.VMEM((count, part, width), bf16),
            dma((count,)), dma((count,)), dma((count,)), dma((count,)),
        ],
        compiler_params=pltpu.CompilerParams(collective_id=collective_id, has_side_effects=True),
        name="exchange_states",
    )(value, logs)


def aligned(x, size):
    return x if isinstance(x, int) else pl.multiple_of(x, size)


def finish_body(seq, plan, n_arrays, *refs):
    heads = 4
    head_masks = [1, 2]
    nz = len(head_masks)
    seq_masks = [1 << k for k in range(seq.bit_length() - 1)]
    split, joined = seq_masks[:3], seq_masks[3:]
    ns, nj = len(split), len(joined)
    lay_out, tok_grad = refs[:2]
    grads = refs[2 : 2 + n_arrays]
    lay_full, tok_full, halos = refs[2 + n_arrays : 5 + n_arrays]
    outs = refs[5 + n_arrays : 5 + 2 * n_arrays]
    scratch = refs[5 + 2 * n_arrays :]
    s, z = lax.axis_index("seq"), lax.axis_index("head")
    count = len(plan)
    per = ns + nj + nz
    owns = scratch[:count]
    recvs = [scratch[count + i * per : count + (i + 1) * per] for i in range(count)]
    (load_sem, send_sem, recv_sem, jsend, jrecv, zsend, zrecv, gsend, grecv, keep_sem, asend, arecv, stay, hsend,
     hrecv) = scratch[count * (1 + per) :]

    def peer(to_s, to_z):
        return {"seq": to_s, "head": to_z}

    def remote(src, dst, send, recv, to_s, to_z):
        return pltpu.make_async_remote_copy(src, dst, send, recv, device_id=peer(to_s, to_z), device_id_type=MESH)

    barrier = pltpu.get_barrier_semaphore()

    def greet(to_s, to_z):
        pl.semaphore_signal(barrier, 1, device_id=peer(to_s, to_z), device_id_type=MESH)

    for mask in seq_masks:
        greet(flipped(s, mask), z)
    for d in range(1, heads):
        greet(s, (z + d) % heads)

    @pl.when(s < seq - 1)
    def _():
        greet(s + 1, 0)

    greeted = len(seq_masks) + heads - 1

    @pl.when((z == 0) & (s > 0))
    def _():
        pl.semaphore_wait(barrier, greeted + heads)

    @pl.when((z != 0) | (s == 0))
    def _():
        pl.semaphore_wait(barrier, greeted)

    seqs, mine, _ = lay_out.shape
    width = lay_full.shape[2]

    def features(q):
        return pl.ds(aligned(q * width, width), width)

    def rows_to(q):
        return pl.ds(aligned(q * mine, mine), mine)

    def back_copies(q, source):
        return [
            (lay_out.at[:, :, features(q)], lay_full.at[:, rows_to(source)]),
            (tok_grad.at[:, pl.ds(HALO, mine), features(q)], tok_full.at[:, rows_to(source)]),
        ]

    def back_send(d):
        q = (z + d) % heads
        return [remote(a, b, asend.at[i, q], arecv.at[i, z], s, q) for i, (a, b) in enumerate(back_copies(q, z))]

    def back_wait(d):
        q = (z + d) % heads
        return [remote(a, b, asend.at[i, q], arecv.at[i, q], s, q) for i, (a, b) in enumerate(back_copies(z, q))]

    def stay_copies():
        return [pltpu.make_async_copy(a, b, stay.at[i]) for i, (a, b) in enumerate(back_copies(z, z))]

    def halo_send(d):
        q = (z + d) % heads
        return remote(tok_grad.at[:, pl.ds(0, HALO), features(q)], halos.at[z], hsend.at[q], hrecv.at[z], s, q)

    def halo_wait(d):
        q = (z + d) % heads
        return remote(tok_grad.at[:, pl.ds(0, HALO), features(z)], halos.at[q], hsend.at[q], hrecv.at[q], s, q)

    def halo_own():
        return pltpu.make_async_copy(tok_grad.at[:, pl.ds(0, HALO), features(z)], halos.at[z], stay.at[2])

    def halo_cross(q):
        return remote(tok_grad.at[:, pl.ds(0, HALO), features(q)], halos.at[0], hsend.at[q], hrecv.at[0], s - 1, q)

    def halo_from_next():
        return remote(tok_grad.at[:, pl.ds(0, HALO), features(z)], halos.at[0], hsend.at[0], hrecv.at[0], s + 1, 0)

    def to_features(first):
        for copy in stay_copies():
            copy.start() if first else copy.wait()
        for d in range(1, heads):
            for copy in back_send(d):
                copy.start() if first else copy.wait_send()
            if not first:
                for copy in back_wait(d):
                    copy.wait_recv()

        @pl.when(z != 0)
        def _():
            halo_own().start() if first else halo_own().wait()
            for d in range(1, heads):
                halo_send(d).start() if first else halo_send(d).wait_send()

        @pl.when((z == 0) & (s > 0))
        def _():
            for q in range(heads):
                halo_cross(q).start() if first else halo_cross(q).wait_send()

        if not first:
            for d in range(1, heads):

                @pl.when((z + d) % heads != 0)
                def _():
                    halo_wait(d).wait_recv()

            @pl.when(s < seq - 1)
            def _():
                halo_from_next().wait_recv()

    def masks(c):
        return split[:1] + (split[1:] if c % 2 == 0 else split[:0:-1])

    def bit(c, k):
        return s // masks(c)[k] % 2

    def extent(c):
        array, axis, first, size = plan[c]
        return size if axis == 0 else grads[array].shape[2]

    def kept(c, k):
        size = extent(c)
        return sum((bit(c, j) * (size >> (j + 1)) for j in range(1, k + 1)), 0)

    def cut(c, begin, size):
        _, axis, _, rows = plan[c]
        part = pl.ds(aligned(begin, size), size)
        return (part, slice(None)) if axis == 0 else (slice(None), part)

    def in_array(c, begin, size):
        _, axis, first, rows = plan[c]
        if axis == 0:
            return pl.ds(aligned(first + begin, size), size), slice(None)
        return pl.ds(first, rows), pl.ds(aligned(begin, size), size)

    def load(c):
        half = extent(c) // 2
        rows, columns = in_array(c, bit(c, 0) * half, half)
        return pltpu.make_async_copy(grads[plan[c][0]].at[:, rows, columns], owns[c], load_sem.at[c])

    def seq_copy(c, k):
        half = extent(c) >> (k + 1)
        other = (1 - bit(c, k)) * half
        if k == 0:
            rows, columns = in_array(c, other, half)
            source = grads[plan[c][0]].at[:, rows, columns]
        else:
            rows, columns = cut(c, kept(c, k - 1) + other, half)
            source = owns[c].at[:, rows, columns]
        return remote(source, recvs[c][k], send_sem.at[c, k], recv_sem.at[c, k], flipped(s, masks(c)[k]), z)

    def final(c):
        size = extent(c) >> ns
        return cut(c, kept(c, ns - 1), size)

    def joined_copy(c, k):
        rows, columns = final(c)
        return remote(
            owns[c].at[:, rows, columns], recvs[c][ns + k], jsend.at[c, k], jrecv.at[c, k], flipped(s, joined[k]), z)

    def head_copies(c, k):
        rows, columns = final(c)
        mask = head_masks[k]
        low, b = z % mask, z // mask % 2
        return [
            remote(
                owns[c].at[low + (1 - b) * mask + i * 2 * mask, rows, columns], recvs[c][ns + nj + k].at[i],
                zsend.at[c, k, i], zrecv.at[c, k, i], s, flipped(z, mask))
            for i in range(heads // (2 * mask))
        ]

    def add(c, k):
        _, axis, _, rows = plan[c]
        if k < ns:
            begin, size = kept(c, k), extent(c) >> (k + 1)
        else:
            begin, size = kept(c, ns - 1), extent(c) >> ns
        if k < ns + nj:
            many, place = heads, lambda i: i
        else:
            mask = head_masks[k - ns - nj]
            many = heads // (2 * mask)
            place = lambda i: z % mask + z // mask % 2 * mask + i * 2 * mask
        n_rows = size if axis == 0 else rows
        tile = min(16, n_rows)
        tiles = n_rows // tile
        received = recvs[c][k]

        def one(t, carry):
            i, r = t // tiles, t % tiles * tile
            there = pl.ds(pl.multiple_of(r, tile), tile)
            if axis == 0:
                here, columns = pl.ds(pl.multiple_of(begin + r, tile), tile), slice(None)
            else:
                here, columns = there, pl.ds(aligned(begin, size), size)
            q = place(i)
            total = owns[c][q, here, columns].astype(f32) + received[i, there].astype(f32)
            owns[c][q, here, columns] = total.astype(bf16)
            return carry

        lax.fori_loop(0, many * tiles, one, 0)

    def held(c, level):
        size = extent(c)
        return in_array(c, sum(bit(c, j) * (size >> (j + 1)) for j in range(level)), size >> level)

    def keep(c):
        rows, columns = final(c)
        to_rows, to_columns = held(c, ns)
        return pltpu.make_async_copy(
            owns[c].at[z, rows, columns], outs[plan[c][0]].at[to_rows, to_columns], keep_sem.at[c])

    def gather_copy(c, j):
        level = ns - j
        rows, columns = held(c, level)
        array = outs[plan[c][0]].at[rows, columns]
        return remote(array, array, gsend.at[c, j], grecv.at[c, j], flipped(s, masks(c)[level - 1]), z)

    for c in range(count):
        seq_copy(c, 0).start()
        load(c).start()
    to_features(True)
    last = per + 1 + ns

    def copies(c, k):
        if k < ns:
            return [seq_copy(c, k)]
        if k < ns + nj:
            return [joined_copy(c, k - ns)]
        if k < per:
            return head_copies(c, k - ns - nj)
        return [gather_copy(c, k - per - 1)]

    def advance(c, k):
        if k == 0:
            load(c).wait()
        if k == per:
            keep(c).wait()
        else:
            for copy in copies(c, k):
                copy.wait_recv()
        if k < per:
            if ns < k + 1 <= ns + nj:
                joined_copy_done(c, k)
            add(c, k)
        n = k + 1
        if n == per:
            keep(c).start()
        elif n < last:
            for copy in copies(c, n):
                copy.start()

    def joined_copy_done(c, k):
        joined_copy(c, k - ns).wait_send()

    pairs = count // 2
    for t in range(pairs + last - 1):
        for k in reversed(range(last)):
            p = t - k
            if 0 <= p < pairs:
                advance(2 * p, k)
                advance(2 * p + 1, k)
    to_features(False)
    for c in range(count):
        for k in range(last):
            if k != per and not ns <= k < ns + nj:
                for copy in copies(c, k):
                    copy.wait_send()


def finish_all(lay_out, tok_grad, arrays, plan, collective_id):
    seq, heads = lax.axis_size("seq"), lax.axis_size("head")
    nj = max(0, seq.bit_length() - 4)
    ns, nz = 3, 2
    seqs, mine, features = lay_out.shape
    width = features // heads
    owns, recvs = [], []
    for a, axis, first, rows in plan:
        columns = arrays[a].shape[2]
        cut = lambda k: (rows >> k, columns) if axis == 0 else (rows, columns >> k)
        owns.append(pltpu.VMEM((heads, *cut(1)), bf16))
        recvs += [pltpu.VMEM((heads, *cut(k + 1)), bf16) for k in range(ns)]
        recvs += [pltpu.VMEM((heads, *cut(ns)), bf16) for k in range(nj)]
        recvs += [pltpu.VMEM((heads >> (k + 1), *cut(ns)), bf16) for k in range(nz)]
    count = len(plan)
    dma = pltpu.SemaphoreType.DMA
    sems = [
        dma((count,)), dma((count, ns)), dma((count, ns)), dma((count, max(nj, 1))), dma((count, max(nj, 1))),
        dma((count, nz, heads // 2)), dma((count, nz, heads // 2)), dma((count, ns)), dma((count, ns)), dma((count,)),
        dma((2, heads)), dma((2, heads)), dma((3,)), dma((heads,)), dma((heads,)),
    ]
    anywhere = pl.BlockSpec(memory_space=pl.ANY)
    out_shape = [jax.ShapeDtypeStruct((seqs, heads * mine, width), bf16)] * 2
    out_shape += [jax.ShapeDtypeStruct((heads, seqs, HALO, width), bf16)]
    out_shape += [jax.ShapeDtypeStruct(a.shape[1:], bf16) for a in arrays]
    return pl.pallas_call(
        partial(finish_body, seq, plan, len(arrays)),
        out_shape=out_shape,
        in_specs=[anywhere] * (2 + len(arrays)),
        out_specs=[anywhere] * len(out_shape),
        scratch_shapes=owns + recvs + sems,
        compiler_params=pltpu.CompilerParams(
            collective_id=collective_id, has_side_effects=True, vmem_limit_bytes=60 * 2**20),
        name="finish_sums",
    )(lay_out, tok_grad, *arrays)


def row_scale(values):
    return lax.rsqrt(jnp.mean(values * values, axis=-1, keepdims=True) + epsilon)


def silu_slope(values):
    logistic = jax.nn.sigmoid(values)
    return logistic * (1.0 + values * (1.0 - logistic))


def norm_back(values, inverse, weights, upstream):
    weighted = weights * upstream
    return inverse * weighted - values * inverse**3 * jnp.mean(
        weighted * values, axis=-1, keepdims=True
    )


def rounded(values):
    return values.astype(bf16).astype(f32)


def dot(spec, left, right):
    return jnp.einsum(spec, left.astype(bf16), right.astype(bf16), preferred_element_type=f32)


def cumulated(spec, values, count):
    at = jnp.arange(count)
    lower = (at[:, None] >= at[None, :]).astype(f32)
    return jnp.einsum(spec, lower, values, precision=lax.Precision.HIGHEST, preferred_element_type=f32)


def whole(weights):
    seq = lax.axis_size("seq")
    parts = []
    for w in weights:
        part = w.shape[0] // seq
        parts.append(lax.dynamic_slice_in_dim(w, lax.axis_index("seq") * part, part, 0))
    mine = jnp.concatenate(parts, axis=0)
    every = lax.all_gather(mine, ("head", "seq"), axis=0, tiled=True)
    every = every.reshape(lax.axis_size("head"), seq, *mine.shape)
    out, at = [], 0
    for w, p in zip(weights, parts):
        out.append(every[:, :, at : at + p.shape[0]].reshape(-1, *w.shape))
        at += p.shape[0]
    return out


def chunks(array, rows, count):
    return [(array, 0, i * (rows // count), rows // count) for i in range(count)]


def local(
    tokens,
    decay_codes,
    cotangent,
    attn_gain,
    w_query,
    w_key,
    w_value,
    w_out_gate,
    conv_query,
    conv_key,
    conv_value,
    out_gain,
    w_out,
    mlp_gain,
    w_gate,
    w_up,
    w_down,
):
    seqs, rows, own_width = tokens.shape
    heads = lax.axis_size("head")
    place = lax.axis_index("seq") * heads + lax.axis_index("head")
    mine = rows // heads
    width = own_width * heads
    key_width = w_query.shape[1]
    value_width = w_value.shape[1]
    conv_width = 2 * key_width + value_width
    mixer_width = conv_width + value_width

    half = width // 2
    items = [
        (0, 0, 0, 0, width, 0),
        (1, 0, 0, 0, width, key_width),
        (2, 0, 0, 0, half, 2 * key_width),
        (2, 0, 0, half, half, 2 * key_width),
        (3, 0, 0, 0, half, conv_width),
        (3, 0, 0, half, half, conv_width),
        (4, 1, 0, 0, w_out.shape[0] // 2, 0),
        (4, 1, 0, w_out.shape[0] // 2, w_out.shape[0] // 2, 0),
    ]
    tokens_ext, codes, upstream, w_mixer, w_proj = start_all(
        tokens,
        decay_codes.astype(jnp.int16),
        cotangent,
        (w_query, w_key, w_value, w_out_gate, w_out),
        items,
        ((width, mixer_width), w_out.shape),
        1,
    )
    (w_gate_all,) = whole((w_gate,))
    (w_up_all,) = whole((w_up,))
    (w_low,) = whole((w_down,))
    taps = lax.all_gather(jnp.concatenate([conv_query, conv_key, conv_value], axis=1), "head")

    first_rows = (jnp.arange(mine + HALO) < HALO) & (place == 0)
    resid_ext = jnp.where(first_rows[None, :, None], 0, tokens_ext).astype(f32)
    first_scale = row_scale(resid_ext)
    normed = (resid_ext * first_scale * attn_gain).astype(bf16)
    projected = dot("std,hde->hste", normed, w_mixer).astype(bf16)
    gate_rows = projected[:, :, HALO:, conv_width:].astype(f32)
    extended = projected[..., :conv_width].astype(f32)
    tap_count = taps.shape[1]
    lead = HALO - tap_count + 1
    conv_sum = sum(
        taps[:, j, None, None, :] * extended[:, :, lead + j : lead + j + mine] for j in range(tap_count)
    )
    activated = jax.nn.silu(conv_sum)
    blocks = mine // SPAN

    def spanned(values):
        return values.reshape(heads, seqs, blocks, SPAN, values.shape[-1])

    query = spanned(activated[..., :key_width])
    keyed = spanned(activated[..., key_width : 2 * key_width])
    valued = spanned(activated[..., 2 * key_width :])
    log_decay = -codes.astype(f32) * decay_unit
    log_decay = jnp.moveaxis(log_decay.reshape(seqs, blocks, SPAN, heads, key_width), 3, 0)
    cumul = cumulated("tu,hanuk->hantk", log_decay, SPAN)
    span_log = cumul[:, :, :, -1]
    running = cumulated("mn,hank->hamk", span_log, blocks)
    carry_decay = jnp.exp(running - span_log)
    log_total = running[:, :, -1].reshape(-1, key_width)
    positions = jnp.arange(SPAN)
    causal = positions[:, None] >= positions[None, :]
    grow = jnp.exp(cumul)
    shrink = jnp.exp(-cumul)
    to_end = jnp.exp(span_log[:, :, :, None] - cumul)
    scale = key_width ** (-0.5)
    query_exp = query * scale * grow
    keyed_exp = keyed * shrink
    keyed_end = keyed * to_end
    update = dot("hantk,hantv->hanvk", keyed_end, valued)
    span_decay = jnp.exp(span_log)
    starts = [jnp.zeros_like(update[:, :, 0])]
    for n in range(blocks):
        starts.append(span_decay[:, :, n, None, :] * starts[n] + update[:, :, n])
    local_end = starts.pop()
    flat = (-1, key_width)
    incoming = exchange(local_end.astype(bf16).reshape(flat), log_total, False, 2)
    incoming = incoming.reshape(local_end.shape).astype(f32)
    scores = jnp.where(causal, dot("hantk,hanuk->hantu", query_exp, keyed_exp), 0.0)
    inner = dot("hantu,hanuv->hantv", scores, valued)
    states = jnp.stack(starts, 2) + carry_decay[:, :, :, None, :] * incoming[:, :, None]
    core_rows = (inner + dot("hantk,hanvk->hantv", query_exp, states)).reshape(heads, seqs, mine, value_width)
    out_scale = row_scale(core_rows)
    normed_out = core_rows * out_scale * out_gain
    gate_silu = jax.nn.silu(gate_rows)
    gated = (normed_out * gate_silu).astype(bf16)
    resid = resid_ext[:, HALO:]
    hidden_in = resid + jnp.sum(rounded(dot("hste,hed->hstd", gated, w_proj)), axis=0)
    second_scale = row_scale(hidden_in)
    normed_two = (hidden_in * second_scale * mlp_gain).astype(bf16)
    gate_val = dot("std,hdf->hstf", normed_two, w_gate_all)
    up_val = dot("std,hdf->hstf", normed_two, w_up_all)
    gate_act = jax.nn.silu(gate_val)
    hidden = (gate_act * up_val).astype(bf16)
    layer_out = hidden_in + jnp.sum(rounded(dot("hstf,hfd->hstd", hidden, w_low)), axis=0)

    d_hidden = rounded(dot("std,hfd->hstf", upstream, w_low))
    grad_down = dot("hstf,std->hfd", hidden, upstream)
    d_gate = (d_hidden * up_val * silu_slope(gate_val)).astype(bf16)
    d_up = (d_hidden * gate_act).astype(bf16)
    grad_gate = dot("std,hstf->hdf", normed_two, d_gate)
    grad_up = dot("std,hstf->hdf", normed_two, d_up)
    d_normed_two = dot("hstf,hdf->std", d_gate, w_gate_all) + dot("hstf,hdf->std", d_up, w_up_all)
    d_hidden_in = upstream.astype(f32) + norm_back(hidden_in, second_scale, mlp_gain, d_normed_two)
    grad_mlp_gain = jnp.sum(d_normed_two * hidden_in * second_scale, axis=(0, 1))
    d_mixer = d_hidden_in.astype(bf16)
    grad_out = dot("hste,std->hed", gated, d_mixer)
    d_gated = rounded(dot("std,hed->hste", d_mixer, w_proj))
    d_normed_out = d_gated * gate_silu
    d_gate_rows = d_gated * normed_out * silu_slope(gate_rows)
    grad_out_gain = jnp.sum(d_normed_out * core_rows * out_scale, axis=(0, 1, 2))
    d_core = spanned(norm_back(core_rows, out_scale, out_gain, d_normed_out))

    d_states = dot("hantk,hantv->hanvk", query_exp, d_core)
    own_grad = jnp.sum(carry_decay[:, :, :, None, :] * d_states, axis=2)
    leaving = exchange(own_grad.astype(bf16).reshape(flat), log_total, True, 3)
    d_ends = [leaving.reshape(own_grad.shape).astype(f32)]
    for n in range(blocks - 1, 0, -1):
        d_ends.append(span_decay[:, :, n, None, :] * d_ends[-1] + d_states[:, :, n])
    d_ends = jnp.stack(d_ends[::-1], 2)
    d_scores = jnp.where(causal, dot("hantv,hanuv->hantu", d_core, valued), 0.0)
    d_query = dot("hantu,hanuk->hantk", d_scores, keyed_exp) + dot("hantv,hanvk->hantk", d_core, states)
    d_query = d_query * scale * grow
    d_keyed = dot("hantu,hantk->hanuk", d_scores, query_exp) * shrink
    d_keyed = d_keyed + dot("hanuv,hanvk->hanuk", valued, d_ends) * to_end
    d_valued = dot("hantu,hantv->hanuv", scores, d_core) + dot("hanuk,hanvk->hanuv", keyed_end, d_ends)
    d_activated = jnp.concatenate(
        [a.reshape(heads, seqs, mine, -1) for a in (d_query, d_keyed, d_valued)], axis=-1
    )
    d_conv = d_activated * silu_slope(conv_sum)
    tap_grads = []
    d_extended = jnp.zeros(extended.shape, f32)
    for j in range(tap_count):
        tap_grads.append(jnp.sum(d_conv * extended[:, :, lead + j : lead + j + mine], axis=(1, 2)))
        d_extended = d_extended + jnp.pad(
            taps[:, j, None, None, :] * d_conv, ((0, 0), (0, 0), (lead + j, tap_count - 1 - j), (0, 0))
        )
    grad_taps = jnp.stack(tap_grads, 1)
    d_gate_ext = jnp.pad(d_gate_rows, ((0, 0), (0, 0), (HALO, 0), (0, 0)))
    d_projected = jnp.concatenate([d_extended, d_gate_ext], axis=-1).astype(bf16)
    grad_mixer = dot("std,hste->hde", normed, d_projected)
    d_normed = dot("hste,hde->std", d_projected, w_mixer)
    grad_attn_gain = jnp.sum(d_normed * resid_ext * first_scale, axis=(0, 1))
    tokens_grad = norm_back(resid_ext, first_scale, attn_gain, d_normed)
    tokens_grad = tokens_grad + jnp.pad(d_hidden_in, ((0, 0), (HALO, 0), (0, 0)))

    small = jnp.concatenate(
        [
            grad_attn_gain.reshape(heads, -1),
            grad_mlp_gain.reshape(heads, -1),
            jnp.broadcast_to(grad_out_gain, (heads, value_width)),
            grad_taps.reshape(heads, -1),
        ],
        axis=1,
    )
    small_rows = 256
    lanes = -(-small.shape[1] // (small_rows * 128)) * 128
    small = jnp.pad(small, ((0, 0), (0, small_rows * lanes - small.shape[1]))).reshape(heads, small_rows, lanes)
    arrays = [a.astype(bf16) for a in (grad_gate, grad_up, grad_down, grad_out, grad_mixer, small)]
    ff = w_gate.shape[1]
    plan = (
        chunks(0, width, 4)
        + chunks(1, width, 4)
        + [(2, 1, 0, ff // 2), (2, 1, ff // 2, ff // 2)]
        + chunks(3, w_out.shape[0], 2)
        + chunks(4, width, 4)
        + chunks(5, small_rows, 2)
    )
    layer_out, tokens_grad, halos, *sums = finish_all(
        layer_out.astype(bf16), tokens_grad.astype(bf16), arrays, plan, 4
    )
    grad_gate, grad_up, grad_down, grad_out, grad_mixer, small = (a.astype(f32) for a in sums)
    layer_out = layer_out.astype(f32)
    last = lax.axis_index("seq") == lax.axis_size("seq") - 1
    halos = jnp.where(last & (jnp.arange(heads) == 0)[:, None, None, None], 0, halos).astype(f32)
    halos = jnp.moveaxis(jnp.roll(halos, -1, axis=0), 0, 1)
    halos = jnp.pad(halos, ((0, 0), (0, 0), (mine - HALO, 0), (0, 0))).reshape(tokens_grad.shape)
    tokens_grad = tokens_grad.astype(f32) + halos
    small = small.reshape(-1)
    at = 2 * own_width + value_width
    grad_taps = small[at : at + tap_count * conv_width].reshape(tap_count, conv_width)
    return (
        layer_out,
        tokens_grad,
        small[:own_width],
        grad_mixer[:, :key_width],
        grad_mixer[:, key_width : 2 * key_width],
        grad_mixer[:, 2 * key_width : conv_width],
        grad_mixer[:, conv_width:],
        grad_taps[:, :key_width],
        grad_taps[:, key_width : 2 * key_width],
        grad_taps[:, 2 * key_width :],
        small[2 * own_width : at],
        grad_out,
        small[own_width : 2 * own_width],
        grad_gate,
        grad_up,
        grad_down,
    )


def solution(mesh):
    in_specs = (
        P(None, "seq", "head"),
        P(None, "seq", "head"),
        P(None, "seq", "head"),
        P(),
        P(None, "head"),
        P(None, "head"),
        P(None, "head"),
        P(None, "head"),
        P(None, "head"),
        P(None, "head"),
        P(None, "head"),
        P(),
        P("head", None),
        P(),
        P(None, "head"),
        P(None, "head"),
        P("head", None),
    )
    out_specs = (
        P(None, "seq", "head"),
        P(None, "seq", "head"),
        P("head"),
        P(None, "head"),
        P(None, "head"),
        P(None, "head"),
        P(None, "head"),
        P(None, "head"),
        P(None, "head"),
        P(None, "head"),
        P(),
        P("head", None),
        P("head"),
        P(None, "head"),
        P(None, "head"),
        P("head", None),
    )
    return jax.shard_map(local, mesh=mesh, in_specs=in_specs, out_specs=out_specs, check_vma=False)
```

```python
from functools import partial

import jax
import jax.numpy as jnp
from jax import lax
from jax.experimental import pallas as pl
from jax.experimental.pallas import tpu as pltpu
from jax.sharding import PartitionSpec as P

SPAN = 64
KEY_HEAD = 128
HALO = 16
MESH = pl.DeviceIdType.MESH

epsilon = 1e-06
decay_unit = 2.0 ** (-17)
f32 = jnp.float32
bf16 = jnp.bfloat16

def flipped(place, mask):
    return place + mask - 2 * mask * (place // mask % 2)


def over_seq(items, gathered, gsend, grecv, s, z):
    heads = 4

    def order(i):
        return [4, 2, 1] if items[i][0] % 2 == 0 else [2, 4, 1]

    def span(i, j):
        _, _, to, axis, first, count, _, _ = items[i]
        size = count if axis == 0 else gathered[to].shape[2]
        begin = first if axis == 0 else 0
        for mask in order(i)[: j - 4 : -1] if j < 3 else []:
            size = size // 2
            begin = begin + (s // mask % 2) * size
        return pl.multiple_of(begin, size), size

    def seq_copies(i, j):
        _, _, to, axis, first, count, column, _ = items[i]
        begin, size = span(i, j)
        copies = []
        for d in range(1, heads):
            q = (z + d) % heads
            if axis == 0:
                place = gathered[to].at[q, pl.ds(begin, size), pl.ds(column, items[i][7])]
            else:
                place = gathered[to].at[q, pl.ds(first, count), pl.ds(begin, size)]
            copies.append(pltpu.make_async_remote_copy(
                place, place, gsend.at[i, j, d - 1], grecv.at[i, j, d - 1],
                device_id={"seq": flipped(s, order(i)[j]), "head": z}, device_id_type=MESH))
        return copies

    return span, seq_copies


def start_body(seq, n_weights, items, steps, *refs):
    tokens, codes, taps = refs[:3]
    weights = refs[3 : 3 + n_weights]
    out_tokens, out_codes, out_taps = refs[3 + n_weights : 6 + n_weights]
    n_sem = 11
    n_items = len(items)
    gathered = refs[6 + n_weights : -n_sem - n_items]
    held = refs[-n_sem - n_items : -n_sem]
    (tsend, trecv, hsend, hrecv, stay, zsend, zrecv, ysend, yrecv, gsend, grecv) = refs[-n_sem:]
    s, z = lax.axis_index("seq"), lax.axis_index("head")
    heads = 4
    masks = [1, 2, 4]

    def peer(to_s, to_z):
        return {"seq": to_s, "head": to_z}

    barrier = pltpu.get_barrier_semaphore()

    def greet(to_s, to_z):
        pl.semaphore_signal(barrier, 1, device_id=peer(to_s, to_z), device_id_type=MESH)

    for d in range(1, heads):
        greet(s, (z + d) % heads)
    for mask in masks:
        greet(flipped(s, mask), z)

    @pl.when((z == 0) & (s > 0))
    def _():
        for q in range(heads):
            greet(s - 1, q)

    greeted = heads - 1 + len(masks)

    @pl.when(s < seq - 1)
    def _():
        pl.semaphore_wait(barrier, greeted + 1)

    @pl.when(s == seq - 1)
    def _():
        pl.semaphore_wait(barrier, greeted)

    seqs, rows, width = tokens.shape
    mine = rows // heads

    def remote(src, dst, send, recv, to_s, to_z):
        return pltpu.make_async_remote_copy(src, dst, send, recv, device_id=peer(to_s, to_z), device_id_type=MESH)

    def columns(ref, q):
        n = ref.shape[2] // heads
        return pl.ds(pl.multiple_of(q * n, n), n)

    def sends(target, act):
        here = pl.ds(target * mine, mine)
        if target == 0:
            src, dst = tokens.at[:, pl.ds(0, mine)], out_tokens.at[:, pl.ds(HALO, mine), columns(out_tokens, z)]
        else:
            src = tokens.at[:, pl.ds(target * mine - HALO, mine + HALO)]
            dst = out_tokens.at[:, :, columns(out_tokens, z)]
        triples = [
            (src, dst),
            (codes.at[:, here], out_codes.at[:, :, columns(out_codes, z)]),
            (taps, out_taps.at[z]),
        ]

        @pl.when(z == target)
        def _():
            for i, (a, b) in enumerate(triples):
                copy = pltpu.make_async_copy(a, b, stay.at[i])
                if act == "start":
                    copy.start()
                else:
                    copy.wait()

        @pl.when(z != target)
        def _():
            for i, (a, b) in enumerate(triples):
                copy = remote(a, b, tsend.at[i, target], trecv.at[i, z], s, target)
                if act == "start":
                    copy.start()
                else:
                    copy.wait_send()

    def arrive(source):
        @pl.when(z != source)
        def _():
            here = pl.ds(0, mine)

            @pl.when(z == 0)
            def _():
                dst = out_tokens.at[:, pl.ds(HALO, mine), columns(out_tokens, source)]
                remote(tokens.at[:, here], dst, tsend.at[0, source], trecv.at[0, source], s, source).wait_recv()

            @pl.when(z != 0)
            def _():
                dst = out_tokens.at[:, :, columns(out_tokens, source)]
                remote(
                    tokens.at[:, pl.ds(0, mine + HALO)], dst, tsend.at[0, source], trecv.at[0, source], s, source
                ).wait_recv()

            for i, (a, b) in enumerate(
                ((codes.at[:, here], out_codes.at[:, :, columns(out_codes, source)]), (taps, out_taps.at[source]))
            ):
                remote(a, b, tsend.at[i + 1, source], trecv.at[i + 1, source], s, source).wait_recv()

    def halo_copy(source, to_s):
        return remote(
            tokens.at[:, pl.ds(rows - HALO, HALO)], out_tokens.at[:, pl.ds(0, HALO), columns(out_tokens, source)],
            hsend, hrecv.at[source], to_s, 0,
        )

    @pl.when(s < seq - 1)
    def _():
        halo_copy(z, s + 1).start()

    span, seq_copies = over_seq(items, gathered, gsend, grecv, s, z)

    def piece(i, j):
        _, weight, _, axis, first, count, column, _ = items[i]
        begin, size = span(i, j)
        wide = weights[weight].shape[1]
        if axis == 0:
            own = weights[weight].at[pl.ds(begin, size)]
            place = lambda ref, q: ref.at[q, pl.ds(begin, size), pl.ds(column, wide)]
        else:
            own = weights[weight].at[pl.ds(first, count), pl.ds(begin, size)]
            place = lambda ref, q: ref.at[q, pl.ds(first, count), pl.ds(begin, size)]
        return own, place

    def own_load(i):
        _, weight, _, _, first, count, _, _ = items[i]
        return pltpu.make_async_copy(weights[weight].at[pl.ds(first, count)], held[i], stay.at[3 + i])

    def own_store(i):
        _, weight, to, _, first, count, column, _ = items[i]
        wide = weights[weight].shape[1]
        return pltpu.make_async_copy(
            held[i], gathered[to].at[z, pl.ds(first, count), pl.ds(column, wide)], stay.at[3 + i])

    def far_copy(i):
        own, place = piece(i, 0)
        return remote(own, place(gathered[items[i][2]], z), zsend.at[i], zrecv.at[i], s, flipped(z, 2))

    def near_copies(i):
        own, place = piece(i, 0)
        to = gathered[items[i][2]]
        far = flipped(z, 2)
        near = flipped(z, 1)
        return [
            remote(own, place(to, z), ysend.at[i, 0], yrecv.at[i, 0], s, near),
            remote(place(to, far), place(to, far), ysend.at[i, 1], yrecv.at[i, 1], s, near),
        ]

    count = len(items)

    def stage(i, k):
        if k == 0:
            return [far_copy(i)]
        return near_copies(i) if k == 1 else seq_copies(i, k - 2)

    stages = 2 + len(masks)
    pairs = (max(item[0] for item in items) + 2) // 2
    for t in range(pairs + stages):
        for k in reversed(range(stages + 1)):
            for i in range(count):
                if items[i][0] // 2 != t - k or k > 2 + steps[i]:
                    continue
                if k > 0:
                    for copy in stage(i, k - 1):
                        copy.wait_recv()
                if k < 2 + steps[i]:
                    for copy in stage(i, k):
                        copy.start()
        if t == 0:
            for target in range(heads):
                sends(target, "start")
            for i in range(count):
                own_load(i).start()
    for i in range(count):
        own_load(i).wait()
        own_store(i).start()
    for source in range(heads):
        arrive(source)
    for target in range(heads):
        sends(target, "wait")

    @pl.when((z == 0) & (s > 0))
    def _():
        for q in range(heads):
            halo_copy(q, s - 1).wait_recv()

    @pl.when(s < seq - 1)
    def _():
        halo_copy(z, s + 1).wait_send()

    for i in range(count):
        own_store(i).wait()
        far_copy(i).wait_send()
        for copy in near_copies(i):
            copy.wait_send()
        for j in range(steps[i]):
            for copy in seq_copies(i, j):
                copy.wait_send()


def start_all(tokens, codes, taps, weights, items, steps, shapes, collective_id):
    seq, heads = lax.axis_size("seq"), lax.axis_size("head")
    seqs, rows, width = tokens.shape
    mine = rows // heads
    count = len(items)
    dma = pltpu.SemaphoreType.DMA
    anywhere = pl.BlockSpec(memory_space=pl.ANY)
    out_shape = [
        jax.ShapeDtypeStruct((seqs, mine + HALO, heads * width), tokens.dtype),
        jax.ShapeDtypeStruct((seqs, mine, heads * codes.shape[2]), codes.dtype),
        jax.ShapeDtypeStruct((heads, *taps.shape), taps.dtype),
    ] + [jax.ShapeDtypeStruct((heads, *shape), bf16) for shape in shapes]
    return pl.pallas_call(
        partial(start_body, seq, len(weights), items, steps),
        out_shape=out_shape,
        in_specs=[anywhere] * (3 + len(weights)),
        out_specs=[anywhere] * len(out_shape),
        scratch_shapes=[pltpu.VMEM((item[5], weights[item[1]].shape[1]), bf16) for item in items]
        + [
            dma((3, heads)), dma((3, heads)), dma, dma((heads,)), dma((3 + count,)),
            dma((count,)), dma((count,)), dma((count, 2)), dma((count, 2)), dma((count, 3, 3)), dma((count, 3, 3)),
        ],
        compiler_params=pltpu.CompilerParams(
            collective_id=collective_id, has_side_effects=True, vmem_limit_bytes=24 * 2**20),
        name="start_exchange",
    )(tokens, codes, taps, *weights)


def exchange_body(count, heads, per_block, backward, items, n_more, *refs):
    value, logs = refs[:2]
    out = refs[2 + n_more]
    gathered = refs[3 + n_more : 3 + 2 * n_more]
    packed, got, ready, send, recv, bsend, brecv, gsend, grecv = refs[3 + 2 * n_more :]
    _, seq_copies = over_seq(items, gathered, gsend, grecv, lax.axis_index("seq"), lax.axis_index("head"))
    me = lax.axis_index("seq") * heads + lax.axis_index("head")
    part = value.shape[0] // count
    tail = packed.shape[1] - part
    others = count - 1

    def peer(p):
        return {"seq": p // heads, "head": p % heads}

    barrier = pltpu.get_barrier_semaphore()

    def greet(d, carry):
        pl.semaphore_signal(barrier, 1, device_id=peer((me + d) % count), device_id_type=MESH)
        return carry

    lax.fori_loop(1, count, greet, 0)
    high = logs[...].astype(bf16)
    low = (logs[...] - high.astype(f32)).astype(bf16)

    def pack(p, carry):
        packed[p, pl.ds(0, part)] = value[pl.ds(pl.multiple_of(p * part, part), part)]
        return carry

    lax.fori_loop(0, count, pack, 0)
    parts_each = count * per_block // value.shape[0]
    for b in range(logs.shape[0]):
        both = jnp.concatenate([high[b : b + 1], low[b : b + 1], jnp.zeros((tail - 2, high.shape[1]), bf16)], axis=0)
        for i in range(parts_each):
            packed[b * parts_each + i, pl.ds(part, tail)] = both
    got[me] = packed[me]
    pl.semaphore_wait(barrier, others)

    def there(p):
        return pltpu.make_async_remote_copy(
            packed.at[p], got.at[me], send.at[p], recv.at[me], device_id=peer(p), device_id_type=MESH)

    def here(p):
        return pltpu.make_async_remote_copy(
            packed.at[p], got.at[p], send.at[p], recv.at[p], device_id=peer(p), device_id_type=MESH)

    def back(p):
        return pltpu.make_async_remote_copy(
            ready.at[p], out.at[pl.ds(pl.multiple_of(me * part, part), part)], bsend.at[p], brecv.at[me],
            device_id=peer(p), device_id_type=MESH)

    def home(p):
        return pltpu.make_async_remote_copy(
            ready.at[p], out.at[pl.ds(pl.multiple_of(p * part, part), part)], bsend.at[p], brecv.at[p],
            device_id=peer(p), device_id_type=MESH)

    def each(act):
        def one(d, carry):
            act((me + d) % count)
            return carry

        lax.fori_loop(1, count, one, 0)

    each(lambda p: there(p).start())
    for i in range(len(items)):
        for copy in seq_copies(i, 1):
            copy.start()

    def step(i, state):
        p = count - 1 - i if backward else i

        @pl.when(p != me)
        def _():
            here(p).wait_recv()

        ready[p] = state.astype(bf16)

        @pl.when(p != me)
        def _():
            back(p).start()

        decay = jnp.exp(got[p, pl.ds(part, 1)].astype(f32) + got[p, pl.ds(part + 1, 1)].astype(f32))
        return decay * state + got[p, pl.ds(0, part)].astype(f32)

    lax.fori_loop(0, count, step, jnp.zeros((part, value.shape[1]), f32))
    out[pl.ds(pl.multiple_of(me * part, part), part)] = ready[me]
    for i in range(len(items)):
        for copy in seq_copies(i, 1):
            copy.wait_recv()
        for copy in seq_copies(i, 2):
            copy.start()
    each(lambda p: home(p).wait_recv())
    each(lambda p: there(p).wait_send())
    each(lambda p: back(p).wait_send())
    for i in range(len(items)):
        for copy in seq_copies(i, 2):
            copy.wait()
        for copy in seq_copies(i, 1):
            copy.wait_send()


def exchange(value, logs, backward, collective_id, items=(), gathered=()):
    heads = lax.axis_size("head")
    count = lax.axis_size("seq") * heads
    rows, width = value.shape
    part = rows // count
    tail = 16
    dma = pltpu.SemaphoreType.DMA
    more = len(gathered)
    anywhere, near = pl.BlockSpec(memory_space=pl.ANY), pl.BlockSpec(memory_space=pltpu.VMEM)
    return pl.pallas_call(
        partial(exchange_body, count, heads, rows // logs.shape[0], backward, items, more),
        out_shape=[jax.ShapeDtypeStruct((rows, width), bf16)]
        + [jax.ShapeDtypeStruct(a.shape, a.dtype) for a in gathered],
        in_specs=[near] * 2 + [anywhere] * more,
        out_specs=[near] + [anywhere] * more,
        input_output_aliases={2 + i: 1 + i for i in range(more)},
        scratch_shapes=[
            pltpu.VMEM((count, part + tail, width), bf16),
            pltpu.VMEM((count, part + tail, width), bf16),
            pltpu.VMEM((count, part, width), bf16),
            dma((count,)), dma((count,)), dma((count,)), dma((count,)),
            dma((max(len(items), 1), 3, 3)), dma((max(len(items), 1), 3, 3)),
        ],
        compiler_params=pltpu.CompilerParams(
            collective_id=collective_id, has_side_effects=True, vmem_limit_bytes=16 * 2**20),
        name="exchange_states",
    )(value, logs, *gathered)


def aligned(x, size):
    return x if isinstance(x, int) else pl.multiple_of(x, size)


def finish_body(seq, plan, n_arrays, *refs):
    heads = 4
    head_masks = [1, 2]
    nz = len(head_masks)
    seq_masks = [1 << k for k in range(seq.bit_length() - 1)]
    split, joined = seq_masks[:3], seq_masks[3:]
    ns, nj = len(split), len(joined)
    lay_out, tok_grad = refs[:2]
    grads = refs[2 : 2 + n_arrays]
    lay_full, tok_full, halos = refs[2 + n_arrays : 5 + n_arrays]
    outs = refs[5 + n_arrays : 5 + 2 * n_arrays]
    scratch = refs[5 + 2 * n_arrays :]
    s, z = lax.axis_index("seq"), lax.axis_index("head")
    count = len(plan)
    per = ns + nj + nz
    owns = scratch[:count]
    recvs = [scratch[count + i * per : count + (i + 1) * per] for i in range(count)]
    (load_sem, send_sem, recv_sem, jsend, jrecv, zsend, zrecv, gsend, grecv, keep_sem, asend, arecv, stay, hsend,
     hrecv) = scratch[count * (1 + per) :]

    def peer(to_s, to_z):
        return {"seq": to_s, "head": to_z}

    def remote(src, dst, send, recv, to_s, to_z):
        return pltpu.make_async_remote_copy(src, dst, send, recv, device_id=peer(to_s, to_z), device_id_type=MESH)

    barrier = pltpu.get_barrier_semaphore()

    def greet(to_s, to_z):
        pl.semaphore_signal(barrier, 1, device_id=peer(to_s, to_z), device_id_type=MESH)

    for mask in seq_masks:
        greet(flipped(s, mask), z)
    for d in range(1, heads):
        greet(s, (z + d) % heads)

    @pl.when(s < seq - 1)
    def _():
        greet(s + 1, 0)

    greeted = len(seq_masks) + heads - 1

    @pl.when((z == 0) & (s > 0))
    def _():
        pl.semaphore_wait(barrier, greeted + heads)

    @pl.when((z != 0) | (s == 0))
    def _():
        pl.semaphore_wait(barrier, greeted)

    seqs, mine, _ = lay_out.shape
    width = lay_full.shape[2]

    def features(q):
        return pl.ds(aligned(q * width, width), width)

    def rows_to(q):
        return pl.ds(aligned(q * mine, mine), mine)

    def back_copies(q, source):
        return [
            (lay_out.at[:, :, features(q)], lay_full.at[:, rows_to(source)]),
            (tok_grad.at[:, pl.ds(HALO, mine), features(q)], tok_full.at[:, rows_to(source)]),
        ]

    def back_send(d):
        q = (z + d) % heads
        return [remote(a, b, asend.at[i, q], arecv.at[i, z], s, q) for i, (a, b) in enumerate(back_copies(q, z))]

    def back_wait(d):
        q = (z + d) % heads
        return [remote(a, b, asend.at[i, q], arecv.at[i, q], s, q) for i, (a, b) in enumerate(back_copies(z, q))]

    def stay_copies():
        return [pltpu.make_async_copy(a, b, stay.at[i]) for i, (a, b) in enumerate(back_copies(z, z))]

    def halo_send(d):
        q = (z + d) % heads
        return remote(tok_grad.at[:, pl.ds(0, HALO), features(q)], halos.at[z], hsend.at[q], hrecv.at[z], s, q)

    def halo_wait(d):
        q = (z + d) % heads
        return remote(tok_grad.at[:, pl.ds(0, HALO), features(z)], halos.at[q], hsend.at[q], hrecv.at[q], s, q)

    def halo_own():
        return pltpu.make_async_copy(tok_grad.at[:, pl.ds(0, HALO), features(z)], halos.at[z], stay.at[2])

    def halo_cross(q):
        return remote(tok_grad.at[:, pl.ds(0, HALO), features(q)], halos.at[0], hsend.at[q], hrecv.at[0], s - 1, q)

    def halo_from_next():
        return remote(tok_grad.at[:, pl.ds(0, HALO), features(z)], halos.at[0], hsend.at[0], hrecv.at[0], s + 1, 0)

    def to_features(first):
        for copy in stay_copies():
            copy.start() if first else copy.wait()
        for d in range(1, heads):
            for copy in back_send(d):
                copy.start() if first else copy.wait_send()
            if not first:
                for copy in back_wait(d):
                    copy.wait_recv()

        @pl.when(z != 0)
        def _():
            halo_own().start() if first else halo_own().wait()
            for d in range(1, heads):
                halo_send(d).start() if first else halo_send(d).wait_send()

        @pl.when((z == 0) & (s > 0))
        def _():
            for q in range(heads):
                halo_cross(q).start() if first else halo_cross(q).wait_send()

        if not first:
            for d in range(1, heads):

                @pl.when((z + d) % heads != 0)
                def _():
                    halo_wait(d).wait_recv()

            @pl.when(s < seq - 1)
            def _():
                halo_from_next().wait_recv()

    def masks(c):
        return split[:1] + (split[1:] if c % 2 == 0 else split[:0:-1])

    def bit(c, k):
        return s // masks(c)[k] % 2

    def extent(c):
        array, axis, first, size = plan[c]
        return size if axis == 0 else grads[array].shape[2]

    def kept(c, k):
        size = extent(c)
        return sum((bit(c, j) * (size >> (j + 1)) for j in range(1, k + 1)), 0)

    def cut(c, begin, size):
        _, axis, _, rows = plan[c]
        part = pl.ds(aligned(begin, size), size)
        return (part, slice(None)) if axis == 0 else (slice(None), part)

    def in_array(c, begin, size):
        _, axis, first, rows = plan[c]
        if axis == 0:
            return pl.ds(aligned(first + begin, size), size), slice(None)
        return pl.ds(first, rows), pl.ds(aligned(begin, size), size)

    def load(c):
        half = extent(c) // 2
        rows, columns = in_array(c, bit(c, 0) * half, half)
        return pltpu.make_async_copy(grads[plan[c][0]].at[:, rows, columns], owns[c], load_sem.at[c])

    def seq_copy(c, k):
        half = extent(c) >> (k + 1)
        other = (1 - bit(c, k)) * half
        if k == 0:
            rows, columns = in_array(c, other, half)
            source = grads[plan[c][0]].at[:, rows, columns]
        else:
            rows, columns = cut(c, kept(c, k - 1) + other, half)
            source = owns[c].at[:, rows, columns]
        return remote(source, recvs[c][k], send_sem.at[c, k], recv_sem.at[c, k], flipped(s, masks(c)[k]), z)

    def final(c):
        size = extent(c) >> ns
        return cut(c, kept(c, ns - 1), size)

    def joined_copy(c, k):
        rows, columns = final(c)
        return remote(
            owns[c].at[:, rows, columns], recvs[c][ns + k], jsend.at[c, k], jrecv.at[c, k], flipped(s, joined[k]), z)

    def head_copies(c, k):
        rows, columns = final(c)
        mask = head_masks[k]
        low, b = z % mask, z // mask % 2
        return [
            remote(
                owns[c].at[low + (1 - b) * mask + i * 2 * mask, rows, columns], recvs[c][ns + nj + k].at[i],
                zsend.at[c, k, i], zrecv.at[c, k, i], s, flipped(z, mask))
            for i in range(heads // (2 * mask))
        ]

    def add(c, k):
        _, axis, _, rows = plan[c]
        if k < ns:
            begin, size = kept(c, k), extent(c) >> (k + 1)
        else:
            begin, size = kept(c, ns - 1), extent(c) >> ns
        if k < ns + nj:
            many, place = heads, lambda i: i
        else:
            mask = head_masks[k - ns - nj]
            many = heads // (2 * mask)
            place = lambda i: z % mask + z // mask % 2 * mask + i * 2 * mask
        n_rows = size if axis == 0 else rows
        tile = min(16, n_rows)
        tiles = n_rows // tile
        received = recvs[c][k]

        def one(t, carry):
            i, r = t // tiles, t % tiles * tile
            there = pl.ds(pl.multiple_of(r, tile), tile)
            if axis == 0:
                here, columns = pl.ds(pl.multiple_of(begin + r, tile), tile), slice(None)
            else:
                here, columns = there, pl.ds(aligned(begin, size), size)
            q = place(i)
            total = owns[c][q, here, columns].astype(f32) + received[i, there].astype(f32)
            owns[c][q, here, columns] = total.astype(bf16)
            return carry

        lax.fori_loop(0, many * tiles, one, 0)

    def held(c, level):
        size = extent(c)
        return in_array(c, sum(bit(c, j) * (size >> (j + 1)) for j in range(level)), size >> level)

    def keep(c):
        rows, columns = final(c)
        to_rows, to_columns = held(c, ns)
        return pltpu.make_async_copy(
            owns[c].at[z, rows, columns], outs[plan[c][0]].at[to_rows, to_columns], keep_sem.at[c])

    def gather_copy(c, j):
        level = ns - j
        rows, columns = held(c, level)
        array = outs[plan[c][0]].at[rows, columns]
        return remote(array, array, gsend.at[c, j], grecv.at[c, j], flipped(s, masks(c)[level - 1]), z)

    for c in range(count):
        seq_copy(c, 0).start()
        load(c).start()
    to_features(True)
    last = per + 1 + ns

    def copies(c, k):
        if k < ns:
            return [seq_copy(c, k)]
        if k < ns + nj:
            return [joined_copy(c, k - ns)]
        if k < per:
            return head_copies(c, k - ns - nj)
        return [gather_copy(c, k - per - 1)]

    def advance(c, k):
        if k == 0:
            load(c).wait()
        if k == per:
            keep(c).wait()
        else:
            for copy in copies(c, k):
                copy.wait_recv()
        if k < per:
            if ns < k + 1 <= ns + nj:
                joined_copy_done(c, k)
            add(c, k)
        n = k + 1
        if n == per:
            keep(c).start()
        elif n < last:
            for copy in copies(c, n):
                copy.start()

    def joined_copy_done(c, k):
        joined_copy(c, k - ns).wait_send()

    pairs = count // 2
    for t in range(pairs + last - 1):
        for k in reversed(range(last)):
            p = t - k
            if 0 <= p < pairs:
                advance(2 * p, k)
                advance(2 * p + 1, k)
    to_features(False)
    for c in range(count):
        for k in range(last):
            if k != per and not ns <= k < ns + nj:
                for copy in copies(c, k):
                    copy.wait_send()


def finish_all(lay_out, tok_grad, arrays, plan, collective_id):
    seq, heads = lax.axis_size("seq"), lax.axis_size("head")
    nj = max(0, seq.bit_length() - 4)
    ns, nz = 3, 2
    seqs, mine, features = lay_out.shape
    width = features // heads
    owns, recvs = [], []
    for a, axis, first, rows in plan:
        columns = arrays[a].shape[2]
        cut = lambda k: (rows >> k, columns) if axis == 0 else (rows, columns >> k)
        owns.append(pltpu.VMEM((heads, *cut(1)), bf16))
        recvs += [pltpu.VMEM((heads, *cut(k + 1)), bf16) for k in range(ns)]
        recvs += [pltpu.VMEM((heads, *cut(ns)), bf16) for k in range(nj)]
        recvs += [pltpu.VMEM((heads >> (k + 1), *cut(ns)), bf16) for k in range(nz)]
    count = len(plan)
    dma = pltpu.SemaphoreType.DMA
    sems = [
        dma((count,)), dma((count, ns)), dma((count, ns)), dma((count, max(nj, 1))), dma((count, max(nj, 1))),
        dma((count, nz, heads // 2)), dma((count, nz, heads // 2)), dma((count, ns)), dma((count, ns)), dma((count,)),
        dma((2, heads)), dma((2, heads)), dma((3,)), dma((heads,)), dma((heads,)),
    ]
    anywhere = pl.BlockSpec(memory_space=pl.ANY)
    out_shape = [jax.ShapeDtypeStruct((seqs, heads * mine, width), bf16)] * 2
    out_shape += [jax.ShapeDtypeStruct((heads, seqs, HALO, width), bf16)]
    out_shape += [jax.ShapeDtypeStruct(a.shape[1:], bf16) for a in arrays]
    return pl.pallas_call(
        partial(finish_body, seq, plan, len(arrays)),
        out_shape=out_shape,
        in_specs=[anywhere] * (2 + len(arrays)),
        out_specs=[anywhere] * len(out_shape),
        scratch_shapes=owns + recvs + sems,
        compiler_params=pltpu.CompilerParams(
            collective_id=collective_id, has_side_effects=True, vmem_limit_bytes=60 * 2**20),
        name="finish_sums",
    )(lay_out, tok_grad, *arrays)


def row_scale(values):
    return lax.rsqrt(jnp.mean(values * values, axis=-1, keepdims=True) + epsilon)


def silu_slope(values):
    logistic = jax.nn.sigmoid(values)
    return logistic * (1.0 + values * (1.0 - logistic))


def norm_back(values, inverse, weights, upstream):
    weighted = weights * upstream
    return inverse * weighted - values * inverse**3 * jnp.mean(
        weighted * values, axis=-1, keepdims=True
    )


def rounded(values):
    return values.astype(bf16).astype(f32)


def dot(spec, left, right):
    return jnp.einsum(spec, left.astype(bf16), right.astype(bf16), preferred_element_type=f32)


def cumulated(spec, values, count):
    at = jnp.arange(count)
    lower = (at[:, None] >= at[None, :]).astype(f32)
    return jnp.einsum(spec, lower, values, precision=lax.Precision.HIGHEST, preferred_element_type=f32)


def whole(weight):
    seq = lax.axis_size("seq")
    part = weight.shape[0] // seq
    mine = lax.dynamic_slice_in_dim(weight, lax.axis_index("seq") * part, part, 0)
    every = lax.all_gather(mine, ("head", "seq"), axis=0, tiled=True)
    return every.reshape(lax.axis_size("head"), *weight.shape)


def chunks(array, rows, count):
    return [(array, 0, i * (rows // count), rows // count) for i in range(count)]


def local(
    tokens,
    decay_codes,
    cotangent,
    attn_gain,
    w_query,
    w_key,
    w_value,
    w_out_gate,
    conv_query,
    conv_key,
    conv_value,
    out_gain,
    w_out,
    mlp_gain,
    w_gate,
    w_up,
    w_down,
):
    seqs, rows, own_width = tokens.shape
    heads = lax.axis_size("head")
    place = lax.axis_index("seq") * heads + lax.axis_index("head")
    mine = rows // heads
    width = own_width * heads
    key_width = w_query.shape[1]
    value_width = w_value.shape[1]
    conv_width = 2 * key_width + value_width
    mixer_width = conv_width + value_width

    half, ff = width // 2, w_gate.shape[1]
    out_half, ff_half = w_out.shape[0] // 2, ff // 2
    items = [(0, 0, 0, 0, 0, width, 0, key_width), (1, 1, 0, 0, 0, width, key_width, key_width)]
    items += [(i, 2, 0, 0, i * half, half, 2 * key_width, value_width) for i in range(2)]
    items += [(i, 3, 0, 0, i * half, half, conv_width, value_width) for i in range(2)]
    items += [(i, 4, 1, 0, i * out_half, out_half, 0, width) for i in range(2)]
    pair = [(2 + 2 * a + i, 5 + a, 2 + a, 1, i * ff_half, ff_half, 0, width) for a in range(2) for i in range(2)]
    tokens_ext, codes, taps, w_mixer, w_proj, w_gate_all, w_up_all = start_all(
        tokens,
        decay_codes.astype(jnp.int16),
        jnp.concatenate([conv_query, conv_key, conv_value], axis=1),
        (w_query, w_key, w_value, w_out_gate, w_out, w_gate.T, w_up.T),
        items + pair,
        [3] * len(items) + [1] * len(pair),
        ((width, mixer_width), w_out.shape, w_down.shape, w_down.shape),
        1,
    )
    w_low = whole(w_down)
    upstream, codes = lax.optimization_barrier((cotangent, codes))
    upstream = lax.all_to_all(upstream, "head", 1, 2, tiled=True)

    first_rows = (jnp.arange(mine + HALO) < HALO) & (place == 0)
    resid_ext = jnp.where(first_rows[None, :, None], 0, tokens_ext).astype(f32)
    first_scale = row_scale(resid_ext)
    normed = (resid_ext * first_scale * attn_gain).astype(bf16)
    projected = dot("std,hde->hste", normed, w_mixer).astype(bf16)
    gate_rows = projected[:, :, HALO:, conv_width:].astype(f32)
    extended = projected[..., :conv_width].astype(f32)
    tap_count = taps.shape[1]
    lead = HALO - tap_count + 1
    conv_sum = sum(
        taps[:, j, None, None, :] * extended[:, :, lead + j : lead + j + mine] for j in range(tap_count)
    )
    activated = jax.nn.silu(conv_sum)
    blocks = mine // SPAN

    def spanned(values):
        return values.reshape(heads, seqs, blocks, SPAN, values.shape[-1])

    query = spanned(activated[..., :key_width])
    keyed = spanned(activated[..., key_width : 2 * key_width])
    valued = spanned(activated[..., 2 * key_width :])
    log_decay = -codes.astype(f32) * decay_unit
    log_decay = jnp.moveaxis(log_decay.reshape(seqs, blocks, SPAN, heads, key_width), 3, 0)
    cumul = cumulated("tu,hanuk->hantk", log_decay, SPAN)
    span_log = cumul[:, :, :, -1]
    running = cumulated("mn,hank->hamk", span_log, blocks)
    carry_decay = jnp.exp(running - span_log)
    log_total = running[:, :, -1].reshape(-1, key_width)
    positions = jnp.arange(SPAN)
    causal = positions[:, None] >= positions[None, :]
    grow = jnp.exp(cumul)
    shrink = jnp.exp(-cumul)
    to_end = jnp.exp(span_log[:, :, :, None] - cumul)
    scale = key_width ** (-0.5)
    query_exp = query * scale * grow
    keyed_exp = keyed * shrink
    keyed_end = keyed * to_end
    update = dot("hantk,hantv->hanvk", keyed_end, valued)
    span_decay = jnp.exp(span_log)
    starts = [jnp.zeros_like(update[:, :, 0])]
    for n in range(blocks):
        starts.append(span_decay[:, :, n, None, :] * starts[n] + update[:, :, n])
    local_end = starts.pop()
    flat = (-1, key_width)
    pair = [(item[0], 0, item[2] - 2, *item[3:]) for item in pair]
    incoming, w_gate_all, w_up_all = exchange(
        local_end.astype(bf16).reshape(flat), log_total, False, 2, pair, (w_gate_all, w_up_all)
    )
    incoming = incoming.reshape(local_end.shape).astype(f32)
    scores = jnp.where(causal, dot("hantk,hanuk->hantu", query_exp, keyed_exp), 0.0)
    inner = dot("hantu,hanuv->hantv", scores, valued)
    states = jnp.stack(starts, 2) + carry_decay[:, :, :, None, :] * incoming[:, :, None]
    core_rows = (inner + dot("hantk,hanvk->hantv", query_exp, states)).reshape(heads, seqs, mine, value_width)
    out_scale = row_scale(core_rows)
    normed_out = core_rows * out_scale * out_gain
    gate_silu = jax.nn.silu(gate_rows)
    gated = (normed_out * gate_silu).astype(bf16)
    resid = resid_ext[:, HALO:]
    hidden_in = resid + jnp.sum(rounded(dot("hste,hed->hstd", gated, w_proj)), axis=0)
    second_scale = row_scale(hidden_in)
    normed_two = (hidden_in * second_scale * mlp_gain).astype(bf16)
    gate_val = dot("std,hfd->hstf", normed_two, w_gate_all)
    up_val = dot("std,hfd->hstf", normed_two, w_up_all)
    gate_act = jax.nn.silu(gate_val)
    hidden = (gate_act * up_val).astype(bf16)
    layer_out = hidden_in + jnp.sum(rounded(dot("hstf,hfd->hstd", hidden, w_low)), axis=0)

    d_hidden = rounded(dot("std,hfd->hstf", upstream, w_low))
    grad_down = dot("hstf,std->hfd", hidden, upstream)
    d_gate = (d_hidden * up_val * silu_slope(gate_val)).astype(bf16)
    d_up = (d_hidden * gate_act).astype(bf16)
    grad_gate = dot("hstf,std->hfd", d_gate, normed_two)
    grad_up = dot("hstf,std->hfd", d_up, normed_two)
    d_normed_two = dot("hstf,hfd->std", d_gate, w_gate_all) + dot("hstf,hfd->std", d_up, w_up_all)
    d_hidden_in = upstream.astype(f32) + norm_back(hidden_in, second_scale, mlp_gain, d_normed_two)
    grad_mlp_gain = jnp.sum(d_normed_two * hidden_in * second_scale, axis=(0, 1))
    d_mixer = d_hidden_in.astype(bf16)
    grad_out = dot("hste,std->hed", gated, d_mixer)
    d_gated = rounded(dot("std,hed->hste", d_mixer, w_proj))
    d_normed_out = d_gated * gate_silu
    d_gate_rows = d_gated * normed_out * silu_slope(gate_rows)
    grad_out_gain = jnp.sum(d_normed_out * core_rows * out_scale, axis=(0, 1, 2))
    d_core = spanned(norm_back(core_rows, out_scale, out_gain, d_normed_out))

    d_states = dot("hantk,hantv->hanvk", query_exp, d_core)
    own_grad = jnp.sum(carry_decay[:, :, :, None, :] * d_states, axis=2)
    (leaving,) = exchange(own_grad.astype(bf16).reshape(flat), log_total, True, 3)
    d_ends = [leaving.reshape(own_grad.shape).astype(f32)]
    for n in range(blocks - 1, 0, -1):
        d_ends.append(span_decay[:, :, n, None, :] * d_ends[-1] + d_states[:, :, n])
    d_ends = jnp.stack(d_ends[::-1], 2)
    d_scores = jnp.where(causal, dot("hantv,hanuv->hantu", d_core, valued), 0.0)
    d_query = dot("hantu,hanuk->hantk", d_scores, keyed_exp) + dot("hantv,hanvk->hantk", d_core, states)
    d_query = d_query * scale * grow
    d_keyed = dot("hantu,hantk->hanuk", d_scores, query_exp) * shrink
    d_keyed = d_keyed + dot("hanuv,hanvk->hanuk", valued, d_ends) * to_end
    d_valued = dot("hantu,hantv->hanuv", scores, d_core) + dot("hanuk,hanvk->hanuv", keyed_end, d_ends)
    d_activated = jnp.concatenate(
        [a.reshape(heads, seqs, mine, -1) for a in (d_query, d_keyed, d_valued)], axis=-1
    )
    d_conv = d_activated * silu_slope(conv_sum)
    tap_grads = []
    d_extended = jnp.zeros(extended.shape, f32)
    for j in range(tap_count):
        tap_grads.append(jnp.sum(d_conv * extended[:, :, lead + j : lead + j + mine], axis=(1, 2)))
        d_extended = d_extended + jnp.pad(
            taps[:, j, None, None, :] * d_conv, ((0, 0), (0, 0), (lead + j, tap_count - 1 - j), (0, 0))
        )
    grad_taps = jnp.stack(tap_grads, 1)
    d_gate_ext = jnp.pad(d_gate_rows, ((0, 0), (0, 0), (HALO, 0), (0, 0)))
    d_projected = jnp.concatenate([d_extended, d_gate_ext], axis=-1).astype(bf16)
    grad_mixer = dot("std,hste->hde", normed, d_projected)
    d_normed = dot("hste,hde->std", d_projected, w_mixer)
    grad_attn_gain = jnp.sum(d_normed * resid_ext * first_scale, axis=(0, 1))
    tokens_grad = norm_back(resid_ext, first_scale, attn_gain, d_normed)
    tokens_grad = tokens_grad + jnp.pad(d_hidden_in, ((0, 0), (HALO, 0), (0, 0)))

    small = jnp.concatenate(
        [
            grad_attn_gain.reshape(heads, -1),
            grad_mlp_gain.reshape(heads, -1),
            jnp.broadcast_to(grad_out_gain, (heads, value_width)),
            grad_taps.reshape(heads, -1),
        ],
        axis=1,
    )
    small_rows = 256
    lanes = -(-small.shape[1] // (small_rows * 128)) * 128
    small = jnp.pad(small, ((0, 0), (0, small_rows * lanes - small.shape[1]))).reshape(heads, small_rows, lanes)
    arrays = [a.astype(bf16) for a in (grad_gate, grad_up, grad_down, grad_out, grad_mixer, small)]
    plan = (
        [(a, 1, i * (ff // 2), ff // 2) for a in range(3) for i in range(2)]
        + chunks(3, w_out.shape[0], 2)
        + chunks(4, width, 4)
        + chunks(5, small_rows, 2)
    )
    layer_out, tokens_grad, halos, *sums = finish_all(
        layer_out.astype(bf16), tokens_grad.astype(bf16), arrays, plan, 4
    )
    grad_gate, grad_up, grad_down, grad_out, grad_mixer, small = (a.astype(f32) for a in sums)
    layer_out = layer_out.astype(f32)
    last = lax.axis_index("seq") == lax.axis_size("seq") - 1
    halos = jnp.where(last & (jnp.arange(heads) == 0)[:, None, None, None], 0, halos).astype(f32)
    halos = jnp.moveaxis(jnp.roll(halos, -1, axis=0), 0, 1)
    halos = jnp.pad(halos, ((0, 0), (0, 0), (mine - HALO, 0), (0, 0))).reshape(tokens_grad.shape)
    tokens_grad = tokens_grad.astype(f32) + halos
    small = small.reshape(-1)
    at = 2 * own_width + value_width
    grad_taps = small[at : at + tap_count * conv_width].reshape(tap_count, conv_width)
    return (
        layer_out,
        tokens_grad,
        small[:own_width],
        grad_mixer[:, :key_width],
        grad_mixer[:, key_width : 2 * key_width],
        grad_mixer[:, 2 * key_width : conv_width],
        grad_mixer[:, conv_width:],
        grad_taps[:, :key_width],
        grad_taps[:, key_width : 2 * key_width],
        grad_taps[:, 2 * key_width :],
        small[2 * own_width : at],
        grad_out,
        small[own_width : 2 * own_width],
        grad_gate.T,
        grad_up.T,
        grad_down,
    )


def solution(mesh):
    in_specs = (
        P(None, "seq", "head"),
        P(None, "seq", "head"),
        P(None, "seq", "head"),
        P(),
        P(None, "head"),
        P(None, "head"),
        P(None, "head"),
        P(None, "head"),
        P(None, "head"),
        P(None, "head"),
        P(None, "head"),
        P(),
        P("head", None),
        P(),
        P(None, "head"),
        P(None, "head"),
        P("head", None),
    )
    out_specs = (
        P(None, "seq", "head"),
        P(None, "seq", "head"),
        P("head"),
        P(None, "head"),
        P(None, "head"),
        P(None, "head"),
        P(None, "head"),
        P(None, "head"),
        P(None, "head"),
        P(None, "head"),
        P(),
        P("head", None),
        P("head"),
        P(None, "head"),
        P(None, "head"),
        P("head", None),
    )
    return jax.shard_map(local, mesh=mesh, in_specs=in_specs, out_specs=out_specs, check_vma=False)
```

```python
from functools import partial

import jax
import jax.numpy as jnp
from jax import lax
from jax.experimental import pallas as pl
from jax.experimental.pallas import tpu as pltpu
from jax.sharding import PartitionSpec as P

SPAN = 64
HALO = 16
MESH = pl.DeviceIdType.MESH

epsilon = 1e-06
decay_unit = 2.0 ** (-17)
f32 = jnp.float32
bf16 = jnp.bfloat16

def row_scale(values):
    return lax.rsqrt(jnp.mean(values * values, axis=-1, keepdims=True) + epsilon)


def silu_slope(values):
    logistic = jax.nn.sigmoid(values)
    return logistic * (1.0 + values * (1.0 - logistic))


def norm_back(values, inverse, weights, upstream):
    weighted = weights * upstream
    return inverse * weighted - values * inverse**3 * jnp.mean(
        weighted * values, axis=-1, keepdims=True
    )


def rounded(values):
    return values.astype(bf16).astype(f32)


def whole(weight):
    seq = lax.axis_size("seq")
    part = weight.shape[0] // seq
    mine = lax.dynamic_slice_in_dim(weight, lax.axis_index("seq") * part, part, 0)
    every = lax.all_gather(mine, ("head", "seq"), axis=0, tiled=True)
    return every.reshape(lax.axis_size("head"), *weight.shape)


def flipped(place, mask):
    return place + mask - 2 * mask * (place // mask % 2)


def over_seq(items, gathered, gsend, grecv, s, z):
    heads = 4

    def order(i):
        return [4, 2, 1] if items[i][0] % 2 == 0 else [2, 4, 1]

    def span(i, j):
        _, _, to, axis, first, count, _, _ = items[i]
        size = count if axis == 0 else gathered[to].shape[2]
        begin = first if axis == 0 else 0
        for mask in order(i)[: j - 4 : -1] if j < 3 else []:
            size = size // 2
            begin = begin + (s // mask % 2) * size
        return pl.multiple_of(begin, size), size

    def seq_copies(i, j):
        _, _, to, axis, first, count, column, _ = items[i]
        begin, size = span(i, j)
        copies = []
        for d in range(1, heads):
            q = (z + d) % heads
            if axis == 0:
                place = gathered[to].at[q, pl.ds(begin, size), pl.ds(column, items[i][7])]
            else:
                place = gathered[to].at[q, pl.ds(first, count), pl.ds(begin, size)]
            copies.append(pltpu.make_async_remote_copy(
                place, place, gsend.at[i, j, d - 1], grecv.at[i, j, d - 1],
                device_id={"seq": flipped(s, order(i)[j]), "head": z}, device_id_type=MESH))
        return copies

    return span, seq_copies


def start_body(seq, n_weights, items, steps, *refs):
    tokens, codes, taps = refs[:3]
    weights = refs[3 : 3 + n_weights]
    out_tokens, out_codes, out_taps = refs[3 + n_weights : 6 + n_weights]
    n_sem = 11
    n_items = len(items)
    gathered = refs[6 + n_weights : -n_sem - n_items]
    held = refs[-n_sem - n_items : -n_sem]
    (tsend, trecv, hsend, hrecv, stay, zsend, zrecv, ysend, yrecv, gsend, grecv) = refs[-n_sem:]
    s, z = lax.axis_index("seq"), lax.axis_index("head")
    heads = 4
    masks = [1, 2, 4]

    def peer(to_s, to_z):
        return {"seq": to_s, "head": to_z}

    barrier = pltpu.get_barrier_semaphore()

    def greet(to_s, to_z):
        pl.semaphore_signal(barrier, 1, device_id=peer(to_s, to_z), device_id_type=MESH)

    for d in range(1, heads):
        greet(s, (z + d) % heads)
    for mask in masks:
        greet(flipped(s, mask), z)

    @pl.when((z == 0) & (s > 0))
    def _():
        for q in range(heads):
            greet(s - 1, q)

    greeted = heads - 1 + len(masks)

    @pl.when(s < seq - 1)
    def _():
        pl.semaphore_wait(barrier, greeted + 1)

    @pl.when(s == seq - 1)
    def _():
        pl.semaphore_wait(barrier, greeted)

    seqs, rows, width = tokens.shape
    mine = rows // heads

    def remote(src, dst, send, recv, to_s, to_z):
        return pltpu.make_async_remote_copy(src, dst, send, recv, device_id=peer(to_s, to_z), device_id_type=MESH)

    def columns(ref, q):
        n = ref.shape[2] // heads
        return pl.ds(pl.multiple_of(q * n, n), n)

    def sends(target, act):
        here = pl.ds(target * mine, mine)
        if target == 0:
            src, dst = tokens.at[:, pl.ds(0, mine)], out_tokens.at[:, pl.ds(HALO, mine), columns(out_tokens, z)]
        else:
            src = tokens.at[:, pl.ds(target * mine - HALO, mine + HALO)]
            dst = out_tokens.at[:, :, columns(out_tokens, z)]
        triples = [
            (src, dst),
            (codes.at[:, here], out_codes.at[:, :, columns(out_codes, z)]),
            (taps, out_taps.at[z]),
        ]

        @pl.when(z == target)
        def _():
            for i, (a, b) in enumerate(triples):
                copy = pltpu.make_async_copy(a, b, stay.at[i])
                if act == "start":
                    copy.start()
                else:
                    copy.wait()

        @pl.when(z != target)
        def _():
            for i, (a, b) in enumerate(triples):
                copy = remote(a, b, tsend.at[i, target], trecv.at[i, z], s, target)
                if act == "start":
                    copy.start()
                else:
                    copy.wait_send()

    def arrive(source):
        @pl.when(z != source)
        def _():
            here = pl.ds(0, mine)

            @pl.when(z == 0)
            def _():
                dst = out_tokens.at[:, pl.ds(HALO, mine), columns(out_tokens, source)]
                remote(tokens.at[:, here], dst, tsend.at[0, source], trecv.at[0, source], s, source).wait_recv()

            @pl.when(z != 0)
            def _():
                dst = out_tokens.at[:, :, columns(out_tokens, source)]
                remote(
                    tokens.at[:, pl.ds(0, mine + HALO)], dst, tsend.at[0, source], trecv.at[0, source], s, source
                ).wait_recv()

            for i, (a, b) in enumerate(
                ((codes.at[:, here], out_codes.at[:, :, columns(out_codes, source)]), (taps, out_taps.at[source]))
            ):
                remote(a, b, tsend.at[i + 1, source], trecv.at[i + 1, source], s, source).wait_recv()

    def halo_copy(source, to_s):
        return remote(
            tokens.at[:, pl.ds(rows - HALO, HALO)], out_tokens.at[:, pl.ds(0, HALO), columns(out_tokens, source)],
            hsend, hrecv.at[source], to_s, 0,
        )

    @pl.when(s < seq - 1)
    def _():
        halo_copy(z, s + 1).start()

    span, seq_copies = over_seq(items, gathered, gsend, grecv, s, z)

    def piece(i, j):
        _, weight, _, axis, first, count, column, _ = items[i]
        begin, size = span(i, j)
        wide = weights[weight].shape[1]
        if axis == 0:
            own = weights[weight].at[pl.ds(begin, size)]
            place = lambda ref, q: ref.at[q, pl.ds(begin, size), pl.ds(column, wide)]
        else:
            own = weights[weight].at[pl.ds(first, count), pl.ds(begin, size)]
            place = lambda ref, q: ref.at[q, pl.ds(first, count), pl.ds(begin, size)]
        return own, place

    def own_load(i):
        _, weight, _, _, first, count, _, _ = items[i]
        return pltpu.make_async_copy(weights[weight].at[pl.ds(first, count)], held[i], stay.at[3 + i])

    def own_store(i):
        _, weight, to, _, first, count, column, _ = items[i]
        wide = weights[weight].shape[1]
        return pltpu.make_async_copy(
            held[i], gathered[to].at[z, pl.ds(first, count), pl.ds(column, wide)], stay.at[3 + i])

    def far_copy(i):
        own, place = piece(i, 0)
        return remote(own, place(gathered[items[i][2]], z), zsend.at[i], zrecv.at[i], s, flipped(z, 2))

    def near_copies(i):
        own, place = piece(i, 0)
        to = gathered[items[i][2]]
        far = flipped(z, 2)
        near = flipped(z, 1)
        return [
            remote(own, place(to, z), ysend.at[i, 0], yrecv.at[i, 0], s, near),
            remote(place(to, far), place(to, far), ysend.at[i, 1], yrecv.at[i, 1], s, near),
        ]

    count = len(items)

    def stage(i, k):
        if k == 0:
            return [far_copy(i)]
        return near_copies(i) if k == 1 else seq_copies(i, k - 2)

    stages = 2 + len(masks)
    pairs = (max(item[0] for item in items) + 2) // 2
    for t in range(pairs + stages):
        for k in reversed(range(stages + 1)):
            for i in range(count):
                if items[i][0] // 2 != t - k or k > 2 + steps[i]:
                    continue
                if k > 0:
                    for copy in stage(i, k - 1):
                        copy.wait_recv()
                if k < 2 + steps[i]:
                    for copy in stage(i, k):
                        copy.start()
        if t == 0:
            for target in range(heads):
                sends(target, "start")
            for i in range(count):
                own_load(i).start()
    for i in range(count):
        own_load(i).wait()
        own_store(i).start()
    for source in range(heads):
        arrive(source)
    for target in range(heads):
        sends(target, "wait")

    @pl.when((z == 0) & (s > 0))
    def _():
        for q in range(heads):
            halo_copy(q, s - 1).wait_recv()

    @pl.when(s < seq - 1)
    def _():
        halo_copy(z, s + 1).wait_send()

    for i in range(count):
        own_store(i).wait()
        far_copy(i).wait_send()
        for copy in near_copies(i):
            copy.wait_send()
        for j in range(steps[i]):
            for copy in seq_copies(i, j):
                copy.wait_send()


def start_all(tokens, codes, taps, weights, items, steps, shapes, collective_id):
    seq, heads = lax.axis_size("seq"), lax.axis_size("head")
    seqs, rows, width = tokens.shape
    mine = rows // heads
    count = len(items)
    dma = pltpu.SemaphoreType.DMA
    anywhere = pl.BlockSpec(memory_space=pl.ANY)
    out_shape = [
        jax.ShapeDtypeStruct((seqs, mine + HALO, heads * width), tokens.dtype),
        jax.ShapeDtypeStruct((seqs, mine, heads * codes.shape[2]), codes.dtype),
        jax.ShapeDtypeStruct((heads, *taps.shape), taps.dtype),
    ] + [jax.ShapeDtypeStruct((heads, *shape), bf16) for shape in shapes]
    return pl.pallas_call(
        partial(start_body, seq, len(weights), items, steps),
        out_shape=out_shape,
        in_specs=[anywhere] * (3 + len(weights)),
        out_specs=[pl.BlockSpec(memory_space=pltpu.HBM)] * len(out_shape),
        scratch_shapes=[pltpu.VMEM((item[5], weights[item[1]].shape[1]), bf16) for item in items]
        + [
            dma((3, heads)), dma((3, heads)), dma, dma((heads,)), dma((3 + count,)),
            dma((count,)), dma((count,)), dma((count, 2)), dma((count, 2)), dma((count, 3, 3)), dma((count, 3, 3)),
        ],
        compiler_params=pltpu.CompilerParams(
            collective_id=collective_id, has_side_effects=True, vmem_limit_bytes=24 * 2**20),
        name="start_exchange",
    )(tokens, codes, taps, *weights)


def states_exchange(heads, count, per_block, backward, value, logs, out, scratch):
    packed, got, ready, send, recv, bsend, brecv = scratch
    me = lax.axis_index("seq") * heads + lax.axis_index("head")
    part = value.shape[0] // count
    tail = packed.shape[1] - part

    def peer(p):
        return {"seq": p // heads, "head": p % heads}

    def each(act):
        def one(d, carry):
            act((me + d) % count)
            return carry

        lax.fori_loop(1, count, one, 0)

    def greet():
        barrier = pltpu.get_barrier_semaphore()
        each(lambda p: pl.semaphore_signal(barrier, 1, device_id=peer(p), device_id_type=MESH))

    def pack():
        high = logs[...].astype(bf16)
        low = (logs[...] - high.astype(f32)).astype(bf16)

        def one(p, carry):
            packed[p, pl.ds(0, part)] = value[pl.ds(pl.multiple_of(p * part, part), part)]
            return carry

        lax.fori_loop(0, count, one, 0)
        parts_each = count * per_block // value.shape[0]
        zeros = jnp.zeros((tail - 2, high.shape[1]), bf16)
        for b in range(logs.shape[0]):
            both = jnp.concatenate([high[b : b + 1], low[b : b + 1], zeros], axis=0)
            for i in range(parts_each):
                packed[b * parts_each + i, pl.ds(part, tail)] = both
        got[me] = packed[me]

    def there(p, to):
        return pltpu.make_async_remote_copy(
            packed.at[p], got.at[to], send.at[p], recv.at[to], device_id=peer(p), device_id_type=MESH)

    def back(p, to):
        return pltpu.make_async_remote_copy(
            ready.at[p], out.at[pl.ds(pl.multiple_of(to * part, part), part)], bsend.at[p], brecv.at[to],
            device_id=peer(p), device_id_type=MESH)

    def begin():
        each(lambda p: there(p, me).start())

    def add_up():
        def step(i, state):
            p = count - 1 - i if backward else i

            @pl.when(p != me)
            def _():
                there(p, p).wait_recv()

            ready[p] = state.astype(bf16)

            @pl.when(p != me)
            def _():
                back(p, me).start()

            decay = jnp.exp(got[p, pl.ds(part, 1)].astype(f32) + got[p, pl.ds(part + 1, 1)].astype(f32))
            return decay * state + got[p, pl.ds(0, part)].astype(f32)

        lax.fori_loop(0, count, step, jnp.zeros((part, value.shape[1]), f32))
        out[pl.ds(pl.multiple_of(me * part, part), part)] = ready[me]

    def end():
        each(lambda p: back(p, p).wait_recv())
        each(lambda p: there(p, me).wait_send())
        each(lambda p: back(p, me).wait_send())

    return greet, pack, begin, add_up, end


def states_scratch(count, rows, width):
    part, tail = rows // count, 16
    dma = pltpu.SemaphoreType.DMA
    return [
        pltpu.VMEM((count, part + tail, width), bf16),
        pltpu.VMEM((count, part + tail, width), bf16),
        pltpu.VMEM((count, part, width), bf16),
        dma((count,)), dma((count,)), dma((count,)), dma((count,)),
    ]


def exchange_body(count, heads, per_block, items, n_more, *refs):
    value, logs = refs[:2]
    out = refs[2 + n_more]
    gathered = refs[3 + n_more : 3 + 2 * n_more]
    *scratch, gsend, grecv = refs[3 + 2 * n_more :]
    _, seq_copies = over_seq(items, gathered, gsend, grecv, lax.axis_index("seq"), lax.axis_index("head"))
    greet, pack, begin, add_up, end = states_exchange(heads, count, per_block, False, value, logs, out, scratch)
    greet()
    pack()
    pl.semaphore_wait(pltpu.get_barrier_semaphore(), count - 1)
    begin()
    for i in range(len(items)):
        for copy in seq_copies(i, 1):
            copy.start()
    add_up()
    for i in range(len(items)):
        for copy in seq_copies(i, 1):
            copy.wait_recv()
        for copy in seq_copies(i, 2):
            copy.start()
    end()
    for i in range(len(items)):
        for copy in seq_copies(i, 2):
            copy.wait()
        for copy in seq_copies(i, 1):
            copy.wait_send()


def exchange(value, logs, collective_id, items, gathered):
    heads = lax.axis_size("head")
    count = lax.axis_size("seq") * heads
    rows, width = value.shape
    more = len(gathered)
    dma = pltpu.SemaphoreType.DMA
    far, near = pl.BlockSpec(memory_space=pltpu.HBM), pl.BlockSpec(memory_space=pltpu.VMEM)
    return pl.pallas_call(
        partial(exchange_body, count, heads, rows // logs.shape[0], items, more),
        out_shape=[jax.ShapeDtypeStruct((rows, width), bf16)]
        + [jax.ShapeDtypeStruct(a.shape, a.dtype) for a in gathered],
        in_specs=[near] * 2 + [far] * more,
        out_specs=[near] + [far] * more,
        input_output_aliases={2 + i: 1 + i for i in range(more)},
        scratch_shapes=states_scratch(count, rows, width) + [dma((len(items), 3, 3)), dma((len(items), 3, 3))],
        compiler_params=pltpu.CompilerParams(
            collective_id=collective_id, has_side_effects=True, vmem_limit_bytes=16 * 2**20),
        name="exchange_states",
    )(value, logs, *gathered)


def aligned(x, size):
    return x if isinstance(x, int) else pl.multiple_of(x, size)


def sums_body(seq, plan, sources, shapes, n_given, n_left, n_right, lead, states, *refs):
    heads = 4
    nz = 1
    seq_masks = [1 << k for k in range(seq.bit_length() - 1)]
    split, joined = seq_masks[:3], seq_masks[3:]
    ns, nj = len(split), len(joined)
    refs = list(refs)

    def take(n):
        taken = refs[:n]
        del refs[:n]
        return taken

    value, logs = take(2) if states else (None, None)
    (act,) = take(1)
    given, lefts, rights = take(n_given), take(n_left), take(n_right)
    (new_state,) = take(1) if states else (None,)
    (act_full,) = take(1)
    (halos,) = take(1) if lead else (None,)
    n_arrays, count = len(sources), len(plan)
    outs = take(n_arrays)
    per = ns + nj + nz
    owns = take(count)
    recvs = [take(per) for _ in range(count)]
    staged = {c: take(1)[0] for c in range(count) if not isinstance(sources[plan[c][0]], int)}
    state_scratch = take(7) if states else None
    (load_sem, send_sem, recv_sem, jsend, jrecv, zsend, zrecv, gsend, grecv, keep_sem, asend, arecv, stay, hsend,
     hrecv) = refs
    s, z = lax.axis_index("seq"), lax.axis_index("head")

    def peer(to_s, to_z):
        return {"seq": to_s, "head": to_z}

    def remote(src, dst, send, recv, to_s, to_z):
        return pltpu.make_async_remote_copy(src, dst, send, recv, device_id=peer(to_s, to_z), device_id_type=MESH)

    seqs, rows_here, _ = act.shape
    mine = rows_here - lead
    width = act_full.shape[2]

    def features(q):
        return pl.ds(aligned(q * width, width), width)

    def rows_to(q):
        return pl.ds(aligned(q * mine, mine), mine)

    def back_copy(d, waits):
        q = (z + d) % heads
        to, of = (z, q) if waits else (q, z)
        return remote(
            act.at[:, pl.ds(lead, mine), features(to)], act_full.at[:, rows_to(of)], asend.at[q], arecv.at[of], s, q)

    def stay_copy():
        return pltpu.make_async_copy(
            act.at[:, pl.ds(lead, mine), features(z)], act_full.at[:, rows_to(z)], stay.at[0])

    def halo_copy(to_s, q, to, of):
        return remote(act.at[:, pl.ds(0, lead), features(to)], halos.at[of], hsend.at[q], hrecv.at[of], to_s, q)

    def halo_own():
        return pltpu.make_async_copy(act.at[:, pl.ds(0, lead), features(z)], halos.at[z], stay.at[1])

    def to_features(first):
        stay_copy().start() if first else stay_copy().wait()
        for d in range(1, heads):
            back_copy(d, False).start() if first else back_copy(d, False).wait_send()
            if not first:
                back_copy(d, True).wait_recv()
        if not lead:
            return

        @pl.when(z != 0)
        def _():
            halo_own().start() if first else halo_own().wait()
            for d in range(1, heads):
                q = (z + d) % heads
                halo_copy(s, q, q, z).start() if first else halo_copy(s, q, q, z).wait_send()

        @pl.when((z == 0) & (s > 0))
        def _():
            for q in range(heads):
                halo_copy(s - 1, q, q, 0).start() if first else halo_copy(s - 1, q, q, 0).wait_send()

        if not first:
            for d in range(1, heads):
                q = (z + d) % heads

                @pl.when(q != 0)
                def _():
                    halo_copy(s, q, z, q).wait_recv()

            @pl.when(s < seq - 1)
            def _():
                halo_copy(s + 1, 0, z, 0).wait_recv()

    def masks(c):
        return split[:1] + (split[1:] if c % 2 == 0 else split[:0:-1])

    def bit(c, k):
        return s // masks(c)[k] % 2

    def extent(c):
        array, axis, first, size = plan[c]
        return size if axis == 0 else shapes[array][1]

    def kept(c, k):
        size = extent(c)
        return sum((bit(c, j) * (size >> (j + 1)) for j in range(1, k + 1)), 0)

    def cut(c, begin, size):
        part = pl.ds(aligned(begin, size), size)
        return (part, slice(None)) if plan[c][1] == 0 else (slice(None), part)

    def in_array(c, begin, size):
        _, axis, first, rows = plan[c]
        if axis == 0:
            return pl.ds(aligned(first + begin, size), size), slice(None)
        return pl.ds(first, rows), pl.ds(aligned(begin, size), size)

    def load(c):
        half = extent(c) // 2
        rows, columns = in_array(c, bit(c, 0) * half, half)
        return pltpu.make_async_copy(given[sources[plan[c][0]]].at[:, rows, columns], owns[c], load_sem.at[c])

    def product(c):
        left_at, right_at, natural = sources[plan[c][0]]
        left, right = lefts[left_at], rights[right_at]
        half = extent(c) // 2

        def one(q, carry):
            for to, b in ((staged[c], 1 - bit(c, 0)), (owns[c], bit(c, 0))):
                rows, columns = in_array(c, b * half, half)
                total = None
                for i in range(left.shape[1]):
                    b_ = right[q if right.shape[0] > 1 else 0, i, :, columns]
                    if natural:
                        term = dot_tn(left[q if left.shape[0] > 1 else 0, i, :, rows], b_)
                    else:
                        term = dot_nn(left[q if left.shape[0] > 1 else 0, i, rows, :], b_)
                    total = term if total is None else total + term
                to[q] = total.astype(bf16)
            return carry

        lax.fori_loop(0, heads, one, 0)

    def seq_copy(c, k):
        half = extent(c) >> (k + 1)
        other = (1 - bit(c, k)) * half
        if k == 0 and c in staged:
            source = staged[c]
        elif k == 0:
            rows, columns = in_array(c, other, half)
            source = given[sources[plan[c][0]]].at[:, rows, columns]
        else:
            rows, columns = cut(c, kept(c, k - 1) + other, half)
            source = owns[c].at[:, rows, columns]
        return remote(source, recvs[c][k], send_sem.at[c, k], recv_sem.at[c, k], flipped(s, masks(c)[k]), z)

    def final(c):
        return cut(c, kept(c, ns - 1), extent(c) >> ns)

    def joined_copy(c, k):
        rows, columns = final(c)
        return remote(
            owns[c].at[:, rows, columns], recvs[c][ns + k], jsend.at[c, k], jrecv.at[c, k], flipped(s, joined[k]), z)

    def head_copy(c, d, waits):
        rows, columns = final(c)
        q = (z + d) % heads
        to, of = (z, q) if waits else (q, z)
        return remote(
            owns[c].at[to, rows, columns], recvs[c][ns + nj].at[of], zsend.at[c, q], zrecv.at[c, of], s, q)

    def add(c, k):
        axis, rows = plan[c][1], plan[c][3]
        if k < ns:
            begin, size = kept(c, k), extent(c) >> (k + 1)
        else:
            begin, size = kept(c, ns - 1), extent(c) >> ns
        received = recvs[c][k]
        tall = size if axis == 0 else rows
        wide = shapes[plan[c][0]][1] if axis == 0 else size
        tile = tall
        while tile * wide > 98304 and tile % 32 == 0:
            tile //= 2
        tiles = tall // tile

        def places(r):
            there = pl.ds(pl.multiple_of(r, tile), tile)
            if axis == 0:
                return there, pl.ds(pl.multiple_of(begin + r, tile), tile), slice(None)
            return there, there, pl.ds(aligned(begin, size), size)

        def one(t, carry):
            i = t // tiles
            there, here, columns = places(t % tiles * tile)
            owns[c][i, here, columns] = owns[c][i, here, columns] + received[i, there]
            return carry

        def last_one(t, carry):
            there, here, columns = places(t * tile)
            total = owns[c][z, here, columns].astype(f32)
            for d in range(1, heads):
                total = total + received[(z + d) % heads, there].astype(f32)
            owns[c][z, here, columns] = total.astype(bf16)
            return carry

        if k < ns + nj:
            lax.fori_loop(0, heads * tiles, one, 0)
        else:
            lax.fori_loop(0, tiles, last_one, 0)

    def held(c, level):
        size = extent(c)
        return in_array(c, sum(bit(c, j) * (size >> (j + 1)) for j in range(level)), size >> level)

    def keep(c):
        rows, columns = final(c)
        to_rows, to_columns = held(c, ns)
        return pltpu.make_async_copy(
            owns[c].at[z, rows, columns], outs[plan[c][0]].at[to_rows, to_columns], keep_sem.at[c])

    def gather_copy(c, j):
        level = ns - j
        rows, columns = held(c, level)
        array = outs[plan[c][0]].at[rows, columns]
        source = owns[c].at[z, *final(c)] if j == 0 else array
        return remote(source, array, gsend.at[c, j], grecv.at[c, j], flipped(s, masks(c)[level - 1]), z)

    barrier = pltpu.get_barrier_semaphore()
    if states:
        everyone = seq * heads
        greet, pack, begin, add_up, end = states_exchange(
            heads, everyone, value.shape[0] // logs.shape[0], True, value, logs, new_state, state_scratch)
        greet()
        pack()
        pl.semaphore_wait(barrier, everyone - 1)
        begin()
    else:

        def greet(to_s, to_z):
            pl.semaphore_signal(barrier, 1, device_id=peer(to_s, to_z), device_id_type=MESH)

        for mask in seq_masks:
            greet(flipped(s, mask), z)
        for d in range(1, heads):
            greet(s, (z + d) % heads)
        greeted = len(seq_masks) + heads - 1

        @pl.when(s < seq - 1)
        def _():
            greet(s + 1, 0)

        @pl.when((z == 0) & (s > 0))
        def _():
            pl.semaphore_wait(barrier, greeted + heads)

        @pl.when((z != 0) | (s == 0))
        def _():
            pl.semaphore_wait(barrier, greeted)

    last = per + ns

    def copies(c, k, waits=False):
        if k < ns:
            return [seq_copy(c, k)]
        if k < ns + nj:
            return [joined_copy(c, k - ns)]
        if k < per:
            return [head_copy(c, d, waits) for d in range(1, heads)]
        return [gather_copy(c, k - per)]

    def advance(c, k):
        if k == 0 and c not in staged:
            load(c).wait()
        if k == per:
            keep(c).wait()
        for copy in copies(c, k, True):
            copy.wait_recv()
        if ns <= k < ns + nj:
            joined_copy(c, k - ns).wait_send()
        if k < per:
            add(c, k)
        if k + 1 == per:
            keep(c).start()
        if k + 1 < last:
            for copy in copies(c, k + 1):
                copy.start()

    def begin_chunk(c):
        if c in staged:
            product(c)
        else:
            load(c).start()
        seq_copy(c, 0).start()

    pairs = count // 2
    for t in range(pairs + last):
        for k in reversed(range(last)):
            p = t - 1 - k
            if 0 <= p < pairs:
                advance(2 * p, k)
                advance(2 * p + 1, k)
        if t < pairs:
            begin_chunk(2 * t)
            begin_chunk(2 * t + 1)
        if t == 0:
            to_features(True)
        if t == 1 and states:
            add_up()
    to_features(False)
    for c in range(count):
        for k in range(last):
            if not ns <= k < ns + nj:
                for copy in copies(c, k):
                    copy.wait_send()
    if states:
        end()


def sums(act, lead, plan, sources, shapes, given, lefts, rights, collective_id, states=()):
    seq, heads = lax.axis_size("seq"), lax.axis_size("head")
    nj = max(0, seq.bit_length() - 4)
    ns = 3
    seqs, rows_here, features = act.shape
    width = features // heads
    owns, recvs, staged = [], [], []
    for a, axis, first, rows in plan:
        columns = shapes[a][1]
        cut = lambda k: (rows >> k, columns) if axis == 0 else (rows, columns >> k)
        owns.append(pltpu.VMEM((heads, *cut(1)), bf16))
        recvs += [pltpu.VMEM((heads, *cut(k + 1)), bf16) for k in range(ns)]
        recvs += [pltpu.VMEM((heads, *cut(ns)), bf16) for k in range(nj)]
        recvs.append(pltpu.VMEM((heads, *cut(ns)), bf16))
        if not isinstance(sources[a], int):
            staged.append(pltpu.VMEM((heads, *cut(1)), bf16))
    count = len(plan)
    dma = pltpu.SemaphoreType.DMA
    sems = [
        dma((count,)), dma((count, ns)), dma((count, ns)), dma((count, max(nj, 1))), dma((count, max(nj, 1))),
        dma((count, heads)), dma((count, heads)), dma((count, ns)), dma((count, ns)), dma((count,)),
        dma((heads,)), dma((heads,)), dma((2,)), dma((heads,)), dma((heads,)),
    ]
    anywhere, near = pl.BlockSpec(memory_space=pl.ANY), pl.BlockSpec(memory_space=pltpu.VMEM)
    out_shape = [jax.ShapeDtypeStruct((seqs, heads * (rows_here - lead), width), bf16)]
    if lead:
        out_shape += [jax.ShapeDtypeStruct((heads, seqs, lead, width), bf16)]
    out_shape += [jax.ShapeDtypeStruct(shape, bf16) for shape in shapes]
    out_specs = [anywhere] * len(out_shape)
    state_scratch = []
    if states:
        out_shape.insert(0, jax.ShapeDtypeStruct(states[0].shape, bf16))
        out_specs.insert(0, near)
        state_scratch = states_scratch(seq * heads, *states[0].shape)
    return pl.pallas_call(
        partial(sums_body, seq, plan, sources, shapes, len(given), len(lefts), len(rights), lead, bool(states)),
        out_shape=out_shape,
        in_specs=[near] * len(states) + [anywhere] * (1 + len(given)) + [near] * (len(lefts) + len(rights)),
        out_specs=out_specs,
        scratch_shapes=owns + recvs + staged + state_scratch + sems,
        compiler_params=pltpu.CompilerParams(
            collective_id=collective_id, has_side_effects=True, vmem_limit_bytes=60 * 2**20),
        name="sum_gradients",
    )(*states, act, *given, *lefts, *rights)


def dot_nt(a, b):
    return lax.dot_general(a, b, (((1,), (1,)), ((), ())), preferred_element_type=f32)


def dot_tn(a, b):
    return lax.dot_general(a, b, (((0,), (0,)), ((), ())), preferred_element_type=f32)


def mlp_body(per_head, hid, gain, cot, w_gate, w_up, w_low, lay, d_hid, normed, hidden, d_gate, d_up, d_gain, acc, part, dx):
    step = pl.program_id(0)

    @pl.when(step == 0)
    def _():
        values = hid[...]
        normed[...] = (values * row_scale(values) * gain[...]).astype(bf16)
        acc[...] = values
        dx[...] = jnp.zeros_like(dx)

    g = dot_nt(w_gate[0], normed[...])
    u = dot_nt(w_up[0], normed[...])
    dh = rounded(dot_nt(w_low[0], cot[...]))
    logistic = jax.nn.sigmoid(g)
    act = g * logistic
    h = (act * u).astype(bf16)
    dg = (dh * u * (logistic * (1.0 + g * (1.0 - logistic)))).astype(bf16)
    du = (dh * act).astype(bf16)
    hidden[0] = h
    d_gate[0] = dg
    d_up[0] = du
    term = dot_tn(h, w_low[0])
    first = step % per_head == 0

    @pl.when(first)
    def _():
        part[...] = term

    @pl.when(jnp.logical_not(first))
    def _():
        part[...] += term

    @pl.when(step % per_head == per_head - 1)
    def _():
        acc[...] += rounded(part[...])

    dx[...] += dot_tn(dg, w_gate[0]) + dot_tn(du, w_up[0])

    @pl.when(step == pl.num_programs(0) - 1)
    def _():
        lay[...] = acc[...].astype(bf16)
        values, upstream = hid[...], dx[...]
        scale = row_scale(values)
        d_gain[...] = jnp.sum(upstream * values * scale, axis=0, keepdims=True)
        d_hid[...] = cot[...].astype(f32) + norm_back(values, scale, gain[...], upstream)


def mlp(hidden_in, gain, upstream, w_gate, w_up, w_low):
    tokens, width = hidden_in.shape
    heads, units, _ = w_gate.shape
    per_head = 2
    block = units // per_head
    weights = pl.BlockSpec((1, block, width), lambda i: (i // per_head, i % per_head, 0))
    units_out = pl.BlockSpec((1, block, tokens), lambda i: (i // per_head, i % per_head, 0))
    all_of = lambda *shape: pl.BlockSpec(shape, lambda i: (0, 0))
    units_shape = jax.ShapeDtypeStruct((heads, units, tokens), bf16)
    token_shape = lambda kind: jax.ShapeDtypeStruct((tokens, width), kind)
    return pl.pallas_call(
        partial(mlp_body, per_head),
        grid=(heads * per_head,),
        in_specs=[all_of(tokens, width), all_of(1, width), all_of(tokens, width), weights, weights, weights],
        out_specs=[all_of(tokens, width)] * 3 + [units_out] * 3 + [all_of(1, width)],
        out_shape=[token_shape(bf16), token_shape(f32), token_shape(bf16)]
        + [units_shape] * 3
        + [jax.ShapeDtypeStruct((1, width), f32)],
        scratch_shapes=[pltpu.VMEM((tokens, width), f32)] * 3,
        compiler_params=pltpu.CompilerParams(vmem_limit_bytes=56 * 2**20),
        name="feed_forward",
    )(hidden_in, gain.reshape(1, width), upstream, w_gate, w_up, w_low)


def rows_after(values, count):
    if count == 0:
        return values
    return jnp.concatenate([values[count:], jnp.zeros((count, values.shape[1]), values.dtype)], axis=0)


def short_conv(pre, taps, rows):
    lead = HALO - taps.shape[0] + 1
    return sum(taps[j : j + 1] * pre[lead + j : lead + j + rows] for j in range(taps.shape[0]))


def spans(values):
    return [values[n * SPAN : (n + 1) * SPAN] for n in range(values.shape[0] // SPAN)]


def lower(count):
    row = lax.broadcasted_iota(jnp.int32, (count, count), 0)
    column = lax.broadcasted_iota(jnp.int32, (count, count), 1)
    return row, column


def causal_scores(left, right):
    row, column = lower(SPAN)
    return jnp.where(row >= column, dot_nt(left, right), 0.0).astype(bf16)


def dot_nn(a, b):
    return jnp.dot(a, b, preferred_element_type=f32)


def without_first(values, first):
    row = lax.broadcasted_iota(jnp.int32, values.shape, 0)
    return jnp.where((row < HALO) & (first > 0), 0.0, values.astype(f32))


def forward_one_body(first, tokens, gain, w, taps, codes, normed, pre, q_exp, k_exp, k_end, value, decay, starts, ends, logs, kept):
    h, i = pl.program_id(0), pl.program_id(1)

    @pl.when(h == 0)
    def _():
        values = without_first(tokens[0], first[0])
        kept[i] = (values * row_scale(values) * gain[...]).astype(bf16)

    normed[0] = kept[i]
    projected = dot_nn(kept[i], w[0]).astype(bf16)
    pre[0, 0] = projected
    rows = codes.shape[1]
    key = codes.shape[2]
    wide = taps.shape[2]
    act = jax.nn.silu(short_conv(projected[:, :wide].astype(f32), taps[0], rows))
    whole_codes = codes[0].astype(jnp.int32)
    high = whole_codes // 128
    row, column = lower(rows)
    within = ((row >= column) & (row // SPAN == column // SPAN)).astype(bf16)
    total = 128.0 * dot_nn(within, high.astype(bf16)) + dot_nn(within, (whole_codes - 128 * high).astype(bf16))
    log = total * -decay_unit
    decay[0, 0] = log
    grow = jnp.exp(log)
    q_exp[0, 0] = (act[:, :key] * key**-0.5 * grow).astype(bf16)
    k_exp[0, 0] = (act[:, key : 2 * key] * jnp.exp(-log)).astype(bf16)
    value[0, 0] = act[:, 2 * key :].astype(bf16)
    state = jnp.zeros((wide - 2 * key, key), f32)
    sums_log = jnp.zeros((1, key), f32)
    for n, part in enumerate(spans(log)):
        at = pl.ds(n * SPAN, SPAN)
        last = part[SPAN - 1 :]
        k_end[0, 0, at] = (act[n * SPAN : (n + 1) * SPAN, key : 2 * key] * jnp.exp(last - part)).astype(bf16)
        starts[0, 0, n] = state.astype(bf16)
        state = jnp.exp(last) * state + dot_tn(value[0, 0, at], k_end[0, 0, at])
        sums_log = sums_log + last
    ends[0, 0] = state.astype(bf16)
    logs[0, 0] = sums_log


def forward_one(first, tokens, gain, w, taps, codes):
    heads, width, columns = w.shape
    seqs, tall, _ = tokens.shape
    rows = tall - HALO
    tap_count, wide = taps.shape[1:]
    key = codes.shape[2] // heads
    wide_value = wide - 2 * key
    blocks = rows // SPAN
    per = lambda *shape: pl.BlockSpec((1, 1, *shape), lambda h, i: (h, i) + (0,) * len(shape))
    shape = lambda kind, *rest: jax.ShapeDtypeStruct((heads, seqs, *rest), kind)
    return pl.pallas_call(
        forward_one_body,
        grid=(heads, seqs),
        in_specs=[
            pl.BlockSpec(memory_space=pltpu.SMEM),
            pl.BlockSpec((1, tall, width), lambda h, i: (i, 0, 0)),
            pl.BlockSpec((1, width), lambda h, i: (0, 0)),
            pl.BlockSpec((1, width, columns), lambda h, i: (h, 0, 0)),
            pl.BlockSpec((1, tap_count, wide), lambda h, i: (h, 0, 0)),
            pl.BlockSpec((1, rows, key), lambda h, i: (i, 0, h)),
        ],
        out_specs=[
            pl.BlockSpec((1, tall, width), lambda h, i: (i, 0, 0)),
            per(tall, columns), per(rows, key), per(rows, key), per(rows, key), per(rows, wide_value), per(rows, key),
            per(blocks, wide_value, key), per(wide_value, key), per(1, key),
        ],
        out_shape=[
            jax.ShapeDtypeStruct((seqs, tall, width), bf16),
            shape(bf16, tall, columns), shape(bf16, rows, key), shape(bf16, rows, key), shape(bf16, rows, key),
            shape(bf16, rows, wide_value), shape(f32, rows, key), shape(bf16, blocks, wide_value, key),
            shape(bf16, wide_value, key), shape(f32, 1, key),
        ],
        scratch_shapes=[pltpu.VMEM((seqs, tall, width), bf16)],
        compiler_params=pltpu.CompilerParams(vmem_limit_bytes=48 * 2**20),
        name="attention_spans",
    )(first, tokens, gain.reshape(1, -1), w, taps, codes)


def forward_two_body(first, tokens, pre, q_exp, k_exp, value, decay, starts, incoming, out_gain, w_out, core, states, gated, hidden_in):
    h = pl.program_id(1)
    wide_value = value.shape[3]
    carry = jnp.ones((1, q_exp.shape[3]), f32)
    entering = incoming[0, 0].astype(f32)
    parts = []
    for n in range(starts.shape[2]):
        at = pl.ds(n * SPAN, SPAN)
        state = (starts[0, 0, n].astype(f32) + carry * entering).astype(bf16)
        states[0, 0, n] = state
        q = q_exp[0, 0, at]
        scores = causal_scores(q, k_exp[0, 0, at])
        parts.append(dot_nn(scores, value[0, 0, at]) + dot_nt(q, state))
        carry = carry * jnp.exp(decay[0, 0, pl.ds((n + 1) * SPAN - 1, 1)])
    out = jnp.concatenate(parts, axis=0)
    core[0, 0] = out
    gate = pre[0, 0, pl.ds(HALO, out.shape[0]), pl.ds(pre.shape[3] - wide_value, wide_value)].astype(f32)
    gated[0, 0] = (out * row_scale(out) * out_gain[...] * jax.nn.silu(gate)).astype(bf16)
    term = rounded(dot_nn(gated[0, 0], w_out[0]))

    @pl.when(h == 0)
    def _():
        hidden_in[0] = without_first(tokens[0], first[0])[HALO:] + term

    @pl.when(h > 0)
    def _():
        hidden_in[0] += term


def head_spec(*shape):
    return pl.BlockSpec((1, 1, *shape), lambda i, h: (h, i) + (0,) * len(shape))


def forward_two(first, tokens, pre, q_exp, k_exp, value, decay, starts, incoming, out_gain, w_out):
    heads, seqs, rows, key = q_exp.shape
    wide_value, width = w_out.shape[1:]
    blocks = rows // SPAN
    tall = rows + HALO
    per = head_spec
    shape = lambda kind, *rest: jax.ShapeDtypeStruct((heads, seqs, *rest), kind)
    return pl.pallas_call(
        forward_two_body,
        grid=(seqs, heads),
        in_specs=[
            pl.BlockSpec(memory_space=pltpu.SMEM),
            pl.BlockSpec((1, tall, width), lambda i, h: (i, 0, 0)),
            per(tall, pre.shape[3]), per(rows, key), per(rows, key), per(rows, wide_value), per(rows, key),
            per(blocks, wide_value, key), per(wide_value, key),
            pl.BlockSpec((1, wide_value), lambda i, h: (0, 0)),
            pl.BlockSpec((1, wide_value, width), lambda i, h: (h, 0, 0)),
        ],
        out_specs=[
            per(rows, wide_value), per(blocks, wide_value, key), per(rows, wide_value),
            pl.BlockSpec((1, rows, width), lambda i, h: (i, 0, 0)),
        ],
        out_shape=[
            shape(f32, rows, wide_value), shape(bf16, blocks, wide_value, key), shape(bf16, rows, wide_value),
            jax.ShapeDtypeStruct((seqs, rows, width), f32),
        ],
        compiler_params=pltpu.CompilerParams(vmem_limit_bytes=48 * 2**20),
        name="attention_outputs",
    )(first, tokens, pre, q_exp, k_exp, value, decay, starts, incoming, out_gain.reshape(1, -1), w_out)


def backward_one_body(d_hidden_in, w_out, core, pre, out_gain, q_exp, decay, d_mixer, d_core, d_gate, d_states, own_grad, d_gain):
    i, h = pl.program_id(0), pl.program_id(1)
    wide_value = core.shape[3]

    @pl.when(h == 0)
    def _():
        d_mixer[0] = d_hidden_in[0].astype(bf16)

    d_gated = rounded(dot_nt(d_mixer[0], w_out[0]))
    out = core[0, 0]
    gate = pre[0, 0, pl.ds(HALO, out.shape[0]), pl.ds(pre.shape[3] - wide_value, wide_value)].astype(f32)
    scale = row_scale(out)
    normed = out * scale
    d_normed = d_gated * jax.nn.silu(gate)
    d_gate[0, 0] = (d_gated * normed * out_gain[...] * silu_slope(gate)).astype(bf16)
    gain_term = jnp.sum(d_normed * normed, axis=0, keepdims=True)

    @pl.when((i == 0) & (h == 0))
    def _():
        d_gain[...] = gain_term

    @pl.when((i > 0) | (h > 0))
    def _():
        d_gain[...] += gain_term

    d_core[0, 0] = norm_back(out, scale, out_gain[...], d_normed).astype(bf16)
    carry = jnp.ones((1, q_exp.shape[3]), f32)
    total = jnp.zeros((wide_value, q_exp.shape[3]), f32)
    for n in range(out.shape[0] // SPAN):
        at = pl.ds(n * SPAN, SPAN)
        term = dot_tn(d_core[0, 0, at], q_exp[0, 0, at])
        d_states[0, 0, n] = term.astype(bf16)
        total = total + carry * term
        carry = carry * jnp.exp(decay[0, 0, pl.ds((n + 1) * SPAN - 1, 1)])
    own_grad[0, 0] = total.astype(bf16)


def backward_one(d_hidden_in, w_out, core, pre, out_gain, q_exp, decay):
    heads, seqs, rows, key = q_exp.shape
    wide_value, width = w_out.shape[1:]
    blocks = rows // SPAN
    per = head_spec
    shape = lambda kind, *rest: jax.ShapeDtypeStruct((heads, seqs, *rest), kind)
    by_seq = pl.BlockSpec((1, rows, width), lambda i, h: (i, 0, 0))
    gain = pl.BlockSpec((1, wide_value), lambda i, h: (0, 0))
    return pl.pallas_call(
        backward_one_body,
        grid=(seqs, heads),
        in_specs=[
            by_seq, pl.BlockSpec((1, wide_value, width), lambda i, h: (h, 0, 0)), per(rows, wide_value),
            per(rows + HALO, pre.shape[3]), gain, per(rows, key), per(rows, key),
        ],
        out_specs=[
            by_seq, per(rows, wide_value), per(rows, wide_value), per(blocks, wide_value, key), per(wide_value, key),
            gain,
        ],
        out_shape=[
            jax.ShapeDtypeStruct((seqs, rows, width), bf16), shape(bf16, rows, wide_value),
            shape(bf16, rows, wide_value), shape(bf16, blocks, wide_value, key), shape(bf16, wide_value, key),
            jax.ShapeDtypeStruct((1, wide_value), f32),
        ],
        compiler_params=pltpu.CompilerParams(vmem_limit_bytes=48 * 2**20),
        name="attention_outputs_back",
    )(d_hidden_in, w_out, core, pre, out_gain.reshape(1, -1), q_exp, decay)


def backward_two_body(
    first, tokens, gain, d_hidden_in, w, taps, pre, q_exp, k_exp, k_end, value, decay, states, d_core, d_states, leaving,
    d_gate, d_projected, d_tokens, d_taps, d_gain, d_normed,
):
    i, h = pl.program_id(0), pl.program_id(1)
    key, wide_value = q_exp.shape[3], value.shape[3]
    rows = q_exp.shape[2]
    blocks = rows // SPAN
    scale = key**-0.5
    d_end = leaving[0, 0].astype(f32)
    pieces = [None] * blocks
    for n in reversed(range(blocks)):
        at = pl.ds(n * SPAN, SPAN)
        q, k, v, dc = q_exp[0, 0, at], k_exp[0, 0, at], value[0, 0, at], d_core[0, 0, at]
        log = decay[0, 0, at]
        last = log[SPAN - 1 :]
        d_end_low = d_end.astype(bf16)
        scores = causal_scores(q, k)
        d_scores = causal_scores(dc, v)
        d_query = (dot_nn(d_scores, k) + dot_nn(dc, states[0, 0, n])) * (scale * jnp.exp(log))
        d_key = dot_tn(d_scores, q) * jnp.exp(-log) + dot_nn(v, d_end_low) * jnp.exp(last - log)
        d_value = dot_tn(scores, dc) + dot_nt(k_end[0, 0, at], d_end_low)
        pieces[n] = jnp.concatenate([d_query, d_key, d_value], axis=1)
        d_end = jnp.exp(last) * d_end + d_states[0, 0, n].astype(f32)
    d_act = jnp.concatenate(pieces, axis=0)
    tap_count, wide = taps.shape[1:]
    ext = pre[0, 0, :, pl.ds(0, wide)].astype(f32)
    d_conv = d_act * silu_slope(short_conv(ext, taps[0], rows))
    lead = HALO - tap_count + 1
    padded = jnp.concatenate([jnp.zeros((HALO, wide), f32), d_conv], axis=0)
    d_ext = jnp.zeros((HALO + rows, wide), f32)
    tap_terms = []
    for j in range(tap_count):
        moved = rows_after(padded, tap_count - 1 - j)
        d_ext = d_ext + taps[0, pl.ds(j, 1)] * moved
        tap_terms.append(jnp.sum(moved * ext, axis=0, keepdims=True))
    tap_terms = jnp.concatenate(tap_terms, axis=0)

    @pl.when(i == 0)
    def _():
        d_taps[h] = tap_terms

    @pl.when(i > 0)
    def _():
        d_taps[h] += tap_terms

    d_gate_ext = jnp.concatenate([jnp.zeros((HALO, wide_value), bf16), d_gate[0, 0]], axis=0)
    d_projected[0, 0] = jnp.concatenate([d_ext.astype(bf16), d_gate_ext], axis=1)
    term = dot_nt(d_projected[0, 0], w[0])

    @pl.when(h == 0)
    def _():
        d_normed[...] = term

    @pl.when(h > 0)
    def _():
        d_normed[...] += term

    @pl.when(h == pl.num_programs(1) - 1)
    def _():
        values, upstream = without_first(tokens[0], first[0]), d_normed[...]
        inverse = row_scale(values)
        gain_term = jnp.sum(upstream * values * inverse, axis=0, keepdims=True)
        d_gain[0] = gain_term
        back = norm_back(values, inverse, gain[...], upstream)
        d_tokens[0, pl.ds(0, HALO)] = back[:HALO].astype(bf16)
        d_tokens[0, pl.ds(HALO, rows)] = (back[HALO:] + d_hidden_in[0]).astype(bf16)


def backward_two(
    first, tokens, gain, d_hidden_in, w, taps, pre, q_exp, k_exp, k_end, value, decay, states, d_core, d_states, leaving, d_gate
):
    heads, seqs, rows, key = q_exp.shape
    width, columns = w.shape[1:]
    wide_value = value.shape[3]
    tap_count, wide = taps.shape[1:]
    blocks = rows // SPAN
    tall = rows + HALO
    per = head_spec
    by_seq = lambda n: pl.BlockSpec((1, n, width), lambda i, h: (i, 0, 0))
    return pl.pallas_call(
        backward_two_body,
        grid=(seqs, heads),
        in_specs=[
            pl.BlockSpec(memory_space=pltpu.SMEM), by_seq(tall), pl.BlockSpec((1, width), lambda i, h: (0, 0)),
            by_seq(rows), pl.BlockSpec((1, width, columns), lambda i, h: (h, 0, 0)),
            pl.BlockSpec((1, tap_count, wide), lambda i, h: (h, 0, 0)),
            per(tall, columns), per(rows, key), per(rows, key), per(rows, key), per(rows, wide_value), per(rows, key),
            per(blocks, wide_value, key), per(rows, wide_value), per(blocks, wide_value, key), per(wide_value, key),
            per(rows, wide_value),
        ],
        out_specs=[
            per(tall, columns), by_seq(tall), pl.BlockSpec((heads, tap_count, wide), lambda i, h: (0, 0, 0)), by_seq(1),
        ],
        out_shape=[
            jax.ShapeDtypeStruct((heads, seqs, tall, columns), bf16),
            jax.ShapeDtypeStruct((seqs, tall, width), bf16),
            jax.ShapeDtypeStruct((heads, tap_count, wide), f32),
            jax.ShapeDtypeStruct((seqs, 1, width), f32),
        ],
        scratch_shapes=[pltpu.VMEM((tall, width), f32)],
        compiler_params=pltpu.CompilerParams(vmem_limit_bytes=48 * 2**20),
        name="attention_spans_back",
    )(
        first, tokens, gain.reshape(1, -1), d_hidden_in, w, taps, pre, q_exp, k_exp, k_end, value, decay, states, d_core,
        d_states, leaving, d_gate,
    )


def chunks(array, rows, count):
    return [(array, 0, i * (rows // count), rows // count) for i in range(count)]


def local(
    tokens,
    decay_codes,
    cotangent,
    attn_gain,
    w_query,
    w_key,
    w_value,
    w_out_gate,
    conv_query,
    conv_key,
    conv_value,
    out_gain,
    w_out,
    mlp_gain,
    w_gate,
    w_up,
    w_down,
):
    seqs, rows, own_width = tokens.shape
    heads = lax.axis_size("head")
    place = lax.axis_index("seq") * heads + lax.axis_index("head")
    mine = rows // heads
    width = own_width * heads
    key_width = w_query.shape[1]
    value_width = w_value.shape[1]
    conv_width = 2 * key_width + value_width
    mixer_width = conv_width + value_width

    half, ff = width // 2, w_gate.shape[1]
    out_half, ff_half = w_out.shape[0] // 2, ff // 2
    items = [(0, 0, 0, 0, 0, width, 0, key_width), (1, 1, 0, 0, 0, width, key_width, key_width)]
    items += [(i, 2, 0, 0, i * half, half, 2 * key_width, value_width) for i in range(2)]
    items += [(i, 3, 0, 0, i * half, half, conv_width, value_width) for i in range(2)]
    items += [(i, 4, 1, 0, i * out_half, out_half, 0, width) for i in range(2)]
    pair = [(2 + 2 * a + i, 5 + a, 2 + a, 1, i * ff_half, ff_half, 0, width) for a in range(2) for i in range(2)]
    tokens_ext, codes, taps, w_mixer, w_proj, w_gate_all, w_up_all = start_all(
        tokens,
        decay_codes.astype(jnp.int16),
        jnp.concatenate([conv_query, conv_key, conv_value], axis=1),
        (w_query, w_key, w_value, w_out_gate, w_out, w_gate.T, w_up.T),
        items + pair,
        [3] * len(items) + [1] * len(pair),
        ((width, mixer_width), w_out.shape, w_down.shape, w_down.shape),
        1,
    )
    upstream, low_part, codes = lax.optimization_barrier((cotangent, w_down, codes))
    upstream = lax.all_to_all(upstream, "head", 1, 2, tiled=True)
    w_low = whole(low_part)

    first = (place == 0).astype(jnp.int32).reshape(1)
    normed, pre, q_exp, k_exp, k_end, value, decay, starts, local_end, log_total = forward_one(
        first, tokens_ext, attn_gain, w_mixer, taps, codes
    )
    flat = (-1, key_width)
    log_total = log_total.reshape(flat)
    pair = [(item[0], 0, item[2] - 2, *item[3:]) for item in pair]
    incoming, w_gate_all, w_up_all = exchange(
        local_end.reshape(flat), log_total, 2, pair, (w_gate_all, w_up_all)
    )
    core, states, gated, hidden_in = forward_two(
        first, tokens_ext, pre, q_exp, k_exp, value, decay, starts, incoming.reshape(local_end.shape), out_gain, w_proj
    )
    layer_out, d_hidden_in, normed_two, hidden, d_gate, d_up, grad_mlp_gain = mlp(
        hidden_in.reshape(-1, width), mlp_gain, upstream.reshape(-1, width), w_gate_all, w_up_all, w_low
    )
    d_hidden_in = d_hidden_in.reshape(hidden_in.shape)
    layer_out = layer_out.reshape(hidden_in.shape)
    d_mixer, d_core, d_gate_rows, d_states, own_grad, grad_out_gain = backward_one(
        d_hidden_in, w_proj, core, pre, out_gain, q_exp, decay
    )
    ff_part = ff // 4
    ff_plan = [(a, 1, i * ff_part, ff_part) for a in range(3) for i in range(4)]
    leaving, layer_out, grad_gate, grad_up, grad_down = sums(
        layer_out,
        0,
        ff_plan,
        [(0, 0, False), (1, 0, False), (2, 1, False)],
        [w_down.shape] * 3,
        (),
        [a[:, None] for a in (d_gate, d_up, hidden)],
        [normed_two[None, None], upstream.reshape(1, 1, -1, width)],
        3,
        (own_grad.reshape(flat), log_total),
    )
    d_projected, tokens_grad, grad_taps, grad_attn_gain = backward_two(
        first, tokens_ext, attn_gain, d_hidden_in, w_mixer, taps, pre, q_exp, k_exp, k_end, value, decay, states, d_core,
        d_states, leaving.reshape(local_end.shape), d_gate_rows,
    )

    small = jnp.concatenate(
        [
            jnp.sum(grad_attn_gain, axis=0).reshape(heads, -1),
            grad_mlp_gain.reshape(heads, -1),
            jnp.broadcast_to(grad_out_gain, (heads, value_width)),
            grad_taps.reshape(heads, -1),
        ],
        axis=1,
    )
    small_rows = 256
    lanes = -(-small.shape[1] // (small_rows * 128)) * 128
    small = jnp.pad(small, ((0, 0), (0, small_rows * lanes - small.shape[1]))).reshape(heads, small_rows, lanes)
    mixer_plan = chunks(0, width, 4) + [(1, 1, i * out_half, out_half) for i in range(2)] + chunks(2, small_rows, 2)
    tokens_grad, halos, grad_mixer, grad_out, small = sums(
        tokens_grad,
        HALO,
        mixer_plan,
        [(0, 0, True), (1, 1, True), 0],
        [(width, mixer_width), w_out.shape, small.shape[1:]],
        [small.astype(bf16)],
        [normed[None], gated],
        [d_projected, d_mixer[None]],
        4,
    )
    grad_gate, grad_up, grad_down, grad_out, grad_mixer, small = (
        a.astype(f32) for a in (grad_gate, grad_up, grad_down, grad_out, grad_mixer, small)
    )
    layer_out = layer_out.astype(f32)
    last = lax.axis_index("seq") == lax.axis_size("seq") - 1
    halos = jnp.where(last & (jnp.arange(heads) == 0)[:, None, None, None], 0, halos).astype(f32)
    halos = jnp.moveaxis(jnp.roll(halos, -1, axis=0), 0, 1)
    halos = jnp.pad(halos, ((0, 0), (0, 0), (mine - HALO, 0), (0, 0))).reshape(tokens_grad.shape)
    tokens_grad = tokens_grad.astype(f32) + halos
    small = small.reshape(-1)
    at = 2 * own_width + value_width
    grad_taps = small[at : at + taps[0].size].reshape(taps.shape[1:])
    return (
        layer_out,
        tokens_grad,
        small[:own_width],
        grad_mixer[:, :key_width],
        grad_mixer[:, key_width : 2 * key_width],
        grad_mixer[:, 2 * key_width : conv_width],
        grad_mixer[:, conv_width:],
        grad_taps[:, :key_width],
        grad_taps[:, key_width : 2 * key_width],
        grad_taps[:, 2 * key_width :],
        small[2 * own_width : at],
        grad_out,
        small[own_width : 2 * own_width],
        grad_gate.T,
        grad_up.T,
        grad_down,
    )


def solution(mesh):
    in_specs = (
        P(None, "seq", "head"),
        P(None, "seq", "head"),
        P(None, "seq", "head"),
        P(),
        P(None, "head"),
        P(None, "head"),
        P(None, "head"),
        P(None, "head"),
        P(None, "head"),
        P(None, "head"),
        P(None, "head"),
        P(),
        P("head", None),
        P(),
        P(None, "head"),
        P(None, "head"),
        P("head", None),
    )
    out_specs = (
        P(None, "seq", "head"),
        P(None, "seq", "head"),
        P("head"),
        P(None, "head"),
        P(None, "head"),
        P(None, "head"),
        P(None, "head"),
        P(None, "head"),
        P(None, "head"),
        P(None, "head"),
        P(),
        P("head", None),
        P("head"),
        P(None, "head"),
        P(None, "head"),
        P("head", None),
    )
    return jax.shard_map(local, mesh=mesh, in_specs=in_specs, out_specs=out_specs, check_vma=False)
```

```python
from functools import partial

import jax
import jax.numpy as jnp
from jax import lax
from jax.experimental import pallas as pl
from jax.experimental.pallas import tpu as pltpu
from jax.sharding import PartitionSpec as P

SPAN = 64
HALO = 16
MESH = pl.DeviceIdType.MESH

epsilon = 1e-06
decay_unit = 2.0 ** (-17)
f32 = jnp.float32
bf16 = jnp.bfloat16

def row_scale(values):
    return lax.rsqrt(jnp.mean(values * values, axis=-1, keepdims=True) + epsilon)


def silu_slope(values):
    logistic = jax.nn.sigmoid(values)
    return logistic * (1.0 + values * (1.0 - logistic))


def norm_back(values, inverse, weights, upstream):
    weighted = weights * upstream
    return inverse * weighted - values * inverse**3 * jnp.mean(
        weighted * values, axis=-1, keepdims=True
    )


def rounded(values):
    return values.astype(bf16).astype(f32)


def whole(weight):
    seq = lax.axis_size("seq")
    part = weight.shape[0] // seq
    mine = lax.dynamic_slice_in_dim(weight, lax.axis_index("seq") * part, part, 0)
    every = lax.all_gather(mine, ("head", "seq"), axis=0, tiled=True)
    return every.reshape(lax.axis_size("head"), *weight.shape)


def flipped(place, mask):
    return place + mask - 2 * mask * (place // mask % 2)


def over_seq(items, gathered, gsend, grecv, s, z):
    heads = 4

    def order(i):
        return [4, 2, 1] if items[i][0] % 2 == 0 else [2, 4, 1]

    def span(i, j):
        _, _, to, axis, first, count, _, _ = items[i]
        size = count if axis == 0 else gathered[to].shape[2]
        begin = first if axis == 0 else 0
        for mask in order(i)[: j - 4 : -1] if j < 3 else []:
            size = size // 2
            begin = begin + (s // mask % 2) * size
        return pl.multiple_of(begin, size), size

    def seq_copies(i, j):
        _, _, to, axis, first, count, column, _ = items[i]
        begin, size = span(i, j)
        copies = []
        for d in range(1, heads):
            q = (z + d) % heads
            if axis == 0:
                place = gathered[to].at[q, pl.ds(begin, size), pl.ds(column, items[i][7])]
            else:
                place = gathered[to].at[q, pl.ds(first, count), pl.ds(begin, size)]
            copies.append(pltpu.make_async_remote_copy(
                place, place, gsend.at[i, j, d - 1], grecv.at[i, j, d - 1],
                device_id={"seq": flipped(s, order(i)[j]), "head": z}, device_id_type=MESH))
        return copies

    return span, seq_copies


def start_body(seq, n_weights, items, steps, *refs):
    tokens, codes, taps = refs[:3]
    weights = refs[3 : 3 + n_weights]
    out_tokens, out_codes, out_taps = refs[3 + n_weights : 6 + n_weights]
    n_sem = 11
    n_items = len(items)
    gathered = refs[6 + n_weights : -n_sem - n_items]
    held = refs[-n_sem - n_items : -n_sem]
    (tsend, trecv, hsend, hrecv, stay, zsend, zrecv, ysend, yrecv, gsend, grecv) = refs[-n_sem:]
    s, z = lax.axis_index("seq"), lax.axis_index("head")
    heads = 4
    masks = [1, 2, 4]

    def peer(to_s, to_z):
        return {"seq": to_s, "head": to_z}

    barrier = pltpu.get_barrier_semaphore()

    def greet(to_s, to_z):
        pl.semaphore_signal(barrier, 1, device_id=peer(to_s, to_z), device_id_type=MESH)

    for d in range(1, heads):
        greet(s, (z + d) % heads)
    for mask in masks:
        greet(flipped(s, mask), z)

    @pl.when((z == 0) & (s > 0))
    def _():
        for q in range(heads):
            greet(s - 1, q)

    greeted = heads - 1 + len(masks)

    @pl.when(s < seq - 1)
    def _():
        pl.semaphore_wait(barrier, greeted + 1)

    @pl.when(s == seq - 1)
    def _():
        pl.semaphore_wait(barrier, greeted)

    seqs, rows, width = tokens.shape
    mine = rows // heads

    def remote(src, dst, send, recv, to_s, to_z):
        return pltpu.make_async_remote_copy(src, dst, send, recv, device_id=peer(to_s, to_z), device_id_type=MESH)

    def columns(ref, q):
        n = ref.shape[2] // heads
        return pl.ds(pl.multiple_of(q * n, n), n)

    def sends(target, act):
        here = pl.ds(target * mine, mine)
        if target == 0:
            src, dst = tokens.at[:, pl.ds(0, mine)], out_tokens.at[:, pl.ds(HALO, mine), columns(out_tokens, z)]
        else:
            src = tokens.at[:, pl.ds(target * mine - HALO, mine + HALO)]
            dst = out_tokens.at[:, :, columns(out_tokens, z)]
        triples = [
            (src, dst),
            (codes.at[:, here], out_codes.at[:, :, columns(out_codes, z)]),
            (taps, out_taps.at[z]),
        ]

        @pl.when(z == target)
        def _():
            for i, (a, b) in enumerate(triples):
                copy = pltpu.make_async_copy(a, b, stay.at[i])
                if act == "start":
                    copy.start()
                else:
                    copy.wait()

        @pl.when(z != target)
        def _():
            for i, (a, b) in enumerate(triples):
                copy = remote(a, b, tsend.at[i, target], trecv.at[i, z], s, target)
                if act == "start":
                    copy.start()
                else:
                    copy.wait_send()

    def arrive(source):
        @pl.when(z != source)
        def _():
            here = pl.ds(0, mine)

            @pl.when(z == 0)
            def _():
                dst = out_tokens.at[:, pl.ds(HALO, mine), columns(out_tokens, source)]
                remote(tokens.at[:, here], dst, tsend.at[0, source], trecv.at[0, source], s, source).wait_recv()

            @pl.when(z != 0)
            def _():
                dst = out_tokens.at[:, :, columns(out_tokens, source)]
                remote(
                    tokens.at[:, pl.ds(0, mine + HALO)], dst, tsend.at[0, source], trecv.at[0, source], s, source
                ).wait_recv()

            for i, (a, b) in enumerate(
                ((codes.at[:, here], out_codes.at[:, :, columns(out_codes, source)]), (taps, out_taps.at[source]))
            ):
                remote(a, b, tsend.at[i + 1, source], trecv.at[i + 1, source], s, source).wait_recv()

    def halo_copy(source, to_s):
        return remote(
            tokens.at[:, pl.ds(rows - HALO, HALO)], out_tokens.at[:, pl.ds(0, HALO), columns(out_tokens, source)],
            hsend, hrecv.at[source], to_s, 0,
        )

    @pl.when(s < seq - 1)
    def _():
        halo_copy(z, s + 1).start()

    span, seq_copies = over_seq(items, gathered, gsend, grecv, s, z)

    def piece(i, j):
        _, weight, _, axis, first, count, column, _ = items[i]
        begin, size = span(i, j)
        wide = weights[weight].shape[1]
        if axis == 0:
            own = weights[weight].at[pl.ds(begin, size)]
            place = lambda ref, q: ref.at[q, pl.ds(begin, size), pl.ds(column, wide)]
        else:
            own = weights[weight].at[pl.ds(first, count), pl.ds(begin, size)]
            place = lambda ref, q: ref.at[q, pl.ds(first, count), pl.ds(begin, size)]
        return own, place

    def own_load(i):
        _, weight, _, _, first, count, _, _ = items[i]
        return pltpu.make_async_copy(weights[weight].at[pl.ds(first, count)], held[i], stay.at[3 + i])

    def own_store(i):
        _, weight, to, _, first, count, column, _ = items[i]
        wide = weights[weight].shape[1]
        return pltpu.make_async_copy(
            held[i], gathered[to].at[z, pl.ds(first, count), pl.ds(column, wide)], stay.at[3 + i])

    def far_copy(i):
        own, place = piece(i, 0)
        return remote(own, place(gathered[items[i][2]], z), zsend.at[i], zrecv.at[i], s, flipped(z, 2))

    def near_copies(i):
        own, place = piece(i, 0)
        to = gathered[items[i][2]]
        far = flipped(z, 2)
        near = flipped(z, 1)
        return [
            remote(own, place(to, z), ysend.at[i, 0], yrecv.at[i, 0], s, near),
            remote(place(to, far), place(to, far), ysend.at[i, 1], yrecv.at[i, 1], s, near),
        ]

    count = len(items)

    def stage(i, k):
        if k == 0:
            return [far_copy(i)]
        return near_copies(i) if k == 1 else seq_copies(i, k - 2)

    stages = 2 + len(masks)
    pairs = (max(item[0] for item in items) + 2) // 2
    for t in range(pairs + stages):
        for k in reversed(range(stages + 1)):
            for i in range(count):
                if items[i][0] // 2 != t - k or k > 2 + steps[i]:
                    continue
                if k > 0:
                    for copy in stage(i, k - 1):
                        copy.wait_recv()
                if k < 2 + steps[i]:
                    for copy in stage(i, k):
                        copy.start()
        if t == 0:
            for target in range(heads):
                sends(target, "start")
            for i in range(count):
                own_load(i).start()
    for i in range(count):
        own_load(i).wait()
        own_store(i).start()
    for source in range(heads):
        arrive(source)
    for target in range(heads):
        sends(target, "wait")

    @pl.when((z == 0) & (s > 0))
    def _():
        for q in range(heads):
            halo_copy(q, s - 1).wait_recv()

    @pl.when(s < seq - 1)
    def _():
        halo_copy(z, s + 1).wait_send()

    for i in range(count):
        own_store(i).wait()
        far_copy(i).wait_send()
        for copy in near_copies(i):
            copy.wait_send()
        for j in range(steps[i]):
            for copy in seq_copies(i, j):
                copy.wait_send()


def start_all(tokens, codes, taps, weights, items, steps, shapes, collective_id):
    seq, heads = lax.axis_size("seq"), lax.axis_size("head")
    seqs, rows, width = tokens.shape
    mine = rows // heads
    count = len(items)
    dma = pltpu.SemaphoreType.DMA
    anywhere = pl.BlockSpec(memory_space=pl.ANY)
    out_shape = [
        jax.ShapeDtypeStruct((seqs, mine + HALO, heads * width), tokens.dtype),
        jax.ShapeDtypeStruct((seqs, mine, heads * codes.shape[2]), codes.dtype),
        jax.ShapeDtypeStruct((heads, *taps.shape), taps.dtype),
    ] + [jax.ShapeDtypeStruct((heads, *shape), bf16) for shape in shapes]
    return pl.pallas_call(
        partial(start_body, seq, len(weights), items, steps),
        out_shape=out_shape,
        in_specs=[anywhere] * (3 + len(weights)),
        out_specs=[pl.BlockSpec(memory_space=pltpu.HBM)] * len(out_shape),
        scratch_shapes=[pltpu.VMEM((item[5], weights[item[1]].shape[1]), bf16) for item in items]
        + [
            dma((3, heads)), dma((3, heads)), dma, dma((heads,)), dma((3 + count,)),
            dma((count,)), dma((count,)), dma((count, 2)), dma((count, 2)), dma((count, 3, 3)), dma((count, 3, 3)),
        ],
        compiler_params=pltpu.CompilerParams(
            collective_id=collective_id, has_side_effects=True, vmem_limit_bytes=60 * 2**20),
        name="start_exchange",
    )(tokens, codes, taps, *weights)


def states_exchange(heads, count, per_block, backward, value, logs, out, scratch):
    packed, got, ready, send, recv, bsend, brecv = scratch
    me = lax.axis_index("seq") * heads + lax.axis_index("head")
    part = value.shape[0] // count
    tail = packed.shape[1] - part

    def peer(p):
        return {"seq": p // heads, "head": p % heads}

    def each(act):
        def one(d, carry):
            act((me + d) % count)
            return carry

        lax.fori_loop(1, count, one, 0)

    def greet():
        barrier = pltpu.get_barrier_semaphore()
        each(lambda p: pl.semaphore_signal(barrier, 1, device_id=peer(p), device_id_type=MESH))

    def pack():
        high = logs[...].astype(bf16)
        low = (logs[...] - high.astype(f32)).astype(bf16)

        def one(p, carry):
            packed[p, pl.ds(0, part)] = value[pl.ds(pl.multiple_of(p * part, part), part)]
            return carry

        lax.fori_loop(0, count, one, 0)
        parts_each = count * per_block // value.shape[0]
        zeros = jnp.zeros((tail - 2, high.shape[1]), bf16)
        for b in range(logs.shape[0]):
            both = jnp.concatenate([high[b : b + 1], low[b : b + 1], zeros], axis=0)
            for i in range(parts_each):
                packed[b * parts_each + i, pl.ds(part, tail)] = both
        got[me] = packed[me]

    def there(p, to):
        return pltpu.make_async_remote_copy(
            packed.at[p], got.at[to], send.at[p], recv.at[to], device_id=peer(p), device_id_type=MESH)

    def back(p, to):
        return pltpu.make_async_remote_copy(
            ready.at[p], out.at[pl.ds(pl.multiple_of(to * part, part), part)], bsend.at[p], brecv.at[to],
            device_id=peer(p), device_id_type=MESH)

    def begin():
        each(lambda p: there(p, me).start())

    def add_up():
        def step(i, state):
            p = count - 1 - i if backward else i

            @pl.when(p != me)
            def _():
                there(p, p).wait_recv()

            ready[p] = state.astype(bf16)

            @pl.when(p != me)
            def _():
                back(p, me).start()

            decay = jnp.exp(got[p, pl.ds(part, 1)].astype(f32) + got[p, pl.ds(part + 1, 1)].astype(f32))
            return decay * state + got[p, pl.ds(0, part)].astype(f32)

        lax.fori_loop(0, count, step, jnp.zeros((part, value.shape[1]), f32))
        out[pl.ds(pl.multiple_of(me * part, part), part)] = ready[me]

    def end():
        each(lambda p: back(p, p).wait_recv())
        each(lambda p: there(p, me).wait_send())
        each(lambda p: back(p, me).wait_send())

    return greet, pack, begin, add_up, end


def states_scratch(count, rows, width):
    part, tail = rows // count, 16
    dma = pltpu.SemaphoreType.DMA
    return [
        pltpu.VMEM((count, part + tail, width), bf16),
        pltpu.VMEM((count, part + tail, width), bf16),
        pltpu.VMEM((count, part, width), bf16),
        dma((count,)), dma((count,)), dma((count,)), dma((count,)),
    ]


def exchange_body(count, heads, per_block, items, n_more, *refs):
    value, logs = refs[:2]
    out = refs[2 + n_more]
    gathered = refs[3 + n_more : 3 + 2 * n_more]
    *scratch, gsend, grecv = refs[3 + 2 * n_more :]
    _, seq_copies = over_seq(items, gathered, gsend, grecv, lax.axis_index("seq"), lax.axis_index("head"))
    greet, pack, begin, add_up, end = states_exchange(heads, count, per_block, False, value, logs, out, scratch)
    greet()
    pack()
    pl.semaphore_wait(pltpu.get_barrier_semaphore(), count - 1)
    begin()
    for i in range(len(items)):
        for copy in seq_copies(i, 1):
            copy.start()
    add_up()
    for i in range(len(items)):
        for copy in seq_copies(i, 1):
            copy.wait_recv()
        for copy in seq_copies(i, 2):
            copy.start()
    end()
    for i in range(len(items)):
        for copy in seq_copies(i, 2):
            copy.wait()
        for copy in seq_copies(i, 1):
            copy.wait_send()


def exchange(value, logs, collective_id, items, gathered):
    heads = lax.axis_size("head")
    count = lax.axis_size("seq") * heads
    rows, width = value.shape
    more = len(gathered)
    dma = pltpu.SemaphoreType.DMA
    far, near = pl.BlockSpec(memory_space=pltpu.HBM), pl.BlockSpec(memory_space=pltpu.VMEM)
    return pl.pallas_call(
        partial(exchange_body, count, heads, rows // logs.shape[0], items, more),
        out_shape=[jax.ShapeDtypeStruct((rows, width), bf16)]
        + [jax.ShapeDtypeStruct(a.shape, a.dtype) for a in gathered],
        in_specs=[near] * 2 + [far] * more,
        out_specs=[near] + [far] * more,
        input_output_aliases={2 + i: 1 + i for i in range(more)},
        scratch_shapes=states_scratch(count, rows, width) + [dma((len(items), 3, 3)), dma((len(items), 3, 3))],
        compiler_params=pltpu.CompilerParams(
            collective_id=collective_id, has_side_effects=True, vmem_limit_bytes=60 * 2**20),
        name="exchange_states",
    )(value, logs, *gathered)


def aligned(x, size):
    return x if isinstance(x, int) else pl.multiple_of(x, size)


def sums_body(seq, plan, sources, shapes, n_given, n_left, n_right, leads, states, spread, more, groups, *refs):
    heads = 4
    nz = 1
    seq_masks = [1 << k for k in range(seq.bit_length() - 1)]
    split, joined = seq_masks[:3], seq_masks[3:]
    ns, nj = len(split), len(joined)
    refs = list(refs)

    def take(n):
        taken = refs[:n]
        del refs[:n]
        return taken

    value, logs = take(2) if states else (None, None)
    acts = take(len(leads))
    n_arrays, count = len(sources), len(plan)
    blocks = take(len(shapes) - n_arrays)
    orders = [c % 2 for c in range(count)] + [item[4] for item in more]
    plan = [*plan, *(item[:4] for item in more)]
    given, lefts, rights = take(n_given), take(n_left), take(n_right)
    (new_state,) = take(1) if states else (None,)
    acts_full = take(len(leads))
    halos = take(sum(map(bool, leads)))
    outs = take(len(shapes))
    per = ns + nj + nz
    owns = take(count)
    recvs = [take(per) for _ in range(count)]
    staged = {c: take(1)[0] for c in range(count) if not isinstance(sources[plan[c][0]], int)}
    state_scratch = take(7) if states else None
    (load_sem, send_sem, recv_sem, jsend, jrecv, zsend, zrecv, gsend, grecv, keep_sem, asend, arecv, stay, hsend,
     hrecv) = refs
    s, z = lax.axis_index("seq"), lax.axis_index("head")

    def peer(to_s, to_z):
        return {"seq": to_s, "head": to_z}

    def remote(src, dst, send, recv, to_s, to_z):
        return pltpu.make_async_remote_copy(src, dst, send, recv, device_id=peer(to_s, to_z), device_id_type=MESH)

    def to_features(a, first):
        act, full, lead = acts[a], acts_full[a], leads[a]
        mine, width = act.shape[1] - lead, full.shape[2]

        def features(q):
            return pl.ds(aligned(q * width, width), width)

        def rows_to(q):
            return pl.ds(aligned(q * mine, mine), mine)

        def back_copy(d, waits):
            q = (z + d) % heads
            to, of = (z, q) if waits else (q, z)
            return remote(
                act.at[:, pl.ds(lead, mine), features(to)], full.at[:, rows_to(of)], asend.at[a, q], arecv.at[a, of], s, q)

        def halo_copy(to_s, q, to, of):
            return remote(
                act.at[:, pl.ds(0, lead), features(to)], halos[0].at[of], hsend.at[q], hrecv.at[of], to_s, q)

        stay_copy = pltpu.make_async_copy(
            act.at[:, pl.ds(lead, mine), features(z)], full.at[:, rows_to(z)], stay.at[a])
        stay_copy.start() if first else stay_copy.wait()
        for d in range(1, heads):
            back_copy(d, False).start() if first else back_copy(d, False).wait_send()
            if not first:
                back_copy(d, True).wait_recv()
        if not lead:
            return

        @pl.when(z != 0)
        def _():
            halo_own = pltpu.make_async_copy(act.at[:, pl.ds(0, lead), features(z)], halos[0].at[z], stay.at[len(acts)])
            halo_own.start() if first else halo_own.wait()
            for d in range(1, heads):
                q = (z + d) % heads
                halo_copy(s, q, q, z).start() if first else halo_copy(s, q, q, z).wait_send()

        @pl.when((z == 0) & (s > 0))
        def _():
            for q in range(heads):
                halo_copy(s - 1, q, q, 0).start() if first else halo_copy(s - 1, q, q, 0).wait_send()

        if not first:
            for d in range(1, heads):
                q = (z + d) % heads

                @pl.when(q != 0)
                def _():
                    halo_copy(s, q, z, q).wait_recv()

            @pl.when(s < seq - 1)
            def _():
                halo_copy(s + 1, 0, z, 0).wait_recv()

    def masks(c):
        return split[:1] + (split[1:] if orders[c] == 0 else split[:0:-1])

    def bit(c, k):
        return s // masks(c)[k] % 2

    def extent(c):
        array, axis, first, size = plan[c]
        return size if axis == 0 else shapes[array][1]

    def kept(c, k):
        size = extent(c)
        return sum((bit(c, j) * (size >> (j + 1)) for j in range(1, k + 1)), 0)

    def cut(c, begin, size):
        part = pl.ds(aligned(begin, size), size)
        return (part, slice(None)) if plan[c][1] == 0 else (slice(None), part)

    def in_array(c, begin, size):
        _, axis, first, rows = plan[c]
        if axis == 0:
            return pl.ds(aligned(first + begin, size), size), slice(None)
        return pl.ds(first, rows), pl.ds(aligned(begin, size), size)

    def load(c):
        half = extent(c) // 2
        rows, columns = in_array(c, bit(c, 0) * half, half)
        return pltpu.make_async_copy(given[sources[plan[c][0]]].at[:, rows, columns], owns[c], load_sem.at[c])

    def product(c):
        left_at, right_at, natural = sources[plan[c][0]]
        left, right = lefts[left_at], rights[right_at]
        half = extent(c) // 2

        def one(q, carry):
            for to, b in ((staged[c], 1 - bit(c, 0)), (owns[c], bit(c, 0))):
                rows, columns = in_array(c, b * half, half)
                total = None
                for i in range(left.shape[1]):
                    b_ = right[q if right.shape[0] > 1 else 0, i, :, columns]
                    if natural:
                        term = dot_tn(left[q if left.shape[0] > 1 else 0, i, :, rows], b_)
                    else:
                        term = dot_nn(left[q if left.shape[0] > 1 else 0, i, rows, :], b_)
                    total = term if total is None else total + term
                to[q] = total.astype(bf16)
            return carry

        lax.fori_loop(0, heads, one, 0)

    def seq_copy(c, k):
        half = extent(c) >> (k + 1)
        other = (1 - bit(c, k)) * half
        if k == 0 and c in staged:
            source = staged[c]
        elif k == 0:
            rows, columns = in_array(c, other, half)
            source = given[sources[plan[c][0]]].at[:, rows, columns]
        else:
            rows, columns = cut(c, kept(c, k - 1) + other, half)
            source = owns[c].at[:, rows, columns]
        return remote(source, recvs[c][k], send_sem.at[c, k], recv_sem.at[c, k], flipped(s, masks(c)[k]), z)

    def final(c):
        return cut(c, kept(c, ns - 1), extent(c) >> ns)

    def joined_copy(c, k):
        rows, columns = final(c)
        return remote(
            owns[c].at[:, rows, columns], recvs[c][ns + k], jsend.at[c, k], jrecv.at[c, k], flipped(s, joined[k]), z)

    def head_copy(c, d, waits):
        rows, columns = final(c)
        q = (z + d) % heads
        to, of = (z, q) if waits else (q, z)
        return remote(
            owns[c].at[to, rows, columns], recvs[c][ns + nj].at[of], zsend.at[c, q], zrecv.at[c, of], s, q)

    def add(c, k):
        axis, rows = plan[c][1], plan[c][3]
        if k < ns:
            begin, size = kept(c, k), extent(c) >> (k + 1)
        else:
            begin, size = kept(c, ns - 1), extent(c) >> ns
        received = recvs[c][k]
        tall = size if axis == 0 else rows
        wide = shapes[plan[c][0]][1] if axis == 0 else size
        tile = tall
        while tile * wide > 98304 and tile % 32 == 0:
            tile //= 2
        tiles = tall // tile

        def places(r):
            there = pl.ds(pl.multiple_of(r, tile), tile)
            if axis == 0:
                return there, pl.ds(pl.multiple_of(begin + r, tile), tile), slice(None)
            return there, there, pl.ds(aligned(begin, size), size)

        def one(t, carry):
            i = t // tiles
            there, here, columns = places(t % tiles * tile)
            owns[c][i, here, columns] = owns[c][i, here, columns] + received[i, there]
            return carry

        def last_one(t, carry):
            there, here, columns = places(t * tile)
            total = owns[c][z, here, columns].astype(f32)
            for d in range(1, heads):
                total = total + received[(z + d) % heads, there].astype(f32)
            owns[c][z, here, columns] = total.astype(bf16)
            return carry

        if k < ns + nj:
            lax.fori_loop(0, heads * tiles, one, 0)
        else:
            lax.fori_loop(0, tiles, last_one, 0)

    def held(c, level):
        size = extent(c)
        return in_array(c, sum(bit(c, j) * (size >> (j + 1)) for j in range(level)), size >> level)

    def own_block(c):
        if c >= count:
            return blocks[plan[c][0] - n_arrays].at[pl.ds(plan[c][2], plan[c][3])]
        return owns[c].at[z, *final(c)]

    def keep(c):
        rows, columns = held(c, ns)
        if not spread:
            columns = slice(None)
        return pltpu.make_async_copy(own_block(c), outs[plan[c][0]].at[rows, columns], keep_sem.at[c])

    def gather_copy(c, j):
        level = ns - j
        rows, columns = held(c, level)
        array = outs[plan[c][0]].at[rows, columns]
        source = own_block(c) if j == 0 else array
        return remote(source, array, gsend.at[c, j], grecv.at[c, j], flipped(s, masks(c)[level - 1]), z)

    barrier = pltpu.get_barrier_semaphore()
    if states:
        everyone = seq * heads
        greet, pack, begin, add_up, end = states_exchange(
            heads, everyone, value.shape[0] // logs.shape[0], True, value, logs, new_state, state_scratch)
        greet()
        pack()
        pl.semaphore_wait(barrier, everyone - 1)
        begin()
    else:

        def greet(to_s, to_z):
            pl.semaphore_signal(barrier, 1, device_id=peer(to_s, to_z), device_id_type=MESH)

        for mask in seq_masks:
            greet(flipped(s, mask), z)
        for d in range(1, heads):
            greet(s, (z + d) % heads)
        greeted = len(seq_masks) + heads - 1

        @pl.when(s < seq - 1)
        def _():
            greet(s + 1, 0)

        @pl.when((z == 0) & (s > 0))
        def _():
            pl.semaphore_wait(barrier, greeted + heads)

        @pl.when((z != 0) | (s == 0))
        def _():
            pl.semaphore_wait(barrier, greeted)

    last = per + (ns if spread else 1)

    def copies(c, k, waits=False):
        if k < ns:
            return [seq_copy(c, k)]
        if k < ns + nj:
            return [joined_copy(c, k - ns)]
        if k < per:
            return [head_copy(c, d, waits) for d in range(1, heads)]
        return [gather_copy(c, k - per)] if spread else []

    def advance(c, k):
        if k == 0 and c not in staged:
            load(c).wait()
        if k == per:
            keep(c).wait()
        for copy in copies(c, k, True):
            copy.wait_recv()
        if ns <= k < ns + nj:
            joined_copy(c, k - ns).wait_send()
        if k < per:
            add(c, k)
        if k + 1 == per:
            keep(c).start()
        if k + 1 < last and c < count:
            for copy in copies(c, k + 1):
                copy.start()

    def begin_chunk(c):
        if c in staged:
            product(c)
        else:
            load(c).start()
        seq_copy(c, 0).start()

    for t in range(len(groups) + last):
        for k in range(last):
            if 0 <= t - 1 - k < len(groups):
                for c in groups[t - 1 - k]:
                    advance(c, k)
        if t < len(groups):
            for c in groups[t]:
                begin_chunk(c)
        for c in range(count, len(plan)):
            if t == 0:
                keep(c).start()
            elif t <= ns:
                advance(c, per + t - 1)
            if t < ns:
                gather_copy(c, t).start()
        if t == 0:
            for a in range(len(acts)):
                to_features(a, True)
        if t == 1 and states:
            add_up()
    for a in range(len(acts)):
        to_features(a, False)
    for c in range(count):
        for k in range(last):
            if not ns <= k < ns + nj:
                for copy in copies(c, k):
                    copy.wait_send()
    for c in range(count, len(plan)):
        for j in range(ns):
            gather_copy(c, j).wait_send()
    if states:
        end()


def sums(acts, leads, plan, sources, shapes, given, lefts, rights, collective_id, states=(), spread=True, blocks=(), more=(), groups=None):
    groups = groups or [(c, c + 1) for c in range(0, len(plan), 2)]
    seq, heads = lax.axis_size("seq"), lax.axis_size("head")
    nj = max(0, seq.bit_length() - 4)
    ns = 3
    owns, recvs, staged = [], [], []
    for a, axis, first, rows in plan:
        columns = shapes[a][1]
        cut = lambda k: (rows >> k, columns) if axis == 0 else (rows, columns >> k)
        owns.append(pltpu.VMEM((heads, *cut(1)), bf16))
        recvs += [pltpu.VMEM((heads, *cut(k + 1)), bf16) for k in range(ns)]
        recvs += [pltpu.VMEM((heads, *cut(ns)), bf16) for k in range(nj)]
        recvs.append(pltpu.VMEM((heads, *cut(ns)), bf16))
        if not isinstance(sources[a], int):
            staged.append(pltpu.VMEM((heads, *cut(1)), bf16))
    count, every = len(plan), len(plan) + len(more)
    dma = pltpu.SemaphoreType.DMA
    sems = [
        dma((count,)), dma((count, ns)), dma((count, ns)), dma((count, max(nj, 1))), dma((count, max(nj, 1))),
        dma((count, heads)), dma((count, heads)), dma((every, ns)), dma((every, ns)), dma((every,)),
        dma((2, heads)), dma((2, heads)), dma((3,)), dma((heads,)), dma((heads,)),
    ]
    anywhere, near = pl.BlockSpec(memory_space=pl.ANY), pl.BlockSpec(memory_space=pltpu.VMEM)
    out_shape, halo_shape = [], []
    for act, lead in zip(acts, leads):
        seqs, rows_here, features = act.shape
        width = features // heads
        out_shape.append(jax.ShapeDtypeStruct((seqs, heads * (rows_here - lead), width), bf16))
        if lead:
            halo_shape.append(jax.ShapeDtypeStruct((heads, seqs, lead, width), bf16))
    out_shape += halo_shape
    if not spread:
        shapes_out = [(rows, columns >> ns) for rows, columns in shapes]
    out_shape += [jax.ShapeDtypeStruct(shape, bf16) for shape in (shapes if spread else shapes_out)]
    out_specs = [anywhere] * len(out_shape)
    state_scratch = []
    if states:
        out_shape.insert(0, jax.ShapeDtypeStruct(states[0].shape, bf16))
        out_specs.insert(0, near)
        state_scratch = states_scratch(seq * heads, *states[0].shape)
    return pl.pallas_call(
        partial(sums_body, seq, plan, sources, shapes, len(given), len(lefts), len(rights), leads, bool(states), spread, more, groups),
        out_shape=out_shape,
        in_specs=[near] * len(states)
        + [anywhere] * len(acts)
        + [near] * len(blocks)
        + [anywhere] * len(given)
        + [near] * (len(lefts) + len(rights)),
        out_specs=out_specs,
        scratch_shapes=owns + recvs + staged + state_scratch + sems,
        compiler_params=pltpu.CompilerParams(
            collective_id=collective_id, has_side_effects=True, vmem_limit_bytes=60 * 2**20),
        name="sum_gradients",
    )(*states, *acts, *blocks, *given, *lefts, *rights)


def dot_nt(a, b):
    return lax.dot_general(a, b, (((1,), (1,)), ((), ())), preferred_element_type=f32)


def dot_tn(a, b):
    return lax.dot_general(a, b, (((0,), (0,)), ((), ())), preferred_element_type=f32)


def mlp_body(per_head, hid, gain, cot, w_gate, w_up, w_low, lay, d_hid, normed, hidden, d_gate, d_up, d_gain, acc, part, dx):
    step = pl.program_id(0)

    @pl.when(step == 0)
    def _():
        values = hid[...]
        normed[...] = (values * row_scale(values) * gain[...]).astype(bf16)
        acc[...] = values
        dx[...] = jnp.zeros_like(dx)

    g = dot_nt(w_gate[0], normed[...])
    u = dot_nt(w_up[0], normed[...])
    dh = rounded(dot_nt(w_low[0], cot[...]))
    logistic = jax.nn.sigmoid(g)
    act = g * logistic
    h = (act * u).astype(bf16)
    dg = (dh * u * (logistic * (1.0 + g * (1.0 - logistic)))).astype(bf16)
    du = (dh * act).astype(bf16)
    hidden[0] = h
    d_gate[0] = dg
    d_up[0] = du
    term = dot_tn(h, w_low[0])
    first = step % per_head == 0

    @pl.when(first)
    def _():
        part[...] = term

    @pl.when(jnp.logical_not(first))
    def _():
        part[...] += term

    @pl.when(step % per_head == per_head - 1)
    def _():
        acc[...] += rounded(part[...])

    dx[...] += dot_tn(dg, w_gate[0]) + dot_tn(du, w_up[0])

    @pl.when(step == pl.num_programs(0) - 1)
    def _():
        lay[...] = acc[...].astype(bf16)
        values, upstream = hid[...], dx[...]
        scale = row_scale(values)
        d_gain[...] = jnp.sum(upstream * values * scale, axis=0, keepdims=True)
        d_hid[...] = cot[...].astype(f32) + norm_back(values, scale, gain[...], upstream)


def mlp(hidden_in, gain, upstream, w_gate, w_up, w_low):
    tokens, width = hidden_in.shape
    heads, units, _ = w_gate.shape
    per_head = 1
    block = units // per_head
    weights = pl.BlockSpec((1, block, width), lambda i: (i // per_head, i % per_head, 0))
    units_out = pl.BlockSpec((1, block, tokens), lambda i: (i // per_head, i % per_head, 0))
    all_of = lambda *shape: pl.BlockSpec(shape, lambda i: (0, 0))
    units_shape = jax.ShapeDtypeStruct((heads, units, tokens), bf16)
    token_shape = lambda kind: jax.ShapeDtypeStruct((tokens, width), kind)
    return pl.pallas_call(
        partial(mlp_body, per_head),
        grid=(heads * per_head,),
        in_specs=[all_of(tokens, width), all_of(1, width), all_of(tokens, width), weights, weights, weights],
        out_specs=[all_of(tokens, width)] * 3 + [units_out] * 3 + [all_of(1, width)],
        out_shape=[token_shape(bf16), token_shape(f32), token_shape(bf16)]
        + [units_shape] * 3
        + [jax.ShapeDtypeStruct((1, width), f32)],
        scratch_shapes=[pltpu.VMEM((tokens, width), f32)] * 3,
        compiler_params=pltpu.CompilerParams(vmem_limit_bytes=60 * 2**20),
        name="feed_forward",
    )(hidden_in, gain.reshape(1, width), upstream, w_gate, w_up, w_low)


def rows_after(values, count):
    if count == 0:
        return values
    return jnp.concatenate([values[count:], jnp.zeros((count, values.shape[1]), values.dtype)], axis=0)


def short_conv(pre, taps, rows):
    lead = HALO - taps.shape[0] + 1
    return sum(taps[j : j + 1] * pre[lead + j : lead + j + rows] for j in range(taps.shape[0]))


def spans(values):
    return [values[n * SPAN : (n + 1) * SPAN] for n in range(values.shape[0] // SPAN)]


def lower(count):
    row = lax.broadcasted_iota(jnp.int32, (count, count), 0)
    column = lax.broadcasted_iota(jnp.int32, (count, count), 1)
    return row, column


def causal_scores(left, right):
    row, column = lower(SPAN)
    return jnp.where(row >= column, dot_nt(left, right), 0.0).astype(bf16)


def dot_nn(a, b):
    return jnp.dot(a, b, preferred_element_type=f32)


def without_first(values, first):
    row = lax.broadcasted_iota(jnp.int32, values.shape, 0)
    return jnp.where((row < HALO) & (first > 0), 0.0, values.astype(f32))


def forward_one_body(first, tokens, gain, w, taps, codes, normed, pre, q_exp, k_exp, k_end, value, decay, starts, ends, logs, kept):
    h, i = pl.program_id(0), pl.program_id(1)

    @pl.when(h == 0)
    def _():
        values = without_first(tokens[0], first[0])
        kept[i] = (values * row_scale(values) * gain[...]).astype(bf16)

    normed[0] = kept[i]
    projected = dot_nn(kept[i], w[0]).astype(bf16)
    pre[0, 0] = projected
    rows = codes.shape[1]
    key = codes.shape[2]
    wide = taps.shape[2]
    act = jax.nn.silu(short_conv(projected[:, :wide].astype(f32), taps[0], rows))
    whole_codes = codes[0].astype(jnp.int32)
    high = whole_codes // 128
    row, column = lower(rows)
    within = ((row >= column) & (row // SPAN == column // SPAN)).astype(bf16)
    total = 128.0 * dot_nn(within, high.astype(bf16)) + dot_nn(within, (whole_codes - 128 * high).astype(bf16))
    log = total * -decay_unit
    decay[0, 0] = log
    grow = jnp.exp(log)
    q_exp[0, 0] = (act[:, :key] * key**-0.5 * grow).astype(bf16)
    k_exp[0, 0] = (act[:, key : 2 * key] * jnp.exp(-log)).astype(bf16)
    value[0, 0] = act[:, 2 * key :].astype(bf16)
    state = jnp.zeros((wide - 2 * key, key), f32)
    sums_log = jnp.zeros((1, key), f32)
    for n, part in enumerate(spans(log)):
        at = pl.ds(n * SPAN, SPAN)
        last = part[SPAN - 1 :]
        k_end[0, 0, at] = (act[n * SPAN : (n + 1) * SPAN, key : 2 * key] * jnp.exp(last - part)).astype(bf16)
        starts[0, 0, n] = state.astype(bf16)
        state = jnp.exp(last) * state + dot_tn(value[0, 0, at], k_end[0, 0, at])
        sums_log = sums_log + last
    ends[0, 0] = state.astype(bf16)
    logs[0, 0] = sums_log


def forward_one(first, tokens, gain, w, taps, codes):
    heads, width, columns = w.shape
    seqs, tall, _ = tokens.shape
    rows = tall - HALO
    tap_count, wide = taps.shape[1:]
    key = codes.shape[2] // heads
    wide_value = wide - 2 * key
    blocks = rows // SPAN
    per = lambda *shape: pl.BlockSpec((1, 1, *shape), lambda h, i: (h, i) + (0,) * len(shape))
    shape = lambda kind, *rest: jax.ShapeDtypeStruct((heads, seqs, *rest), kind)
    return pl.pallas_call(
        forward_one_body,
        grid=(heads, seqs),
        in_specs=[
            pl.BlockSpec(memory_space=pltpu.SMEM),
            pl.BlockSpec((1, tall, width), lambda h, i: (i, 0, 0)),
            pl.BlockSpec((1, width), lambda h, i: (0, 0)),
            pl.BlockSpec((1, width, columns), lambda h, i: (h, 0, 0)),
            pl.BlockSpec((1, tap_count, wide), lambda h, i: (h, 0, 0)),
            pl.BlockSpec((1, rows, key), lambda h, i: (i, 0, h)),
        ],
        out_specs=[
            pl.BlockSpec((1, tall, width), lambda h, i: (i, 0, 0)),
            per(tall, columns), per(rows, key), per(rows, key), per(rows, key), per(rows, wide_value), per(rows, key),
            per(blocks, wide_value, key), per(wide_value, key), per(1, key),
        ],
        out_shape=[
            jax.ShapeDtypeStruct((seqs, tall, width), bf16),
            shape(bf16, tall, columns), shape(bf16, rows, key), shape(bf16, rows, key), shape(bf16, rows, key),
            shape(bf16, rows, wide_value), shape(f32, rows, key), shape(bf16, blocks, wide_value, key),
            shape(bf16, wide_value, key), shape(f32, 1, key),
        ],
        scratch_shapes=[pltpu.VMEM((seqs, tall, width), bf16)],
        compiler_params=pltpu.CompilerParams(vmem_limit_bytes=60 * 2**20),
        name="attention_spans",
    )(first, tokens, gain.reshape(1, -1), w, taps, codes)


def forward_two_body(first, tokens, pre, q_exp, k_exp, value, decay, starts, incoming, out_gain, w_out, core, states, gated, hidden_in):
    h = pl.program_id(1)
    wide_value = value.shape[3]
    carry = jnp.ones((1, q_exp.shape[3]), f32)
    entering = incoming[0, 0].astype(f32)
    parts = []
    for n in range(starts.shape[2]):
        at = pl.ds(n * SPAN, SPAN)
        state = (starts[0, 0, n].astype(f32) + carry * entering).astype(bf16)
        states[0, 0, n] = state
        q = q_exp[0, 0, at]
        scores = causal_scores(q, k_exp[0, 0, at])
        parts.append(dot_nn(scores, value[0, 0, at]) + dot_nt(q, state))
        carry = carry * jnp.exp(decay[0, 0, pl.ds((n + 1) * SPAN - 1, 1)])
    out = jnp.concatenate(parts, axis=0)
    core[0, 0] = out
    gate = pre[0, 0, pl.ds(HALO, out.shape[0]), pl.ds(pre.shape[3] - wide_value, wide_value)].astype(f32)
    gated[0, 0] = (out * row_scale(out) * out_gain[...] * jax.nn.silu(gate)).astype(bf16)
    term = rounded(dot_nn(gated[0, 0], w_out[0]))

    @pl.when(h == 0)
    def _():
        hidden_in[0] = without_first(tokens[0], first[0])[HALO:] + term

    @pl.when(h > 0)
    def _():
        hidden_in[0] += term


def head_spec(*shape):
    return pl.BlockSpec((1, 1, *shape), lambda i, h: (h, i) + (0,) * len(shape))


def forward_two(first, tokens, pre, q_exp, k_exp, value, decay, starts, incoming, out_gain, w_out):
    heads, seqs, rows, key = q_exp.shape
    wide_value, width = w_out.shape[1:]
    blocks = rows // SPAN
    tall = rows + HALO
    per = head_spec
    shape = lambda kind, *rest: jax.ShapeDtypeStruct((heads, seqs, *rest), kind)
    return pl.pallas_call(
        forward_two_body,
        grid=(seqs, heads),
        in_specs=[
            pl.BlockSpec(memory_space=pltpu.SMEM),
            pl.BlockSpec((1, tall, width), lambda i, h: (i, 0, 0)),
            per(tall, pre.shape[3]), per(rows, key), per(rows, key), per(rows, wide_value), per(rows, key),
            per(blocks, wide_value, key), per(wide_value, key),
            pl.BlockSpec((1, wide_value), lambda i, h: (0, 0)),
            pl.BlockSpec((1, wide_value, width), lambda i, h: (h, 0, 0)),
        ],
        out_specs=[
            per(rows, wide_value), per(blocks, wide_value, key), per(rows, wide_value),
            pl.BlockSpec((1, rows, width), lambda i, h: (i, 0, 0)),
        ],
        out_shape=[
            shape(f32, rows, wide_value), shape(bf16, blocks, wide_value, key), shape(bf16, rows, wide_value),
            jax.ShapeDtypeStruct((seqs, rows, width), f32),
        ],
        compiler_params=pltpu.CompilerParams(vmem_limit_bytes=60 * 2**20),
        name="attention_outputs",
    )(first, tokens, pre, q_exp, k_exp, value, decay, starts, incoming, out_gain.reshape(1, -1), w_out)


def backward_one_body(d_hidden_in, w_out, core, pre, out_gain, q_exp, decay, d_mixer, d_core, d_gate, d_states, own_grad, d_gain):
    i, h = pl.program_id(0), pl.program_id(1)
    wide_value = core.shape[3]

    @pl.when(h == 0)
    def _():
        d_mixer[0] = d_hidden_in[0].astype(bf16)

    d_gated = rounded(dot_nt(d_mixer[0], w_out[0]))
    out = core[0, 0]
    gate = pre[0, 0, pl.ds(HALO, out.shape[0]), pl.ds(pre.shape[3] - wide_value, wide_value)].astype(f32)
    scale = row_scale(out)
    normed = out * scale
    d_normed = d_gated * jax.nn.silu(gate)
    d_gate[0, 0] = (d_gated * normed * out_gain[...] * silu_slope(gate)).astype(bf16)
    gain_term = jnp.sum(d_normed * normed, axis=0, keepdims=True)

    @pl.when((i == 0) & (h == 0))
    def _():
        d_gain[...] = gain_term

    @pl.when((i > 0) | (h > 0))
    def _():
        d_gain[...] += gain_term

    d_core[0, 0] = norm_back(out, scale, out_gain[...], d_normed).astype(bf16)
    carry = jnp.ones((1, q_exp.shape[3]), f32)
    total = jnp.zeros((wide_value, q_exp.shape[3]), f32)
    for n in range(out.shape[0] // SPAN):
        at = pl.ds(n * SPAN, SPAN)
        term = dot_tn(d_core[0, 0, at], q_exp[0, 0, at])
        d_states[0, 0, n] = term.astype(bf16)
        total = total + carry * term
        carry = carry * jnp.exp(decay[0, 0, pl.ds((n + 1) * SPAN - 1, 1)])
    own_grad[0, 0] = total.astype(bf16)


def backward_one(d_hidden_in, w_out, core, pre, out_gain, q_exp, decay):
    heads, seqs, rows, key = q_exp.shape
    wide_value, width = w_out.shape[1:]
    blocks = rows // SPAN
    per = head_spec
    shape = lambda kind, *rest: jax.ShapeDtypeStruct((heads, seqs, *rest), kind)
    by_seq = pl.BlockSpec((1, rows, width), lambda i, h: (i, 0, 0))
    gain = pl.BlockSpec((1, wide_value), lambda i, h: (0, 0))
    return pl.pallas_call(
        backward_one_body,
        grid=(seqs, heads),
        in_specs=[
            by_seq, pl.BlockSpec((1, wide_value, width), lambda i, h: (h, 0, 0)), per(rows, wide_value),
            per(rows + HALO, pre.shape[3]), gain, per(rows, key), per(rows, key),
        ],
        out_specs=[
            by_seq, per(rows, wide_value), per(rows, wide_value), per(blocks, wide_value, key), per(wide_value, key),
            gain,
        ],
        out_shape=[
            jax.ShapeDtypeStruct((seqs, rows, width), bf16), shape(bf16, rows, wide_value),
            shape(bf16, rows, wide_value), shape(bf16, blocks, wide_value, key), shape(bf16, wide_value, key),
            jax.ShapeDtypeStruct((1, wide_value), f32),
        ],
        compiler_params=pltpu.CompilerParams(vmem_limit_bytes=60 * 2**20),
        name="attention_outputs_back",
    )(d_hidden_in, w_out, core, pre, out_gain.reshape(1, -1), q_exp, decay)


def backward_two_body(
    first, tokens, gain, d_hidden_in, w, taps, pre, q_exp, k_exp, k_end, value, decay, states, d_core, d_states, leaving,
    d_gate, d_projected, d_tokens, d_taps, d_gain, d_normed,
):
    i, h = pl.program_id(0), pl.program_id(1)
    key, wide_value = q_exp.shape[3], value.shape[3]
    rows = q_exp.shape[2]
    blocks = rows // SPAN
    scale = key**-0.5
    d_end = leaving[0, 0].astype(f32)
    pieces = [None] * blocks
    for n in reversed(range(blocks)):
        at = pl.ds(n * SPAN, SPAN)
        q, k, v, dc = q_exp[0, 0, at], k_exp[0, 0, at], value[0, 0, at], d_core[0, 0, at]
        log = decay[0, 0, at]
        last = log[SPAN - 1 :]
        d_end_low = d_end.astype(bf16)
        scores = causal_scores(q, k)
        d_scores = causal_scores(dc, v)
        d_query = (dot_nn(d_scores, k) + dot_nn(dc, states[0, 0, n])) * (scale * jnp.exp(log))
        d_key = dot_tn(d_scores, q) * jnp.exp(-log) + dot_nn(v, d_end_low) * jnp.exp(last - log)
        d_value = dot_tn(scores, dc) + dot_nt(k_end[0, 0, at], d_end_low)
        pieces[n] = jnp.concatenate([d_query, d_key, d_value], axis=1)
        d_end = jnp.exp(last) * d_end + d_states[0, 0, n].astype(f32)
    d_act = jnp.concatenate(pieces, axis=0)
    tap_count, wide = taps.shape[1:]
    ext = pre[0, 0, :, pl.ds(0, wide)].astype(f32)
    d_conv = d_act * silu_slope(short_conv(ext, taps[0], rows))
    lead = HALO - tap_count + 1
    padded = jnp.concatenate([jnp.zeros((HALO, wide), f32), d_conv], axis=0)
    d_ext = jnp.zeros((HALO + rows, wide), f32)
    tap_terms = []
    for j in range(tap_count):
        moved = rows_after(padded, tap_count - 1 - j)
        d_ext = d_ext + taps[0, pl.ds(j, 1)] * moved
        tap_terms.append(jnp.sum(moved * ext, axis=0, keepdims=True))
    tap_terms = jnp.concatenate(tap_terms, axis=0)

    @pl.when(i == 0)
    def _():
        d_taps[h] = tap_terms

    @pl.when(i > 0)
    def _():
        d_taps[h] += tap_terms

    d_gate_ext = jnp.concatenate([jnp.zeros((HALO, wide_value), bf16), d_gate[0, 0]], axis=0)
    d_projected[0, 0] = jnp.concatenate([d_ext.astype(bf16), d_gate_ext], axis=1)
    term = dot_nt(d_projected[0, 0], w[0])

    @pl.when(h == 0)
    def _():
        d_normed[...] = term

    @pl.when(h > 0)
    def _():
        d_normed[...] += term

    @pl.when(h == pl.num_programs(1) - 1)
    def _():
        values, upstream = without_first(tokens[0], first[0]), d_normed[...]
        inverse = row_scale(values)
        gain_term = jnp.sum(upstream * values * inverse, axis=0, keepdims=True)
        d_gain[0] = gain_term
        back = norm_back(values, inverse, gain[...], upstream)
        d_tokens[0, pl.ds(0, HALO)] = back[:HALO].astype(bf16)
        d_tokens[0, pl.ds(HALO, rows)] = (back[HALO:] + d_hidden_in[0]).astype(bf16)


def backward_two(
    first, tokens, gain, d_hidden_in, w, taps, pre, q_exp, k_exp, k_end, value, decay, states, d_core, d_states, leaving, d_gate
):
    heads, seqs, rows, key = q_exp.shape
    width, columns = w.shape[1:]
    wide_value = value.shape[3]
    tap_count, wide = taps.shape[1:]
    blocks = rows // SPAN
    tall = rows + HALO
    per = head_spec
    by_seq = lambda n: pl.BlockSpec((1, n, width), lambda i, h: (i, 0, 0))
    return pl.pallas_call(
        backward_two_body,
        grid=(seqs, heads),
        in_specs=[
            pl.BlockSpec(memory_space=pltpu.SMEM), by_seq(tall), pl.BlockSpec((1, width), lambda i, h: (0, 0)),
            by_seq(rows), pl.BlockSpec((1, width, columns), lambda i, h: (h, 0, 0)),
            pl.BlockSpec((1, tap_count, wide), lambda i, h: (h, 0, 0)),
            per(tall, columns), per(rows, key), per(rows, key), per(rows, key), per(rows, wide_value), per(rows, key),
            per(blocks, wide_value, key), per(rows, wide_value), per(blocks, wide_value, key), per(wide_value, key),
            per(rows, wide_value),
        ],
        out_specs=[
            per(tall, columns), by_seq(tall), pl.BlockSpec((heads, tap_count, wide), lambda i, h: (0, 0, 0)), by_seq(1),
        ],
        out_shape=[
            jax.ShapeDtypeStruct((heads, seqs, tall, columns), bf16),
            jax.ShapeDtypeStruct((seqs, tall, width), bf16),
            jax.ShapeDtypeStruct((heads, tap_count, wide), f32),
            jax.ShapeDtypeStruct((seqs, 1, width), f32),
        ],
        scratch_shapes=[pltpu.VMEM((tall, width), f32)],
        compiler_params=pltpu.CompilerParams(vmem_limit_bytes=60 * 2**20),
        name="attention_spans_back",
    )(
        first, tokens, gain.reshape(1, -1), d_hidden_in, w, taps, pre, q_exp, k_exp, k_end, value, decay, states, d_core,
        d_states, leaving, d_gate,
    )


def finalize_body(key, value, last, lay, tok, halo, mixer, out, gate, up, down, small, *outs):
    step = pl.program_id(0)
    o_lay, o_tok, o_query, o_key, o_value, o_gate_proj, o_out, o_gate, o_up, o_down, o_small = outs
    o_lay[...] = lay[...].astype(f32)
    o_tok[...] = tok[...].astype(f32)
    steps = pl.num_programs(0)

    @pl.when((step % 2 == 1) & ((step < steps - 1) | (last[0] == 0)))
    def _():
        at = pl.ds(tok.shape[1] - HALO, HALO)
        o_tok[:, at] += halo[0].astype(f32)

    begin = 0
    for ref, wide in ((o_query, key), (o_key, key), (o_value, value), (o_gate_proj, value)):
        ref[...] = mixer[:, pl.ds(begin, wide)].astype(f32)
        begin += wide
    for to, of in ((o_out, out), (o_gate, gate), (o_up, up), (o_down, down)):
        to[...] = of[...].astype(f32)

    @pl.when(step == 0)
    def _():
        o_small[...] = small[...].astype(f32)


def finalize(last, lay, tok, halos, mixer, out, gate, up, down, small, key, value):
    heads, seqs, _, width = halos.shape
    steps = 2 * heads
    rows = lay.shape[1] // steps
    acts = pl.BlockSpec((seqs, rows, width), lambda i: (0, i, 0))

    def by_rows(array, columns=None):
        return pl.BlockSpec((array.shape[0] // steps, columns or array.shape[1]), lambda i: (i, 0))

    whole_small = pl.BlockSpec(small.shape, lambda i: (0, 0))
    full = lambda *shape: jax.ShapeDtypeStruct(shape, f32)
    tall = mixer.shape[0]
    grads = (out, gate, up, down)
    return pl.pallas_call(
        partial(finalize_body, key, value),
        grid=(steps,),
        in_specs=[
            pl.BlockSpec(memory_space=pltpu.SMEM), acts, acts,
            pl.BlockSpec((1, seqs, HALO, width), lambda i: ((i + 1) // 2 % heads, 0, 0, 0)),
            by_rows(mixer), *map(by_rows, grads), whole_small,
        ],
        out_specs=[acts, acts] + [by_rows(mixer, n) for n in (key, key, value, value)] + [*map(by_rows, grads), whole_small],
        out_shape=[full(*lay.shape), full(*tok.shape)]
        + [full(tall, n) for n in (key, key, value, value)]
        + [full(*a.shape) for a in grads]
        + [full(*small.shape)],
        compiler_params=pltpu.CompilerParams(vmem_limit_bytes=60 * 2**20),
        name="outputs",
    )(last, lay, tok, halos, mixer, out, gate, up, down, small)


def chunks(array, rows, count):
    return [(array, 0, i * (rows // count), rows // count) for i in range(count)]


def local(
    tokens,
    decay_codes,
    cotangent,
    attn_gain,
    w_query,
    w_key,
    w_value,
    w_out_gate,
    conv_query,
    conv_key,
    conv_value,
    out_gain,
    w_out,
    mlp_gain,
    w_gate,
    w_up,
    w_down,
):
    seqs, rows, own_width = tokens.shape
    heads = lax.axis_size("head")
    place = lax.axis_index("seq") * heads + lax.axis_index("head")
    mine = rows // heads
    width = own_width * heads
    key_width = w_query.shape[1]
    value_width = w_value.shape[1]
    conv_width = 2 * key_width + value_width
    mixer_width = conv_width + value_width

    half, ff = width // 2, w_gate.shape[1]
    out_half, ff_half = w_out.shape[0] // 2, ff // 2
    items = [(0, 0, 0, 0, 0, width, 0, key_width), (1, 1, 0, 0, 0, width, key_width, key_width)]
    items += [(i, 2, 0, 0, i * half, half, 2 * key_width, value_width) for i in range(2)]
    items += [(i, 3, 0, 0, i * half, half, conv_width, value_width) for i in range(2)]
    items += [(i, 4, 1, 0, i * out_half, out_half, 0, width) for i in range(2)]
    pair = [(2 + 2 * a + i, 5 + a, 2 + a, 1, i * ff_half, ff_half, 0, width) for a in range(2) for i in range(2)]
    tokens_ext, codes, taps, w_mixer, w_proj, w_gate_all, w_up_all = start_all(
        tokens,
        decay_codes.astype(jnp.int16),
        jnp.concatenate([conv_query, conv_key, conv_value], axis=1),
        (w_query, w_key, w_value, w_out_gate, w_out, w_gate.T, w_up.T),
        items + pair,
        [3] * len(items) + [1] * len(pair),
        ((width, mixer_width), w_out.shape, w_down.shape, w_down.shape),
        1,
    )
    upstream, low_part, codes = lax.optimization_barrier((cotangent, w_down, codes))
    upstream = lax.all_to_all(upstream, "head", 1, 2, tiled=True)
    w_low = whole(low_part)

    first = (place == 0).astype(jnp.int32).reshape(1)
    normed, pre, q_exp, k_exp, k_end, value, decay, starts, local_end, log_total = forward_one(
        first, tokens_ext, attn_gain, w_mixer, taps, codes
    )
    flat = (-1, key_width)
    log_total = log_total.reshape(flat)
    pair = [(item[0], 0, item[2] - 2, *item[3:]) for item in pair]
    incoming, w_gate_all, w_up_all = exchange(
        local_end.reshape(flat), log_total, 2, pair, (w_gate_all, w_up_all)
    )
    core, states, gated, hidden_in = forward_two(
        first, tokens_ext, pre, q_exp, k_exp, value, decay, starts, incoming.reshape(local_end.shape), out_gain, w_proj
    )
    layer_out, d_hidden_in, normed_two, hidden, d_gate, d_up, grad_mlp_gain = mlp(
        hidden_in.reshape(-1, width), mlp_gain, upstream.reshape(-1, width), w_gate_all, w_up_all, w_low
    )
    d_hidden_in = d_hidden_in.reshape(hidden_in.shape)
    layer_out = layer_out.reshape(hidden_in.shape)
    d_mixer, d_core, d_gate_rows, d_states, own_grad, grad_out_gain = backward_one(
        d_hidden_in, w_proj, core, pre, out_gain, q_exp, decay
    )
    ff_part = ff // 4
    ff_plan = [(a, 1, i * ff_part, ff_part) for a in range(3) for i in range(4)]
    leaving, *blocks = sums(
        (),
        (),
        ff_plan,
        [(0, 0, False), (1, 0, False), (2, 1, False)],
        [w_down.shape] * 3,
        (),
        [a[:, None] for a in (d_gate, d_up, hidden)],
        [normed_two[None, None], upstream.reshape(1, 1, -1, width)],
        3,
        (own_grad.reshape(flat), log_total),
        False,
    )
    d_projected, tokens_grad, grad_taps, grad_attn_gain = backward_two(
        first, tokens_ext, attn_gain, d_hidden_in, w_mixer, taps, pre, q_exp, k_exp, k_end, value, decay, states, d_core,
        d_states, leaving.reshape(local_end.shape), d_gate_rows,
    )

    small = jnp.concatenate(
        [
            jnp.sum(grad_attn_gain, axis=0).reshape(heads, -1),
            grad_mlp_gain.reshape(heads, -1),
            jnp.broadcast_to(grad_out_gain, (heads, value_width)),
            grad_taps.reshape(heads, -1),
        ],
        axis=1,
    )
    small_rows = 256
    lanes = -(-small.shape[1] // (small_rows * 128)) * 128
    small = jnp.pad(small, ((0, 0), (0, small_rows * lanes - small.shape[1]))).reshape(heads, small_rows, lanes)
    mixer_plan = chunks(0, width, 4) + [(1, 1, i * out_half, out_half) for i in range(2)] + chunks(2, small_rows, 2)
    more = [(3 + a, axis, row, size, c % 2) for c, (a, axis, row, size) in enumerate(ff_plan)]
    layer_out, tokens_grad, halos, grad_mixer, grad_out, small, grad_gate, grad_up, grad_down = sums(
        (layer_out, tokens_grad),
        (0, HALO),
        mixer_plan,
        [(0, 0, True), (1, 1, True), 0],
        [(width, mixer_width), w_out.shape, small.shape[1:]] + [w_down.shape] * 3,
        [small.astype(bf16)],
        [normed[None], gated],
        [d_projected, d_mixer[None]],
        4,
        blocks=blocks,
        more=more,
        groups=[(0, 1, 4, 5), (2, 3, 6, 7)],
    )
    last = lax.axis_index("seq") == lax.axis_size("seq") - 1
    (layer_out, tokens_grad, grad_query, grad_key, grad_value, grad_out_gate, grad_out, grad_gate, grad_up, grad_down, small) = finalize(
        last.astype(jnp.int32).reshape(1), layer_out, tokens_grad, halos, grad_mixer, grad_out, grad_gate, grad_up, grad_down,
        small, key_width, value_width,
    )
    small = small.reshape(-1)
    at = 2 * own_width + value_width
    grad_taps = small[at : at + taps[0].size].reshape(taps.shape[1:])
    return (
        layer_out,
        tokens_grad,
        small[:own_width],
        grad_query,
        grad_key,
        grad_value,
        grad_out_gate,
        grad_taps[:, :key_width],
        grad_taps[:, key_width : 2 * key_width],
        grad_taps[:, 2 * key_width :],
        small[2 * own_width : at],
        grad_out,
        small[own_width : 2 * own_width],
        grad_gate.T,
        grad_up.T,
        grad_down,
    )


def solution(mesh):
    in_specs = (
        P(None, "seq", "head"),
        P(None, "seq", "head"),
        P(None, "seq", "head"),
        P(),
        P(None, "head"),
        P(None, "head"),
        P(None, "head"),
        P(None, "head"),
        P(None, "head"),
        P(None, "head"),
        P(None, "head"),
        P(),
        P("head", None),
        P(),
        P(None, "head"),
        P(None, "head"),
        P("head", None),
    )
    out_specs = (
        P(None, "seq", "head"),
        P(None, "seq", "head"),
        P("head"),
        P(None, "head"),
        P(None, "head"),
        P(None, "head"),
        P(None, "head"),
        P(None, "head"),
        P(None, "head"),
        P(None, "head"),
        P(),
        P("head", None),
        P("head"),
        P(None, "head"),
        P(None, "head"),
        P("head", None),
    )
    return jax.shard_map(local, mesh=mesh, in_specs=in_specs, out_specs=out_specs, check_vma=False)
```

```python
from functools import partial

import jax
import jax.numpy as jnp
from jax import lax
from jax.experimental import pallas as pl
from jax.experimental.pallas import tpu as pltpu
from jax.sharding import PartitionSpec as P

SPAN = 64
HALO = 16
MESH = pl.DeviceIdType.MESH

epsilon = 1e-06
decay_unit = 2.0 ** (-17)
f32 = jnp.float32
bf16 = jnp.bfloat16

def row_scale(values):
    return lax.rsqrt(jnp.mean(values * values, axis=-1, keepdims=True) + epsilon)


def silu_slope(values):
    logistic = jax.nn.sigmoid(values)
    return logistic * (1.0 + values * (1.0 - logistic))


def norm_back(values, inverse, weights, upstream):
    weighted = weights * upstream
    return inverse * weighted - values * inverse**3 * jnp.mean(
        weighted * values, axis=-1, keepdims=True
    )


def rounded(values):
    return values.astype(bf16).astype(f32)


def flipped(place, mask):
    return place + mask - 2 * mask * (place // mask % 2)


def over_seq(items, gathered, gsend, grecv, s, z):
    heads = 4

    def order(i):
        return [4, 2, 1] if items[i][0] % 2 == 0 else [2, 4, 1]

    def span(i, j):
        _, _, to, axis, first, count, _, _ = items[i]
        size = count if axis == 0 else gathered[to].shape[2]
        begin = first if axis == 0 else 0
        for mask in order(i)[: j - 4 : -1] if j < 3 else []:
            size = size // 2
            begin = begin + (s // mask % 2) * size
        return pl.multiple_of(begin, size), size

    def seq_copies(i, j):
        _, _, to, axis, first, count, column, _ = items[i]
        begin, size = span(i, j)
        copies = []
        for d in range(1, heads):
            q = (z + d) % heads
            if axis == 0:
                place = gathered[to].at[q, pl.ds(begin, size), pl.ds(column, items[i][7])]
            else:
                place = gathered[to].at[q, pl.ds(first, count), pl.ds(begin, size)]
            copies.append(pltpu.make_async_remote_copy(
                place, place, gsend.at[i, j, d - 1], grecv.at[i, j, d - 1],
                device_id={"seq": flipped(s, order(i)[j]), "head": z}, device_id_type=MESH))
        return copies

    return span, seq_copies


def start_body(seq, n_weights, items, steps, *refs):
    tokens, codes, taps = refs[:3]
    weights = refs[3 : 3 + n_weights]
    out_tokens, out_codes, out_taps = refs[3 + n_weights : 6 + n_weights]
    n_sem = 11
    n_items = len(items)
    gathered = refs[6 + n_weights : -n_sem - n_items]
    held = refs[-n_sem - n_items : -n_sem]
    (tsend, trecv, hsend, hrecv, stay, zsend, zrecv, ysend, yrecv, gsend, grecv) = refs[-n_sem:]
    s, z = lax.axis_index("seq"), lax.axis_index("head")
    heads = 4
    masks = [1, 2, 4]

    def peer(to_s, to_z):
        return {"seq": to_s, "head": to_z}

    barrier = pltpu.get_barrier_semaphore()

    def greet(to_s, to_z):
        pl.semaphore_signal(barrier, 1, device_id=peer(to_s, to_z), device_id_type=MESH)

    for d in range(1, heads):
        greet(s, (z + d) % heads)
    for mask in masks:
        greet(flipped(s, mask), z)

    @pl.when((z == 0) & (s > 0))
    def _():
        for q in range(heads):
            greet(s - 1, q)

    greeted = heads - 1 + len(masks)

    @pl.when(s < seq - 1)
    def _():
        pl.semaphore_wait(barrier, greeted + 1)

    @pl.when(s == seq - 1)
    def _():
        pl.semaphore_wait(barrier, greeted)

    seqs, rows, width = tokens.shape
    mine = rows // heads

    def remote(src, dst, send, recv, to_s, to_z):
        return pltpu.make_async_remote_copy(src, dst, send, recv, device_id=peer(to_s, to_z), device_id_type=MESH)

    def columns(ref, q):
        n = ref.shape[2] // heads
        return pl.ds(pl.multiple_of(q * n, n), n)

    def sends(target, act):
        here = pl.ds(target * mine, mine)
        if target == 0:
            src, dst = tokens.at[:, pl.ds(0, mine)], out_tokens.at[:, pl.ds(HALO, mine), columns(out_tokens, z)]
        else:
            src = tokens.at[:, pl.ds(target * mine - HALO, mine + HALO)]
            dst = out_tokens.at[:, :, columns(out_tokens, z)]
        triples = [
            (src, dst),
            (codes.at[:, here], out_codes.at[:, :, columns(out_codes, z)]),
            (taps, out_taps.at[z]),
        ]

        @pl.when(z == target)
        def _():
            for i, (a, b) in enumerate(triples):
                copy = pltpu.make_async_copy(a, b, stay.at[i])
                if act == "start":
                    copy.start()
                else:
                    copy.wait()

        @pl.when(z != target)
        def _():
            for i, (a, b) in enumerate(triples):
                copy = remote(a, b, tsend.at[i, target], trecv.at[i, z], s, target)
                if act == "start":
                    copy.start()
                else:
                    copy.wait_send()

    def arrive(source):
        @pl.when(z != source)
        def _():
            here = pl.ds(0, mine)

            @pl.when(z == 0)
            def _():
                dst = out_tokens.at[:, pl.ds(HALO, mine), columns(out_tokens, source)]
                remote(tokens.at[:, here], dst, tsend.at[0, source], trecv.at[0, source], s, source).wait_recv()

            @pl.when(z != 0)
            def _():
                dst = out_tokens.at[:, :, columns(out_tokens, source)]
                remote(
                    tokens.at[:, pl.ds(0, mine + HALO)], dst, tsend.at[0, source], trecv.at[0, source], s, source
                ).wait_recv()

            for i, (a, b) in enumerate(
                ((codes.at[:, here], out_codes.at[:, :, columns(out_codes, source)]), (taps, out_taps.at[source]))
            ):
                remote(a, b, tsend.at[i + 1, source], trecv.at[i + 1, source], s, source).wait_recv()

    def halo_copy(source, to_s):
        return remote(
            tokens.at[:, pl.ds(rows - HALO, HALO)], out_tokens.at[:, pl.ds(0, HALO), columns(out_tokens, source)],
            hsend, hrecv.at[source], to_s, 0,
        )

    @pl.when(s < seq - 1)
    def _():
        halo_copy(z, s + 1).start()

    span, seq_copies = over_seq(items, gathered, gsend, grecv, s, z)

    def piece(i, j):
        _, weight, _, axis, first, count, column, _ = items[i]
        begin, size = span(i, j)
        wide = weights[weight].shape[1]
        if axis == 0:
            own = weights[weight].at[pl.ds(begin, size)]
            place = lambda ref, q: ref.at[q, pl.ds(begin, size), pl.ds(column, wide)]
        else:
            own = weights[weight].at[pl.ds(first, count), pl.ds(begin, size)]
            place = lambda ref, q: ref.at[q, pl.ds(first, count), pl.ds(begin, size)]
        return own, place

    def own_load(i):
        _, weight, _, _, first, count, _, _ = items[i]
        return pltpu.make_async_copy(weights[weight].at[pl.ds(first, count)], held[i], stay.at[3 + i])

    def own_store(i):
        _, weight, to, _, first, count, column, _ = items[i]
        wide = weights[weight].shape[1]
        return pltpu.make_async_copy(
            held[i], gathered[to].at[z, pl.ds(first, count), pl.ds(column, wide)], stay.at[3 + i])

    def far_copy(i):
        own, place = piece(i, 0)
        return remote(own, place(gathered[items[i][2]], z), zsend.at[i], zrecv.at[i], s, flipped(z, 2))

    def near_copies(i):
        own, place = piece(i, 0)
        to = gathered[items[i][2]]
        far = flipped(z, 2)
        near = flipped(z, 1)
        return [
            remote(own, place(to, z), ysend.at[i, 0], yrecv.at[i, 0], s, near),
            remote(place(to, far), place(to, far), ysend.at[i, 1], yrecv.at[i, 1], s, near),
        ]

    count = len(items)

    def stage(i, k):
        if k == 0:
            return [far_copy(i)]
        return near_copies(i) if k == 1 else seq_copies(i, k - 2)

    sends_at = 4
    stages = 2 + len(masks)
    pairs = (max(item[0] for item in items) + 2) // 2
    for t in range(pairs + stages):
        for k in reversed(range(stages + 1)):
            for i in range(count):
                if items[i][0] // 2 != t - k or k > 2 + steps[i]:
                    continue
                if k > 0:
                    for copy in stage(i, k - 1):
                        copy.wait_recv()
                if k < 2 + steps[i]:
                    for copy in stage(i, k):
                        copy.start()
        if t == sends_at:
            for target in range(heads):
                sends(target, "start")
        if t == 0:
            for i in range(count):
                own_load(i).start()
    for i in range(count):
        own_load(i).wait()
        own_store(i).start()
    for source in range(heads):
        arrive(source)
    for target in range(heads):
        sends(target, "wait")

    @pl.when((z == 0) & (s > 0))
    def _():
        for q in range(heads):
            halo_copy(q, s - 1).wait_recv()

    @pl.when(s < seq - 1)
    def _():
        halo_copy(z, s + 1).wait_send()

    for i in range(count):
        own_store(i).wait()
        far_copy(i).wait_send()
        for copy in near_copies(i):
            copy.wait_send()
        for j in range(steps[i]):
            for copy in seq_copies(i, j):
                copy.wait_send()


def start_all(tokens, codes, taps, weights, items, steps, shapes, collective_id):
    seq, heads = lax.axis_size("seq"), lax.axis_size("head")
    seqs, rows, width = tokens.shape
    mine = rows // heads
    count = len(items)
    dma = pltpu.SemaphoreType.DMA
    anywhere = pl.BlockSpec(memory_space=pl.ANY)
    out_shape = [
        jax.ShapeDtypeStruct((seqs, mine + HALO, heads * width), tokens.dtype),
        jax.ShapeDtypeStruct((seqs, mine, heads * codes.shape[2]), codes.dtype),
        jax.ShapeDtypeStruct((heads, *taps.shape), taps.dtype),
    ] + [jax.ShapeDtypeStruct((heads, *shape), bf16) for shape in shapes]
    return pl.pallas_call(
        partial(start_body, seq, len(weights), items, steps),
        out_shape=out_shape,
        in_specs=[anywhere] * (3 + len(weights)),
        out_specs=[pl.BlockSpec(memory_space=pltpu.HBM)] * len(out_shape),
        scratch_shapes=[pltpu.VMEM((item[5], weights[item[1]].shape[1]), bf16) for item in items]
        + [
            dma((3, heads)), dma((3, heads)), dma, dma((heads,)), dma((3 + count,)),
            dma((count,)), dma((count,)), dma((count, 2)), dma((count, 2)), dma((count, 3, 3)), dma((count, 3, 3)),
        ],
        compiler_params=pltpu.CompilerParams(
            collective_id=collective_id, has_side_effects=True, vmem_limit_bytes=60 * 2**20),
        name="start_exchange",
    )(tokens, codes, taps, *weights)


def states_exchange(heads, count, per_block, backward, value, logs, out, scratch):
    packed, got, ready, send, recv, bsend, brecv = scratch
    me = lax.axis_index("seq") * heads + lax.axis_index("head")
    part = value.shape[0] // count
    tail = packed.shape[1] - part

    def peer(p):
        return {"seq": p // heads, "head": p % heads}

    def each(act):
        def one(d, carry):
            act((me + d) % count)
            return carry

        lax.fori_loop(1, count, one, 0)

    def greet():
        barrier = pltpu.get_barrier_semaphore()
        each(lambda p: pl.semaphore_signal(barrier, 1, device_id=peer(p), device_id_type=MESH))

    def pack():
        high = logs[...].astype(bf16)
        low = (logs[...] - high.astype(f32)).astype(bf16)

        def one(p, carry):
            packed[p, pl.ds(0, part)] = value[pl.ds(pl.multiple_of(p * part, part), part)]
            return carry

        lax.fori_loop(0, count, one, 0)
        parts_each = count * per_block // value.shape[0]
        zeros = jnp.zeros((tail - 2, high.shape[1]), bf16)
        for b in range(logs.shape[0]):
            both = jnp.concatenate([high[b : b + 1], low[b : b + 1], zeros], axis=0)
            for i in range(parts_each):
                packed[b * parts_each + i, pl.ds(part, tail)] = both
        got[me] = packed[me]

    def there(p, to):
        return pltpu.make_async_remote_copy(
            packed.at[p], got.at[to], send.at[p], recv.at[to], device_id=peer(p), device_id_type=MESH)

    def back(p, to):
        return pltpu.make_async_remote_copy(
            ready.at[p], out.at[pl.ds(pl.multiple_of(to * part, part), part)], bsend.at[p], brecv.at[to],
            device_id=peer(p), device_id_type=MESH)

    def begin():
        each(lambda p: there(p, me).start())

    def add_up():
        def step(i, state):
            p = count - 1 - i if backward else i

            @pl.when(p != me)
            def _():
                there(p, p).wait_recv()

            ready[p] = state.astype(bf16)

            @pl.when(p != me)
            def _():
                back(p, me).start()

            decay = jnp.exp(got[p, pl.ds(part, 1)].astype(f32) + got[p, pl.ds(part + 1, 1)].astype(f32))
            return decay * state + got[p, pl.ds(0, part)].astype(f32)

        lax.fori_loop(0, count, step, jnp.zeros((part, value.shape[1]), f32))
        out[pl.ds(pl.multiple_of(me * part, part), part)] = ready[me]

    def end():
        each(lambda p: back(p, p).wait_recv())
        each(lambda p: there(p, me).wait_send())
        each(lambda p: back(p, me).wait_send())

    return greet, pack, begin, add_up, end


def states_scratch(count, rows, width):
    part, tail = rows // count, 16
    dma = pltpu.SemaphoreType.DMA
    return [
        pltpu.VMEM((count, part + tail, width), bf16),
        pltpu.VMEM((count, part + tail, width), bf16),
        pltpu.VMEM((count, part, width), bf16),
        dma((count,)), dma((count,)), dma((count,)), dma((count,)),
    ]


def exchange_body(count, heads, per_block, items, n_more, *refs):
    value, logs = refs[:2]
    out = refs[2 + n_more]
    gathered = refs[3 + n_more : 3 + 2 * n_more]
    *scratch, gsend, grecv = refs[3 + 2 * n_more :]
    _, seq_copies = over_seq(items, gathered, gsend, grecv, lax.axis_index("seq"), lax.axis_index("head"))
    greet, pack, begin, add_up, end = states_exchange(heads, count, per_block, False, value, logs, out, scratch)
    greet()
    pack()
    pl.semaphore_wait(pltpu.get_barrier_semaphore(), count - 1)
    begin()
    for i in range(len(items)):
        for copy in seq_copies(i, 1):
            copy.start()
    add_up()
    for i in range(len(items)):
        for copy in seq_copies(i, 1):
            copy.wait_recv()
        for copy in seq_copies(i, 2):
            copy.start()
    end()
    for i in range(len(items)):
        for copy in seq_copies(i, 2):
            copy.wait()
        for copy in seq_copies(i, 1):
            copy.wait_send()


def exchange(value, logs, collective_id, items=(), gathered=()):
    heads = lax.axis_size("head")
    count = lax.axis_size("seq") * heads
    rows, width = value.shape
    more = len(gathered)
    dma = pltpu.SemaphoreType.DMA
    far, near = pl.BlockSpec(memory_space=pltpu.HBM), pl.BlockSpec(memory_space=pltpu.VMEM)
    return pl.pallas_call(
        partial(exchange_body, count, heads, rows // logs.shape[0], items, more),
        out_shape=[jax.ShapeDtypeStruct((rows, width), bf16)]
        + [jax.ShapeDtypeStruct(a.shape, a.dtype) for a in gathered],
        in_specs=[near] * 2 + [far] * more,
        out_specs=[near] + [far] * more,
        input_output_aliases={2 + i: 1 + i for i in range(more)},
        scratch_shapes=states_scratch(count, rows, width)
        + [dma((max(len(items), 1), 3, 3)), dma((max(len(items), 1), 3, 3))],
        compiler_params=pltpu.CompilerParams(
            collective_id=collective_id, has_side_effects=True, vmem_limit_bytes=60 * 2**20),
        name="exchange_states",
    )(value, logs, *gathered)


def aligned(x, size):
    return x if isinstance(x, int) else pl.multiple_of(x, size)


def sums_body(seq, plan, sources, shapes, n_given, n_left, n_right, leads, states, spread, more, groups, n_ring, rider, *refs):
    heads = 4
    nz = 1
    seq_masks = [1 << k for k in range(seq.bit_length() - 1)]
    split, joined = seq_masks[:3], seq_masks[3:]
    ns, nj = len(split), len(joined)
    refs = list(refs)

    def take(n):
        taken = refs[:n]
        del refs[:n]
        return taken

    value, logs = take(2) if states else (None, None)
    acts = take(len(leads))
    n_arrays, count = len(sources), len(plan)
    blocks = take(len(shapes) - n_arrays)
    orders = [c % 2 for c in range(count)] + [item[4] for item in more]
    plan = [*plan, *(item[:4] for item in more)]
    given, lefts, rights = take(n_given), take(n_left), take(n_right)
    rider_in = take(rider[0]) if rider else None
    (new_state,) = take(1) if states else (None,)
    acts_full = take(len(leads))
    halos = take(sum(map(bool, leads)))
    outs = take(len(shapes))
    rider_out = take(rider[1]) if rider else None
    per = ns + nj + nz
    owns = take(count)
    recvs = [take(per) for _ in range(count)]
    dots = [c for c in range(count) if not isinstance(sources[plan[c][0]], int)]
    ring = take(min(len(dots), n_ring))
    staged = {c: ring[n % n_ring] for n, c in enumerate(dots)}
    state_scratch = take(7) if states else None
    rider_scratch = take(rider[2]) if rider else None
    (load_sem, send_sem, recv_sem, jsend, jrecv, zsend, zrecv, gsend, grecv, keep_sem, asend, arecv, stay, hsend,
     hrecv) = refs
    s, z = lax.axis_index("seq"), lax.axis_index("head")

    def peer(to_s, to_z):
        return {"seq": to_s, "head": to_z}

    def remote(src, dst, send, recv, to_s, to_z):
        return pltpu.make_async_remote_copy(src, dst, send, recv, device_id=peer(to_s, to_z), device_id_type=MESH)

    def to_features(a, first):
        act, full, lead = acts[a], acts_full[a], leads[a]
        mine, width = act.shape[1] - lead, full.shape[2]

        def features(q):
            return pl.ds(aligned(q * width, width), width)

        def rows_to(q):
            return pl.ds(aligned(q * mine, mine), mine)

        def back_copy(d, waits):
            q = (z + d) % heads
            to, of = (z, q) if waits else (q, z)
            return remote(
                act.at[:, pl.ds(lead, mine), features(to)], full.at[:, rows_to(of)], asend.at[a, q], arecv.at[a, of], s, q)

        def halo_copy(to_s, q, to, of):
            return remote(
                act.at[:, pl.ds(0, lead), features(to)], halos[0].at[of], hsend.at[q], hrecv.at[of], to_s, q)

        stay_copy = pltpu.make_async_copy(
            act.at[:, pl.ds(lead, mine), features(z)], full.at[:, rows_to(z)], stay.at[a])
        stay_copy.start() if first else stay_copy.wait()
        for d in range(1, heads):
            back_copy(d, False).start() if first else back_copy(d, False).wait_send()
            if not first:
                back_copy(d, True).wait_recv()
        if not lead:
            return

        @pl.when(z != 0)
        def _():
            halo_own = pltpu.make_async_copy(act.at[:, pl.ds(0, lead), features(z)], halos[0].at[z], stay.at[len(acts)])
            halo_own.start() if first else halo_own.wait()
            for d in range(1, heads):
                q = (z + d) % heads
                halo_copy(s, q, q, z).start() if first else halo_copy(s, q, q, z).wait_send()

        @pl.when((z == 0) & (s > 0))
        def _():
            for q in range(heads):
                halo_copy(s - 1, q, q, 0).start() if first else halo_copy(s - 1, q, q, 0).wait_send()

        if not first:
            for d in range(1, heads):
                q = (z + d) % heads

                @pl.when(q != 0)
                def _():
                    halo_copy(s, q, z, q).wait_recv()

            @pl.when(s < seq - 1)
            def _():
                halo_copy(s + 1, 0, z, 0).wait_recv()

    def masks(c):
        return split[:1] + (split[1:] if orders[c] == 0 else split[:0:-1])

    def bit(c, k):
        return s // masks(c)[k] % 2

    def extent(c):
        array, axis, first, size = plan[c]
        return size if axis == 0 else shapes[array][1]

    def kept(c, k):
        size = extent(c)
        return sum((bit(c, j) * (size >> (j + 1)) for j in range(1, k + 1)), 0)

    def cut(c, begin, size):
        part = pl.ds(aligned(begin, size), size)
        return (part, slice(None)) if plan[c][1] == 0 else (slice(None), part)

    def in_array(c, begin, size):
        _, axis, first, rows = plan[c]
        if axis == 0:
            return pl.ds(aligned(first + begin, size), size), slice(None)
        return pl.ds(first, rows), pl.ds(aligned(begin, size), size)

    def load(c):
        half = extent(c) // 2
        rows, columns = in_array(c, bit(c, 0) * half, half)
        return pltpu.make_async_copy(given[sources[plan[c][0]]].at[:, rows, columns], owns[c], load_sem.at[c])

    def product(c):
        left_at, right_at, natural = sources[plan[c][0]]
        left, right = lefts[left_at], rights[right_at]
        half = extent(c) // 2

        def one(q, carry):
            for to, b in ((staged[c], 1 - bit(c, 0)), (owns[c], bit(c, 0))):
                rows, columns = in_array(c, b * half, half)
                total = None
                for i in range(left.shape[1]):
                    b_ = right[q if right.shape[0] > 1 else 0, i, :, columns]
                    if natural:
                        term = dot_tn(left[q if left.shape[0] > 1 else 0, i, :, rows], b_)
                    else:
                        term = dot_nn(left[q if left.shape[0] > 1 else 0, i, rows, :], b_)
                    total = term if total is None else total + term
                to[q] = total.astype(bf16)
            return carry

        lax.fori_loop(0, heads, one, 0)

    def seq_copy(c, k):
        half = extent(c) >> (k + 1)
        other = (1 - bit(c, k)) * half
        if k == 0 and c in staged:
            source = staged[c]
        elif k == 0:
            rows, columns = in_array(c, other, half)
            source = given[sources[plan[c][0]]].at[:, rows, columns]
        else:
            rows, columns = cut(c, kept(c, k - 1) + other, half)
            source = owns[c].at[:, rows, columns]
        return remote(source, recvs[c][k], send_sem.at[c, k], recv_sem.at[c, k], flipped(s, masks(c)[k]), z)

    def final(c):
        return cut(c, kept(c, ns - 1), extent(c) >> ns)

    def joined_copy(c, k):
        rows, columns = final(c)
        return remote(
            owns[c].at[:, rows, columns], recvs[c][ns + k], jsend.at[c, k], jrecv.at[c, k], flipped(s, joined[k]), z)

    def head_copy(c, d, waits):
        rows, columns = final(c)
        q = (z + d) % heads
        to, of = (z, q) if waits else (q, z)
        return remote(
            owns[c].at[to, rows, columns], recvs[c][ns + nj].at[of], zsend.at[c, q], zrecv.at[c, of], s, q)

    def add(c, k):
        axis, rows = plan[c][1], plan[c][3]
        if k < ns:
            begin, size = kept(c, k), extent(c) >> (k + 1)
        else:
            begin, size = kept(c, ns - 1), extent(c) >> ns
        received = recvs[c][k]
        tall = size if axis == 0 else rows
        wide = shapes[plan[c][0]][1] if axis == 0 else size
        tile = tall
        while tile * wide > 98304 and tile % 32 == 0:
            tile //= 2
        tiles = tall // tile

        def places(r):
            there = pl.ds(pl.multiple_of(r, tile), tile)
            if axis == 0:
                return there, pl.ds(pl.multiple_of(begin + r, tile), tile), slice(None)
            return there, there, pl.ds(aligned(begin, size), size)

        def one(t, carry):
            i = t // tiles
            there, here, columns = places(t % tiles * tile)
            owns[c][i, here, columns] = owns[c][i, here, columns] + received[i, there]
            return carry

        def last_one(t, carry):
            there, here, columns = places(t * tile)
            total = owns[c][z, here, columns].astype(f32)
            for d in range(1, heads):
                total = total + received[(z + d) % heads, there].astype(f32)
            owns[c][z, here, columns] = total.astype(bf16)
            return carry

        if k < ns + nj:
            lax.fori_loop(0, heads * tiles, one, 0)
        else:
            lax.fori_loop(0, tiles, last_one, 0)

    def held(c, level):
        size = extent(c)
        return in_array(c, sum(bit(c, j) * (size >> (j + 1)) for j in range(level)), size >> level)

    def own_block(c):
        if c >= count:
            return blocks[plan[c][0] - n_arrays].at[pl.ds(plan[c][2], plan[c][3])]
        return owns[c].at[z, *final(c)]

    def keep(c):
        rows, columns = held(c, ns)
        if not spread:
            columns = slice(None)
        return pltpu.make_async_copy(own_block(c), outs[plan[c][0]].at[rows, columns], keep_sem.at[c])

    def gather_copy(c, j):
        level = ns - j
        rows, columns = held(c, level)
        array = outs[plan[c][0]].at[rows, columns]
        source = own_block(c) if j == 0 else array
        return remote(source, array, gsend.at[c, j], grecv.at[c, j], flipped(s, masks(c)[level - 1]), z)

    barrier = pltpu.get_barrier_semaphore()
    if states:
        everyone = seq * heads
        greet, pack, begin, add_up, end = states_exchange(
            heads, everyone, value.shape[0] // logs.shape[0], True, value, logs, new_state, state_scratch)
        greet()
        pack()
        pl.semaphore_wait(barrier, everyone - 1)
        begin()
    else:

        def greet(to_s, to_z):
            pl.semaphore_signal(barrier, 1, device_id=peer(to_s, to_z), device_id_type=MESH)

        for mask in seq_masks:
            greet(flipped(s, mask), z)
        for d in range(1, heads):
            greet(s, (z + d) % heads)
        greeted = len(seq_masks) + heads - 1

        @pl.when(s < seq - 1)
        def _():
            greet(s + 1, 0)

        @pl.when((z == 0) & (s > 0))
        def _():
            pl.semaphore_wait(barrier, greeted + heads)

        @pl.when((z != 0) | (s == 0))
        def _():
            pl.semaphore_wait(barrier, greeted)

    last = per + (ns if spread else 1)

    def copies(c, k, waits=False):
        if k < ns:
            return [seq_copy(c, k)]
        if k < ns + nj:
            return [joined_copy(c, k - ns)]
        if k < per:
            return [head_copy(c, d, waits) for d in range(1, heads)]
        return [gather_copy(c, k - per)] if spread else []

    def advance(c, k):
        if k == 0 and c not in staged:
            load(c).wait()
        if k == per:
            keep(c).wait()
        for copy in copies(c, k, True):
            copy.wait_recv()
        if ns <= k < ns + nj:
            joined_copy(c, k - ns).wait_send()
        if k < per:
            add(c, k)
        if k + 1 == per:
            keep(c).start()
        if k + 1 < last and c < count:
            for copy in copies(c, k + 1):
                copy.start()

    def begin_chunk(c):
        if c in staged:
            if dots.index(c) >= n_ring:
                seq_copy(dots[dots.index(c) - n_ring], 0).wait_send()
            product(c)
        else:
            load(c).start()
        seq_copy(c, 0).start()

    ride_at, ride_parts = 4, 4
    for t in range(len(groups) + last):
        for k in range(last):
            if 0 <= t - 1 - k < len(groups):
                for c in groups[t - 1 - k]:
                    advance(c, k)
        if t < len(groups):
            for c in groups[t]:
                begin_chunk(c)
        for c in range(count, len(plan)):
            if t == 0:
                keep(c).start()
            elif t <= ns:
                advance(c, per + t - 1)
            if t < ns:
                gather_copy(c, t).start()
        if t == 0:
            for a in range(len(acts)):
                to_features(a, True)
        if t == 1 and states:
            add_up()
        if states and t == ride_at:
            end()
            load_first, run, finish_run = rider[3](s * heads + z == 0, new_state, rider_in, rider_out, rider_scratch)
            load_first()
        if states and ride_at <= t < ride_at + ride_parts:
            run(t - ride_at, ride_parts)
    for a in range(len(acts)):
        to_features(a, False)
    for c in range(count):
        for k in range(last):
            if not ns <= k < ns + nj and not (k == 0 and c in dots[: max(len(dots) - n_ring, 0)]):
                for copy in copies(c, k):
                    copy.wait_send()
    for c in range(count, len(plan)):
        for j in range(ns):
            gather_copy(c, j).wait_send()
    if states:
        finish_run()


def sums(acts, leads, plan, sources, shapes, given, lefts, rights, collective_id, states=(), spread=True, blocks=(), more=(), groups=None, rider=None):
    groups = groups or [(c, c + 1) for c in range(0, len(plan), 2)]
    seq, heads = lax.axis_size("seq"), lax.axis_size("head")
    nj = max(0, seq.bit_length() - 4)
    ns = 3
    owns, recvs, staged = [], [], []
    n_ring = 4 if states else 8
    ride_args, ride_specs, ride_shapes, ride_outs, ride_scratch, ride_body = rider or ((), (), (), (), (), None)
    ride = (len(ride_args), len(ride_shapes), len(ride_scratch), ride_body) if rider else None
    for a, axis, first, rows in plan:
        columns = shapes[a][1]
        cut = lambda k: (rows >> k, columns) if axis == 0 else (rows, columns >> k)
        owns.append(pltpu.VMEM((heads, *cut(1)), bf16))
        recvs += [pltpu.VMEM((heads, *cut(k + 1)), bf16) for k in range(ns)]
        recvs += [pltpu.VMEM((heads, *cut(ns)), bf16) for k in range(nj)]
        recvs.append(pltpu.VMEM((heads, *cut(ns)), bf16))
        if not isinstance(sources[a], int):
            staged.append(pltpu.VMEM((heads, *cut(1)), bf16))
    count, every = len(plan), len(plan) + len(more)
    dma = pltpu.SemaphoreType.DMA
    sems = [
        dma((count,)), dma((count, ns)), dma((count, ns)), dma((count, max(nj, 1))), dma((count, max(nj, 1))),
        dma((count, heads)), dma((count, heads)), dma((every, ns)), dma((every, ns)), dma((every,)),
        dma((2, heads)), dma((2, heads)), dma((3,)), dma((heads,)), dma((heads,)),
    ]
    anywhere, near = pl.BlockSpec(memory_space=pl.ANY), pl.BlockSpec(memory_space=pltpu.VMEM)
    out_shape, halo_shape = [], []
    for act, lead in zip(acts, leads):
        seqs, rows_here, features = act.shape
        width = features // heads
        out_shape.append(jax.ShapeDtypeStruct((seqs, heads * (rows_here - lead), width), bf16))
        if lead:
            halo_shape.append(jax.ShapeDtypeStruct((heads, seqs, lead, width), bf16))
    out_shape += halo_shape
    if not spread:
        shapes_out = [(rows, columns >> ns) for rows, columns in shapes]
    out_shape += [jax.ShapeDtypeStruct(shape, bf16) for shape in (shapes if spread else shapes_out)]
    out_specs = [anywhere] * len(out_shape) + list(ride_outs)
    out_shape += ride_shapes
    state_scratch = []
    if states:
        out_shape.insert(0, jax.ShapeDtypeStruct(states[0].shape, bf16))
        out_specs.insert(0, near)
        state_scratch = states_scratch(seq * heads, *states[0].shape)
    return pl.pallas_call(
        partial(sums_body, seq, plan, sources, shapes, len(given), len(lefts), len(rights), leads, bool(states), spread, more, groups, n_ring, ride),
        out_shape=out_shape,
        in_specs=[near] * len(states)
        + [anywhere] * len(acts)
        + [near] * len(blocks)
        + [anywhere] * len(given)
        + [near] * (len(lefts) + len(rights))
        + list(ride_specs),
        out_specs=out_specs,
        scratch_shapes=owns + recvs + staged[:n_ring] + state_scratch + list(ride_scratch) + sems,
        compiler_params=pltpu.CompilerParams(
            collective_id=collective_id, has_side_effects=True, vmem_limit_bytes=60 * 2**20),
        name="sum_gradients",
    )(*states, *acts, *blocks, *given, *lefts, *rights, *ride_args)


def dot_nt(a, b):
    return lax.dot_general(a, b, (((1,), (1,)), ((), ())), preferred_element_type=f32)


def dot_tn(a, b):
    return lax.dot_general(a, b, (((0,), (0,)), ((), ())), preferred_element_type=f32)


def mlp_body(per_head, hid, gain, cot, w_gate, w_up, w_low, lay, d_hid, normed, hidden, d_gate, d_up, d_gain, acc, part, dx):
    step = pl.program_id(0)

    @pl.when(step == 0)
    def _():
        values = hid[...]
        normed[...] = (values * row_scale(values) * gain[...]).astype(bf16)
        acc[...] = values
        dx[...] = jnp.zeros_like(dx)

    g = dot_nt(w_gate[0], normed[...])
    u = dot_nt(w_up[0], normed[...])
    dh = rounded(dot_nt(w_low[0], cot[...]))
    logistic = jax.nn.sigmoid(g)
    act = g * logistic
    h = (act * u).astype(bf16)
    dg = (dh * u * (logistic * (1.0 + g * (1.0 - logistic)))).astype(bf16)
    du = (dh * act).astype(bf16)
    hidden[0] = h
    d_gate[0] = dg
    d_up[0] = du
    term = dot_tn(h, w_low[0])
    first = step % per_head == 0

    @pl.when(first)
    def _():
        part[...] = term

    @pl.when(jnp.logical_not(first))
    def _():
        part[...] += term

    @pl.when(step % per_head == per_head - 1)
    def _():
        acc[...] += rounded(part[...])

    dx[...] += dot_tn(dg, w_gate[0]) + dot_tn(du, w_up[0])

    @pl.when(step == pl.num_programs(0) - 1)
    def _():
        lay[...] = acc[...].astype(bf16)
        values, upstream = hid[...], dx[...]
        scale = row_scale(values)
        d_gain[...] = jnp.sum(upstream * values * scale, axis=0, keepdims=True)
        d_hid[...] = cot[...].astype(f32) + norm_back(values, scale, gain[...], upstream)


def mlp(hidden_in, gain, upstream, w_gate, w_up, w_low):
    tokens, width = hidden_in.shape
    heads, units, _ = w_gate.shape
    per_head = 1
    block = units // per_head
    weights = pl.BlockSpec((1, block, width), lambda i: (i // per_head, i % per_head, 0))
    units_out = pl.BlockSpec((1, block, tokens), lambda i: (i // per_head, i % per_head, 0))
    all_of = lambda *shape: pl.BlockSpec(shape, lambda i: (0, 0))
    units_shape = jax.ShapeDtypeStruct((heads, units, tokens), bf16)
    token_shape = lambda kind: jax.ShapeDtypeStruct((tokens, width), kind)
    return pl.pallas_call(
        partial(mlp_body, per_head),
        grid=(heads * per_head,),
        in_specs=[all_of(tokens, width), all_of(1, width), all_of(tokens, width), weights, weights, weights],
        out_specs=[all_of(tokens, width)] * 3 + [units_out] * 3 + [all_of(1, width)],
        out_shape=[token_shape(bf16), token_shape(f32), token_shape(bf16)]
        + [units_shape] * 3
        + [jax.ShapeDtypeStruct((1, width), f32)],
        scratch_shapes=[pltpu.VMEM((tokens, width), f32)] * 3,
        compiler_params=pltpu.CompilerParams(vmem_limit_bytes=60 * 2**20),
        name="feed_forward",
    )(hidden_in, gain.reshape(1, width), upstream, w_gate, w_up, w_low)


def rows_after(values, count):
    if count == 0:
        return values
    return jnp.concatenate([values[count:], jnp.zeros((count, values.shape[1]), values.dtype)], axis=0)


def short_conv(pre, taps, rows):
    lead = HALO - taps.shape[0] + 1
    return sum(taps[j : j + 1] * pre[lead + j : lead + j + rows] for j in range(taps.shape[0]))


def spans(values):
    return [values[n * SPAN : (n + 1) * SPAN] for n in range(values.shape[0] // SPAN)]


def lower(count):
    row = lax.broadcasted_iota(jnp.int32, (count, count), 0)
    column = lax.broadcasted_iota(jnp.int32, (count, count), 1)
    return row, column


def causal_scores(left, right):
    row, column = lower(SPAN)
    return jnp.where(row >= column, dot_nt(left, right), 0.0).astype(bf16)


def dot_nn(a, b):
    return jnp.dot(a, b, preferred_element_type=f32)


def without_first(values, first):
    row = lax.broadcasted_iota(jnp.int32, values.shape, 0)
    return jnp.where((row < HALO) & (first > 0), 0.0, values.astype(f32))


def forward_one_body(first, tokens, gain, w, taps, codes, normed, pre, q_exp, k_exp, k_end, value, decay, starts, ends, logs, kept):
    h, i = pl.program_id(0), pl.program_id(1)

    @pl.when(h == 0)
    def _():
        values = without_first(tokens[0], first[0])
        kept[i] = (values * row_scale(values) * gain[...]).astype(bf16)

    normed[0] = kept[i]
    projected = dot_nn(kept[i], w[0]).astype(bf16)
    pre[0, 0] = projected
    rows = codes.shape[1]
    key = codes.shape[2]
    wide = taps.shape[2]
    act = jax.nn.silu(short_conv(projected[:, :wide].astype(f32), taps[0], rows))
    whole_codes = codes[0].astype(jnp.int32)
    high = whole_codes // 128
    row, column = lower(rows)
    within = ((row >= column) & (row // SPAN == column // SPAN)).astype(bf16)
    total = 128.0 * dot_nn(within, high.astype(bf16)) + dot_nn(within, (whole_codes - 128 * high).astype(bf16))
    log = total * -decay_unit
    decay[0, 0] = log
    grow = jnp.exp(log)
    q_exp[0, 0] = (act[:, :key] * key**-0.5 * grow).astype(bf16)
    k_exp[0, 0] = (act[:, key : 2 * key] * jnp.exp(-log)).astype(bf16)
    value[0, 0] = act[:, 2 * key :].astype(bf16)
    state = jnp.zeros((wide - 2 * key, key), f32)
    sums_log = jnp.zeros((1, key), f32)
    for n, part in enumerate(spans(log)):
        at = pl.ds(n * SPAN, SPAN)
        last = part[SPAN - 1 :]
        k_end[0, 0, at] = (act[n * SPAN : (n + 1) * SPAN, key : 2 * key] * jnp.exp(last - part)).astype(bf16)
        starts[0, 0, n] = state.astype(bf16)
        state = jnp.exp(last) * state + dot_tn(value[0, 0, at], k_end[0, 0, at])
        sums_log = sums_log + last
    ends[0, 0] = state.astype(bf16)
    logs[0, 0] = sums_log


def forward_one(first, tokens, gain, w, taps, codes):
    heads, width, columns = w.shape
    seqs, tall, _ = tokens.shape
    rows = tall - HALO
    tap_count, wide = taps.shape[1:]
    key = codes.shape[2] // heads
    wide_value = wide - 2 * key
    blocks = rows // SPAN
    per = lambda *shape: pl.BlockSpec((1, 1, *shape), lambda h, i: (h, i) + (0,) * len(shape))
    shape = lambda kind, *rest: jax.ShapeDtypeStruct((heads, seqs, *rest), kind)
    return pl.pallas_call(
        forward_one_body,
        grid=(heads, seqs),
        in_specs=[
            pl.BlockSpec(memory_space=pltpu.SMEM),
            pl.BlockSpec((1, tall, width), lambda h, i: (i, 0, 0)),
            pl.BlockSpec((1, width), lambda h, i: (0, 0)),
            pl.BlockSpec((1, width, columns), lambda h, i: (h, 0, 0)),
            pl.BlockSpec((1, tap_count, wide), lambda h, i: (h, 0, 0)),
            pl.BlockSpec((1, rows, key), lambda h, i: (i, 0, h)),
        ],
        out_specs=[
            pl.BlockSpec((1, tall, width), lambda h, i: (i, 0, 0)),
            per(tall, columns), per(rows, key), per(rows, key), per(rows, key), per(rows, wide_value), per(rows, key),
            per(blocks, wide_value, key), per(wide_value, key), per(1, key),
        ],
        out_shape=[
            jax.ShapeDtypeStruct((seqs, tall, width), bf16),
            shape(bf16, tall, columns), shape(bf16, rows, key), shape(bf16, rows, key), shape(bf16, rows, key),
            shape(bf16, rows, wide_value), shape(f32, rows, key), shape(bf16, blocks, wide_value, key),
            shape(bf16, wide_value, key), shape(f32, 1, key),
        ],
        scratch_shapes=[pltpu.VMEM((seqs, tall, width), bf16)],
        compiler_params=pltpu.CompilerParams(vmem_limit_bytes=60 * 2**20),
        name="attention_spans",
    )(first, tokens, gain.reshape(1, -1), w, taps, codes)


def forward_two_body(first, tokens, pre, q_exp, k_exp, value, decay, starts, incoming, out_gain, w_out, core, states, gated, hidden_in):
    h = pl.program_id(1)
    wide_value = value.shape[3]
    carry = jnp.ones((1, q_exp.shape[3]), f32)
    entering = incoming[0, 0].astype(f32)
    parts = []
    for n in range(starts.shape[2]):
        at = pl.ds(n * SPAN, SPAN)
        state = (starts[0, 0, n].astype(f32) + carry * entering).astype(bf16)
        states[0, 0, n] = state
        q = q_exp[0, 0, at]
        scores = causal_scores(q, k_exp[0, 0, at])
        parts.append(dot_nn(scores, value[0, 0, at]) + dot_nt(q, state))
        carry = carry * jnp.exp(decay[0, 0, pl.ds((n + 1) * SPAN - 1, 1)])
    out = jnp.concatenate(parts, axis=0)
    core[0, 0] = out
    gate = pre[0, 0, pl.ds(HALO, out.shape[0]), pl.ds(pre.shape[3] - wide_value, wide_value)].astype(f32)
    gated[0, 0] = (out * row_scale(out) * out_gain[...] * jax.nn.silu(gate)).astype(bf16)
    term = rounded(dot_nn(gated[0, 0], w_out[0]))

    @pl.when(h == 0)
    def _():
        hidden_in[0] = without_first(tokens[0], first[0])[HALO:] + term

    @pl.when(h > 0)
    def _():
        hidden_in[0] += term


def head_spec(*shape):
    return pl.BlockSpec((1, 1, *shape), lambda i, h: (h, i) + (0,) * len(shape))


def forward_two(first, tokens, pre, q_exp, k_exp, value, decay, starts, incoming, out_gain, w_out):
    heads, seqs, rows, key = q_exp.shape
    wide_value, width = w_out.shape[1:]
    blocks = rows // SPAN
    tall = rows + HALO
    per = head_spec
    shape = lambda kind, *rest: jax.ShapeDtypeStruct((heads, seqs, *rest), kind)
    return pl.pallas_call(
        forward_two_body,
        grid=(seqs, heads),
        in_specs=[
            pl.BlockSpec(memory_space=pltpu.SMEM),
            pl.BlockSpec((1, tall, width), lambda i, h: (i, 0, 0)),
            per(tall, pre.shape[3]), per(rows, key), per(rows, key), per(rows, wide_value), per(rows, key),
            per(blocks, wide_value, key), per(wide_value, key),
            pl.BlockSpec((1, wide_value), lambda i, h: (0, 0)),
            pl.BlockSpec((1, wide_value, width), lambda i, h: (h, 0, 0)),
        ],
        out_specs=[
            per(rows, wide_value), per(blocks, wide_value, key), per(rows, wide_value),
            pl.BlockSpec((1, rows, width), lambda i, h: (i, 0, 0)),
        ],
        out_shape=[
            shape(f32, rows, wide_value), shape(bf16, blocks, wide_value, key), shape(bf16, rows, wide_value),
            jax.ShapeDtypeStruct((seqs, rows, width), f32),
        ],
        compiler_params=pltpu.CompilerParams(vmem_limit_bytes=60 * 2**20),
        name="attention_outputs",
    )(first, tokens, pre, q_exp, k_exp, value, decay, starts, incoming, out_gain.reshape(1, -1), w_out)


def backward_one_body(d_hidden_in, w_out, core, pre, out_gain, q_exp, decay, d_mixer, d_core, d_gate, d_states, own_grad, d_gain):
    i, h = pl.program_id(0), pl.program_id(1)
    wide_value = core.shape[3]

    @pl.when(h == 0)
    def _():
        d_mixer[0] = d_hidden_in[0].astype(bf16)

    d_gated = rounded(dot_nt(d_mixer[0], w_out[0]))
    out = core[0, 0]
    gate = pre[0, 0, pl.ds(HALO, out.shape[0]), pl.ds(pre.shape[3] - wide_value, wide_value)].astype(f32)
    scale = row_scale(out)
    normed = out * scale
    d_normed = d_gated * jax.nn.silu(gate)
    d_gate[0, 0] = (d_gated * normed * out_gain[...] * silu_slope(gate)).astype(bf16)
    gain_term = jnp.sum(d_normed * normed, axis=0, keepdims=True)

    @pl.when((i == 0) & (h == 0))
    def _():
        d_gain[...] = gain_term

    @pl.when((i > 0) | (h > 0))
    def _():
        d_gain[...] += gain_term

    d_core[0, 0] = norm_back(out, scale, out_gain[...], d_normed).astype(bf16)
    carry = jnp.ones((1, q_exp.shape[3]), f32)
    total = jnp.zeros((wide_value, q_exp.shape[3]), f32)
    for n in range(out.shape[0] // SPAN):
        at = pl.ds(n * SPAN, SPAN)
        term = dot_tn(d_core[0, 0, at], q_exp[0, 0, at])
        d_states[0, 0, n] = term.astype(bf16)
        total = total + carry * term
        carry = carry * jnp.exp(decay[0, 0, pl.ds((n + 1) * SPAN - 1, 1)])
    own_grad[0, 0] = total.astype(bf16)


def backward_one(d_hidden_in, w_out, core, pre, out_gain, q_exp, decay):
    heads, seqs, rows, key = q_exp.shape
    wide_value, width = w_out.shape[1:]
    blocks = rows // SPAN
    per = head_spec
    shape = lambda kind, *rest: jax.ShapeDtypeStruct((heads, seqs, *rest), kind)
    by_seq = pl.BlockSpec((1, rows, width), lambda i, h: (i, 0, 0))
    gain = pl.BlockSpec((1, wide_value), lambda i, h: (0, 0))
    return pl.pallas_call(
        backward_one_body,
        grid=(seqs, heads),
        in_specs=[
            by_seq, pl.BlockSpec((1, wide_value, width), lambda i, h: (h, 0, 0)), per(rows, wide_value),
            per(rows + HALO, pre.shape[3]), gain, per(rows, key), per(rows, key),
        ],
        out_specs=[
            by_seq, per(rows, wide_value), per(rows, wide_value), per(blocks, wide_value, key), per(wide_value, key),
            gain,
        ],
        out_shape=[
            jax.ShapeDtypeStruct((seqs, rows, width), bf16), shape(bf16, rows, wide_value),
            shape(bf16, rows, wide_value), shape(bf16, blocks, wide_value, key), shape(bf16, wide_value, key),
            jax.ShapeDtypeStruct((1, wide_value), f32),
        ],
        compiler_params=pltpu.CompilerParams(vmem_limit_bytes=60 * 2**20),
        name="attention_outputs_back",
    )(d_hidden_in, w_out, core, pre, out_gain.reshape(1, -1), q_exp, decay)


def backward_two_step(
    i, h, heads, first, tokens, gain, d_hidden_in, w, taps, pre, q_exp, k_exp, k_end, value, decay, states, d_core, d_states, leaving,
    d_gate, d_projected, d_tokens, d_taps, d_gain, d_normed,
):
    key, wide_value = q_exp.shape[3], value.shape[3]
    rows = q_exp.shape[2]
    blocks = rows // SPAN
    scale = key**-0.5
    d_end = leaving[...].astype(f32)
    pieces = [None] * blocks
    for n in reversed(range(blocks)):
        at = pl.ds(n * SPAN, SPAN)
        q, k, v, dc = q_exp[0, 0, at], k_exp[0, 0, at], value[0, 0, at], d_core[0, 0, at]
        log = decay[0, 0, at]
        last = log[SPAN - 1 :]
        d_end_low = d_end.astype(bf16)
        scores = causal_scores(q, k)
        d_scores = causal_scores(dc, v)
        d_query = (dot_nn(d_scores, k) + dot_nn(dc, states[0, 0, n])) * (scale * jnp.exp(log))
        d_key = dot_tn(d_scores, q) * jnp.exp(-log) + dot_nn(v, d_end_low) * jnp.exp(last - log)
        d_value = dot_tn(scores, dc) + dot_nt(k_end[0, 0, at], d_end_low)
        pieces[n] = jnp.concatenate([d_query, d_key, d_value], axis=1)
        d_end = jnp.exp(last) * d_end + d_states[0, 0, n].astype(f32)
    d_act = jnp.concatenate(pieces, axis=0)
    tap_count, wide = taps.shape[1:]
    ext = pre[0, 0, :, pl.ds(0, wide)].astype(f32)
    d_conv = d_act * silu_slope(short_conv(ext, taps[0], rows))
    lead = HALO - tap_count + 1
    padded = jnp.concatenate([jnp.zeros((HALO, wide), f32), d_conv], axis=0)
    d_ext = jnp.zeros((HALO + rows, wide), f32)
    tap_terms = []
    for j in range(tap_count):
        moved = rows_after(padded, tap_count - 1 - j)
        d_ext = d_ext + taps[0, pl.ds(j, 1)] * moved
        tap_terms.append(jnp.sum(moved * ext, axis=0, keepdims=True))
    tap_terms = jnp.concatenate(tap_terms, axis=0)

    @pl.when(i == 0)
    def _():
        d_taps[h] = tap_terms

    @pl.when(i > 0)
    def _():
        d_taps[h] += tap_terms

    d_gate_ext = jnp.concatenate([jnp.zeros((HALO, wide_value), bf16), d_gate[0, 0]], axis=0)
    d_projected[0, 0] = jnp.concatenate([d_ext.astype(bf16), d_gate_ext], axis=1)
    term = dot_nt(d_projected[0, 0], w[0])

    @pl.when(h == 0)
    def _():
        d_normed[...] = term

    @pl.when(h > 0)
    def _():
        d_normed[...] += term

    @pl.when(h == heads - 1)
    def _():
        values, upstream = without_first(tokens[0], first), d_normed[...]
        inverse = row_scale(values)
        gain_term = jnp.sum(upstream * values * inverse, axis=0, keepdims=True)
        d_gain[0] = gain_term
        back = norm_back(values, inverse, gain[...], upstream)
        d_tokens[0, pl.ds(0, HALO)] = back[:HALO].astype(bf16)
        d_tokens[0, pl.ds(HALO, rows)] = (back[HALO:] + d_hidden_in[0]).astype(bf16)


def backward_two_body(first, leaving, operands, outs, scratch):
    tokens, d_hidden_in, w, *by_head, gain, taps = operands
    d_projected, d_tokens, d_taps, d_gain = outs
    tokens_here, hidden_here, w_here, *here, projected_here, tokens_out, d_normed, load_sem, once_sem, store_sem = scratch
    heads, seqs, rows, key = by_head[1].shape
    wide_value = by_head[4].shape[3]
    steps = heads * seqs
    first = first.astype(jnp.int32)

    def once():
        return [
            pltpu.make_async_copy(tokens, tokens_here, once_sem.at[0]),
            pltpu.make_async_copy(d_hidden_in, hidden_here, once_sem.at[1]),
        ]

    def loads(n):
        i, h = n // heads, n % heads
        copies = [pltpu.make_async_copy(w.at[pl.ds(h, 1)], w_here, load_sem.at[0])]
        return copies + [
            pltpu.make_async_copy(a.at[pl.ds(h, 1), pl.ds(i, 1)], b, load_sem.at[1 + k])
            for k, (a, b) in enumerate(zip(by_head, here))
        ]

    def store(n):
        return pltpu.make_async_copy(
            projected_here, d_projected.at[pl.ds(n % heads, 1), pl.ds(n // heads, 1)], store_sem.at[0])

    def step(n, carry):
        i, h = n // heads, n % heads
        for copy in loads(n):
            copy.wait()

        @pl.when(n > 0)
        def _():
            store(n - 1).wait()

        at = pl.ds(pl.multiple_of((h * seqs + i) * wide_value, wide_value), wide_value)
        backward_two_step(
            i, h, heads, first, tokens_here.at[pl.ds(i, 1)], gain, hidden_here.at[pl.ds(i, 1)], w_here, taps.at[pl.ds(h, 1)],
            *here[:-1], leaving.at[at], here[-1], projected_here, tokens_out, d_taps, d_gain.at[pl.ds(i, 1)], d_normed)
        store(n).start()

        @pl.when(n < steps - 1)
        def _():
            for copy in loads(n + 1):
                copy.start()

        @pl.when(h == heads - 1)
        def _():
            copy = pltpu.make_async_copy(tokens_out, d_tokens.at[pl.ds(i, 1)], store_sem.at[1])
            copy.start()
            copy.wait()

        return carry

    def load_first():
        for copy in once() + loads(0):
            copy.start()
        for copy in once():
            copy.wait()

    def run(part, parts):
        lax.fori_loop(part * steps // parts, (part + 1) * steps // parts, step, 0)

    def finish_run():
        store(steps - 1).wait()

    return load_first, run, finish_run


def backward_two(tokens, gain, d_hidden_in, w, taps, *by_head):
    heads, seqs, rows, key = by_head[1].shape
    width, columns = w.shape[1:]
    tap_count, wide = taps.shape[1:]
    tall = rows + HALO
    anywhere, near = pl.BlockSpec(memory_space=pl.ANY), pl.BlockSpec(memory_space=pltpu.VMEM)
    dma = pltpu.SemaphoreType.DMA
    shape = jax.ShapeDtypeStruct
    return (
        (tokens, d_hidden_in, w, *by_head, gain.reshape(1, -1), taps),
        [anywhere] * (3 + len(by_head)) + [near] * 2,
        [
            shape((heads, seqs, tall, columns), bf16), shape((seqs, tall, width), bf16), shape((heads, tap_count, wide), f32),
            shape((seqs, 1, width), f32),
        ],
        [anywhere] * 2 + [near] * 2,
        [pltpu.VMEM(tokens.shape, bf16), pltpu.VMEM(d_hidden_in.shape, f32), pltpu.VMEM((1, *w.shape[1:]), bf16)]
        + [pltpu.VMEM((1, 1, *a.shape[2:]), a.dtype) for a in by_head]
        + [pltpu.VMEM((1, 1, tall, columns), bf16), pltpu.VMEM((1, tall, width), bf16), pltpu.VMEM((tall, width), f32)]
        + [dma((1 + len(by_head),)), dma((2,)), dma((2,))],
        backward_two_body,
    )


def finalize_body(key, value, last, lay, tok, halo, mixer, out, gate, up, down, small, *outs):
    step = pl.program_id(0)
    o_lay, o_tok, o_query, o_key, o_value, o_gate_proj, o_out, o_gate, o_up, o_down, o_small = outs
    o_lay[...] = lay[...].astype(f32)
    o_tok[...] = tok[...].astype(f32)
    steps = pl.num_programs(0)

    @pl.when((step % 2 == 1) & ((step < steps - 1) | (last[0] == 0)))
    def _():
        at = pl.ds(tok.shape[1] - HALO, HALO)
        o_tok[:, at] += halo[0].astype(f32)

    begin = 0
    for ref, wide in ((o_query, key), (o_key, key), (o_value, value), (o_gate_proj, value)):
        ref[...] = mixer[:, pl.ds(begin, wide)].astype(f32)
        begin += wide
    for to, of in ((o_out, out), (o_gate, gate), (o_up, up), (o_down, down)):
        to[...] = of[...].astype(f32)

    @pl.when(step == 0)
    def _():
        o_small[...] = small[...].astype(f32)


def finalize(last, lay, tok, halos, mixer, out, gate, up, down, small, key, value):
    heads, seqs, _, width = halos.shape
    steps = 2 * heads
    rows = lay.shape[1] // steps
    acts = pl.BlockSpec((seqs, rows, width), lambda i: (0, i, 0))

    def by_rows(array, columns=None):
        return pl.BlockSpec((array.shape[0] // steps, columns or array.shape[1]), lambda i: (i, 0))

    whole_small = pl.BlockSpec(small.shape, lambda i: (0, 0))
    full = lambda *shape: jax.ShapeDtypeStruct(shape, f32)
    tall = mixer.shape[0]
    grads = (out, gate, up, down)
    return pl.pallas_call(
        partial(finalize_body, key, value),
        grid=(steps,),
        in_specs=[
            pl.BlockSpec(memory_space=pltpu.SMEM), acts, acts,
            pl.BlockSpec((1, seqs, HALO, width), lambda i: ((i + 1) // 2 % heads, 0, 0, 0)),
            by_rows(mixer), *map(by_rows, grads), whole_small,
        ],
        out_specs=[acts, acts] + [by_rows(mixer, n) for n in (key, key, value, value)] + [*map(by_rows, grads), whole_small],
        out_shape=[full(*lay.shape), full(*tok.shape)]
        + [full(tall, n) for n in (key, key, value, value)]
        + [full(*a.shape) for a in grads]
        + [full(*small.shape)],
        compiler_params=pltpu.CompilerParams(vmem_limit_bytes=60 * 2**20),
        name="outputs",
    )(last, lay, tok, halos, mixer, out, gate, up, down, small)


def chunks(array, rows, count):
    return [(array, 0, i * (rows // count), rows // count) for i in range(count)]


def local(
    tokens,
    decay_codes,
    cotangent,
    attn_gain,
    w_query,
    w_key,
    w_value,
    w_out_gate,
    conv_query,
    conv_key,
    conv_value,
    out_gain,
    w_out,
    mlp_gain,
    w_gate,
    w_up,
    w_down,
):
    seqs, rows, own_width = tokens.shape
    heads = lax.axis_size("head")
    place = lax.axis_index("seq") * heads + lax.axis_index("head")
    mine = rows // heads
    width = own_width * heads
    key_width = w_query.shape[1]
    value_width = w_value.shape[1]
    conv_width = 2 * key_width + value_width
    mixer_width = conv_width + value_width

    half, ff = width // 2, w_gate.shape[1]
    out_half, ff_half = w_out.shape[0] // 2, ff // 2
    items = [(0, 0, 0, 0, 0, width, 0, key_width), (1, 1, 0, 0, 0, width, key_width, key_width)]
    items += [(i, 2, 0, 0, i * half, half, 2 * key_width, value_width) for i in range(2)]
    items += [(i, 3, 0, 0, i * half, half, conv_width, value_width) for i in range(2)]
    items += [(i, 4, 1, 0, i * out_half, out_half, 0, width) for i in range(2)]
    pair = [(2 + 2 * a + i, 5 + a, 2 + a, 1, i * ff_half, ff_half, 0, width) for a in range(3) for i in range(2)]
    tokens_ext, codes, taps, w_mixer, w_proj, w_gate_all, w_up_all, w_low = start_all(
        tokens,
        decay_codes.astype(jnp.int16),
        jnp.concatenate([conv_query, conv_key, conv_value], axis=1),
        (w_query, w_key, w_value, w_out_gate, w_out, w_gate.T, w_up.T, w_down),
        items + pair,
        [3] * (len(items) + len(pair)),
        ((width, mixer_width), w_out.shape, w_down.shape, w_down.shape, w_down.shape),
        1,
    )
    upstream, codes = lax.optimization_barrier((cotangent, codes))
    upstream = lax.all_to_all(upstream, "head", 1, 2, tiled=True)

    first = (place == 0).astype(jnp.int32).reshape(1)
    normed, pre, q_exp, k_exp, k_end, value, decay, starts, local_end, log_total = forward_one(
        first, tokens_ext, attn_gain, w_mixer, taps, codes
    )
    flat = (-1, key_width)
    log_total = log_total.reshape(flat)
    (incoming,) = exchange(local_end.reshape(flat), log_total, 2)
    core, states, gated, hidden_in = forward_two(
        first, tokens_ext, pre, q_exp, k_exp, value, decay, starts, incoming.reshape(local_end.shape), out_gain, w_proj
    )
    layer_out, d_hidden_in, normed_two, hidden, d_gate, d_up, grad_mlp_gain = mlp(
        hidden_in.reshape(-1, width), mlp_gain, upstream.reshape(-1, width), w_gate_all, w_up_all, w_low
    )
    d_hidden_in = d_hidden_in.reshape(hidden_in.shape)
    layer_out = layer_out.reshape(hidden_in.shape)
    d_mixer, d_core, d_gate_rows, d_states, own_grad, grad_out_gain = backward_one(
        d_hidden_in, w_proj, core, pre, out_gain, q_exp, decay
    )
    ff_part = ff // 4
    ff_plan = [(a, 1, i * ff_part, ff_part) for a in range(3) for i in range(4)]
    _, *blocks, d_projected, tokens_grad, grad_taps, grad_attn_gain = sums(
        (),
        (),
        ff_plan,
        [(0, 0, False), (1, 0, False), (2, 1, False)],
        [w_down.shape] * 3,
        (),
        [a[:, None] for a in (d_gate, d_up, hidden)],
        [normed_two[None, None], upstream.reshape(1, 1, -1, width)],
        3,
        (own_grad.reshape(flat), log_total),
        False,
        rider=backward_two(
            tokens_ext, attn_gain, d_hidden_in, w_mixer, taps, pre, q_exp, k_exp, k_end, value, decay, states, d_core, d_states,
            d_gate_rows,
        ),
    )
    small = jnp.concatenate(
        [
            jnp.sum(grad_attn_gain, axis=0).reshape(heads, -1),
            grad_mlp_gain.reshape(heads, -1),
            jnp.broadcast_to(grad_out_gain, (heads, value_width)),
            grad_taps.reshape(heads, -1),
        ],
        axis=1,
    )
    small_rows = 256
    lanes = -(-small.shape[1] // (small_rows * 128)) * 128
    small = jnp.pad(small, ((0, 0), (0, small_rows * lanes - small.shape[1]))).reshape(heads, small_rows, lanes)
    mixer_plan = chunks(0, width, 4) + [(1, 1, i * out_half, out_half) for i in range(2)] + chunks(2, small_rows, 2)
    more = [(3 + a, axis, row, size, c % 2) for c, (a, axis, row, size) in enumerate(ff_plan)]
    layer_out, tokens_grad, halos, grad_mixer, grad_out, small, grad_gate, grad_up, grad_down = sums(
        (layer_out, tokens_grad),
        (0, HALO),
        mixer_plan,
        [(0, 0, True), (1, 1, True), 0],
        [(width, mixer_width), w_out.shape, small.shape[1:]] + [w_down.shape] * 3,
        [small.astype(bf16)],
        [normed[None], gated],
        [d_projected, d_mixer[None]],
        4,
        blocks=blocks,
        more=more,
        groups=[(0, 1, 4, 5), (2, 3, 6, 7)],
    )
    last = lax.axis_index("seq") == lax.axis_size("seq") - 1
    (layer_out, tokens_grad, grad_query, grad_key, grad_value, grad_out_gate, grad_out, grad_gate, grad_up, grad_down, small) = finalize(
        last.astype(jnp.int32).reshape(1), layer_out, tokens_grad, halos, grad_mixer, grad_out, grad_gate, grad_up, grad_down,
        small, key_width, value_width,
    )
    small = small.reshape(-1)
    at = 2 * own_width + value_width
    grad_taps = small[at : at + taps[0].size].reshape(taps.shape[1:])
    return (
        layer_out,
        tokens_grad,
        small[:own_width],
        grad_query,
        grad_key,
        grad_value,
        grad_out_gate,
        grad_taps[:, :key_width],
        grad_taps[:, key_width : 2 * key_width],
        grad_taps[:, 2 * key_width :],
        small[2 * own_width : at],
        grad_out,
        small[own_width : 2 * own_width],
        grad_gate.T,
        grad_up.T,
        grad_down,
    )


def solution(mesh):
    in_specs = (
        P(None, "seq", "head"),
        P(None, "seq", "head"),
        P(None, "seq", "head"),
        P(),
        P(None, "head"),
        P(None, "head"),
        P(None, "head"),
        P(None, "head"),
        P(None, "head"),
        P(None, "head"),
        P(None, "head"),
        P(),
        P("head", None),
        P(),
        P(None, "head"),
        P(None, "head"),
        P("head", None),
    )
    out_specs = (
        P(None, "seq", "head"),
        P(None, "seq", "head"),
        P("head"),
        P(None, "head"),
        P(None, "head"),
        P(None, "head"),
        P(None, "head"),
        P(None, "head"),
        P(None, "head"),
        P(None, "head"),
        P(),
        P("head", None),
        P("head"),
        P(None, "head"),
        P(None, "head"),
        P("head", None),
    )
    return jax.shard_map(local, mesh=mesh, in_specs=in_specs, out_specs=out_specs, check_vma=False)
```
